128 devices in a mesh: rows: 32 (over x, z_lo, y), seq: 4 (over z_hi, core).
Axes of the slice: x: 4, y: 4, z: 4 (z_hi: 2, z_lo: 2; z = z_hi * 2 + z_lo), core: 2. Of those that a mesh axis runs over, the one named last changes fastest.
Arguments:
- text_in: bfloat16 [96, 128, 768], P('rows', 'seq'), may hold values from -6 to 6
- image_in: bfloat16 [96, 144, 1024], P('rows', 'seq'), may hold values from -6 to 6
- text_lengths: int32 [96, 4], P('rows'), may hold values from 1 to 100, 128 in all within a row
- image_lengths: int32 [96, 4], P('rows'), may hold values from 1 to 112, 144 in all within a row
- text_cotangent: bfloat16 [96, 128, 768], P('rows', 'seq'), may hold values from -6 to 6
- image_cotangent: bfloat16 [96, 144, 1024], P('rows', 'seq'), may hold values from -6 to 6
- cross_text_proj: bfloat16 [768, 3, 1024], P('rows', None, 'seq'), may hold values from -0.21875 to 0.21875
- cross_text_out: bfloat16 [768, 1024], P('rows', 'seq'), may hold values from -0.75 to 0.75
- cross_text_up: bfloat16 [768, 3072], P('rows', 'seq'), may hold values from -0.21875 to 0.21875
- cross_text_down: bfloat16 [768, 3072], P('rows', 'seq'), may hold values from -0.109375 to 0.109375
- cross_text_head_bias: bfloat16 [2, 1024], P(None, 'seq'), may hold values from -1 to 1
- cross_text_up_bias: bfloat16 [1, 3072], P(None, 'seq'), may hold values from -1 to 1
- cross_text_bias: bfloat16 [4, 768], replicated, may hold values from -1 to 1
- cross_text_gain: bfloat16 [2, 768], replicated, may hold values from 0.5 to 1.5
- cross_image_proj: bfloat16 [1024, 3, 1024], P('rows', None, 'seq'), may hold values from -0.1875 to 0.1875
- cross_image_out: bfloat16 [1024, 1024], P('rows', 'seq'), may hold values from -0.75 to 0.75
- cross_image_up: bfloat16 [1024, 1024], P('rows', 'seq'), may hold values from -0.1875 to 0.1875
- cross_image_down: bfloat16 [1024, 1024], P('rows', 'seq'), may hold values from -0.1875 to 0.1875
- cross_image_head_bias: bfloat16 [2, 1024], P(None, 'seq'), may hold values from -1 to 1
- cross_image_up_bias: bfloat16 [1, 1024], P(None, 'seq'), may hold values from -1 to 1
- cross_image_bias: bfloat16 [4, 1024], replicated, may hold values from -1 to 1
- cross_image_gain: bfloat16 [2, 1024], replicated, may hold values from 0.5 to 1.5
- self_text_proj: bfloat16 [768, 3, 768], P('rows', None, 'seq'), may hold values from -0.21875 to 0.21875
- self_text_out: bfloat16 [768, 768], P('rows', 'seq'), may hold values from -0.875 to 0.875
- self_text_up: bfloat16 [768, 3072], P('rows', 'seq'), may hold values from -0.21875 to 0.21875
- self_text_down: bfloat16 [768, 3072], P('rows', 'seq'), may hold values from -0.109375 to 0.109375
- self_text_head_bias: bfloat16 [2, 768], P(None, 'seq'), may hold values from -1 to 1
- self_text_up_bias: bfloat16 [1, 3072], P(None, 'seq'), may hold values from -1 to 1
- self_text_bias: bfloat16 [4, 768], replicated, may hold values from -1 to 1
- self_text_gain: bfloat16 [2, 768], replicated, may hold values from 0.5 to 1.5
- self_image_proj: bfloat16 [1024, 3, 1024], P('rows', None, 'seq'), may hold values from -0.1875 to 0.1875
- self_image_out: bfloat16 [1024, 1024], P('rows', 'seq'), may hold values from -0.75 to 0.75
- self_image_up: bfloat16 [1024, 1024], P('rows', 'seq'), may hold values from -0.1875 to 0.1875
- self_image_down: bfloat16 [1024, 1024], P('rows', 'seq'), may hold values from -0.1875 to 0.1875
- self_image_head_bias: bfloat16 [2, 1024], P(None, 'seq'), may hold values from -1 to 1
- self_image_up_bias: bfloat16 [1, 1024], P(None, 'seq'), may hold values from -1 to 1
- self_image_bias: bfloat16 [4, 1024], replicated, may hold values from -1 to 1
- self_image_gain: bfloat16 [2, 1024], replicated, may hold values from 0.5 to 1.5
Outputs:
- text_out: bfloat16 [96, 128, 768], P('rows', 'seq')
- image_out: bfloat16 [96, 144, 1024], P('rows', 'seq')
- text_grad: bfloat16 [96, 128, 768], P('rows', 'seq')
- image_grad: bfloat16 [96, 144, 1024], P('rows', 'seq')
- grad_cross_text_proj: float32 [768, 3, 1024], P('rows', None, 'seq')
- grad_cross_text_out: float32 [768, 1024], P('rows', 'seq')
- grad_cross_text_up: float32 [768, 3072], P('rows', 'seq')
- grad_cross_text_down: float32 [768, 3072], P('rows', 'seq')
- grad_cross_text_head_bias: float32 [2, 1024], P(None, 'seq')
- grad_cross_text_up_bias: float32 [1, 3072], P(None, 'seq')
- grad_cross_text_bias: float32 [4, 768], replicated
- grad_cross_text_gain: float32 [2, 768], replicated
- grad_cross_image_proj: float32 [1024, 3, 1024], P('rows', None, 'seq')
- grad_cross_image_out: float32 [1024, 1024], P('rows', 'seq')
- grad_cross_image_up: float32 [1024, 1024], P('rows', 'seq')
- grad_cross_image_down: float32 [1024, 1024], P('rows', 'seq')
- grad_cross_image_head_bias: float32 [2, 1024], P(None, 'seq')
- grad_cross_image_up_bias: float32 [1, 1024], P(None, 'seq')
- grad_cross_image_bias: float32 [4, 1024], replicated
- grad_cross_image_gain: float32 [2, 1024], replicated
- grad_self_text_proj: float32 [768, 3, 768], P('rows', None, 'seq')
- grad_self_text_out: float32 [768, 768], P('rows', 'seq')
- grad_self_text_up: float32 [768, 3072], P('rows', 'seq')
- grad_self_text_down: float32 [768, 3072], P('rows', 'seq')
- grad_self_text_head_bias: float32 [2, 768], P(None, 'seq')
- grad_self_text_up_bias: float32 [1, 3072], P(None, 'seq')
- grad_self_text_bias: float32 [4, 768], replicated
- grad_self_text_gain: float32 [2, 768], replicated
- grad_self_image_proj: float32 [1024, 3, 1024], P('rows', None, 'seq')
- grad_self_image_out: float32 [1024, 1024], P('rows', 'seq')
- grad_self_image_up: float32 [1024, 1024], P('rows', 'seq')
- grad_self_image_down: float32 [1024, 1024], P('rows', 'seq')
- grad_self_image_head_bias: float32 [2, 1024], P(None, 'seq')
- grad_self_image_up_bias: float32 [1, 1024], P(None, 'seq')
- grad_self_image_bias: float32 [4, 1024], replicated
- grad_self_image_gain: float32 [2, 1024], replicated
The draws below stay inside these ranges and needn't reach their ends.
Inputs may be any that keep to these rules, and one draw needn't show every extreme that they name: `text_lengths`: each row's 4 caption lengths sum to 128, and one of them is exactly 100. `image_lengths`: each row's 4 image lengths sum to 144, and one of them is exactly 112.
All inputs are finite; a program needn't handle non-finite values.
Results may differ from the reference program's by a relative error of at most 0.038.
Values may be sent and summed in bfloat16 or wider, within the bound.
A program may use at most 128 MiB of HBM per device.

```python
import math
import jax
import jax.numpy as jnp
import numpy as np
from jax import lax

ROWS_DEV = 3
ROWS = 96
LT = 128
LI = 144
CAPS = 4
MOST_T = 100
MOST_I = 112
DT = 768
DI = 1024
DC = 1024
FT = 3072
FI = 1024
HEADS_CROSS = 8
HEADS_TEXT = 12
HEADS_IMAGE = 8


def strengthened(drawn, key, source, target, shards_of, factor):
    owner, partner = [(jnp.arange(drawn.shape[axis_at]) // (drawn.shape[axis_at] // shards_of)).reshape([-1 if axis == axis_at else 1 for axis in range(drawn.ndim)]) for axis_at in (source, target)]
    chosen = jax.random.permutation(key, shards_of)[partner]
    strong = (owner == chosen) | (owner == (partner + shards_of // 2) % shards_of)
    return jnp.where(strong, factor * drawn, drawn)


def levels(stream_key, shape, split, low, high):
    def one(dim, blocks):
        heights = jax.random.uniform(jax.random.fold_in(jax.random.fold_in(stream_key, 6), dim), (blocks,), jnp.float32, low / len(split), high / len(split))
        return jnp.repeat(jnp.exp(heights), shape[dim] // blocks).reshape((-1,) + (1,) * (len(shape) - dim - 1))

    level = one(*split[0])
    for cut in split[1:]:
        level = level * one(*cut)
    return level


def profile(count, total, limit, slope):
    portions = [(1 << 20) // math.isqrt(rank ** slope) + 1 for rank in range(2, count + 1)]
    surplus, given = total - limit - (count - 1), [1] * (count - 1)
    while surplus > 0:
        free = [i for i in range(count - 1) if given[i] < limit]
        whole, budget = sum([portions[i] for i in free]), surplus
        for i in free:
            extra = min(limit - given[i], max(1, budget * portions[i] // whole), surplus)
            given[i] = given[i] + extra
            surplus = surplus - extra
    return np.array([limit] + given)


def ragged(own_key, count, total, reach, lean):
    if count == 2:
        one = jax.random.randint(own_key, (), max(1, total - reach), min(reach, total - 1) + 1)
        return jnp.stack([one, total - one])
    sizes = jnp.asarray(profile(count, total, reach, lean), jnp.int32)
    pairs = (count - 1) // 2
    source_of, receiver = sizes[1:1 + 2 * pairs:2], sizes[2:2 + 2 * pairs:2]
    margin = jnp.minimum(source_of - 1, reach - receiver)
    passed = jax.random.randint(jax.random.fold_in(own_key, 1), (pairs,), 0, 1 << 20) % (margin + 1)
    sizes = sizes.at[1:1 + 2 * pairs:2].set(source_of - passed).at[2:2 + 2 * pairs:2].set(receiver + passed)
    return sizes[jax.random.permutation(jax.random.fold_in(own_key, 2), count)]


def gaussian(rng, extent, deviation, reach, pieces=(), kind=jnp.bfloat16):
    factor_of = levels(rng, extent, pieces, -0.22, 0.18) if pieces else 1.0
    entries = jax.random.normal(rng, extent, jnp.float32) * deviation * factor_of
    return jnp.minimum(jnp.maximum(entries, -reach), reach).astype(kind)


def noise_with(stream_key, shape, deviation, limit, cuts, heavy, held_as=jnp.bfloat16):
    drawn = deviation * jax.random.normal(stream_key, shape, jnp.float32)
    if cuts:
        drawn = drawn * levels(stream_key, shape, cuts, -0.22, 0.18)
    return jnp.clip(strengthened(drawn, jax.random.fold_in(stream_key, 3), *heavy), -limit, limit).astype(held_as)


def setup_inputs(seed: int = 0) -> dict:
    splits = jax.random.split(jax.random.key(seed), 39)
    return {
        "text_in": gaussian(splits[0], (ROWS, LT, DT), 1.0, 6.0, ((0, 32), (1, 4))),
        "image_in": gaussian(splits[1], (ROWS, LI, DI), 1.0, 6.0, ((0, 32), (1, 4))),
        "text_lengths": jax.vmap(lambda own: ragged(own, CAPS, LT, MOST_T, 2))(jax.random.split(splits[2], ROWS)).reshape((ROWS, CAPS)).astype(jnp.int32),
        "image_lengths": jax.vmap(lambda own: ragged(own, CAPS, LI, MOST_I, 2))(jax.random.split(splits[3], ROWS)).reshape((ROWS, CAPS)).astype(jnp.int32),
        "text_cotangent": noise_with(splits[4], (ROWS, LT, DT), 1.0, 6.0, ((0, 32), (1, 4)), (0, 2, 32, 2.75)),
        "image_cotangent": noise_with(splits[5], (ROWS, LI, DI), 1.0, 6.0, ((0, 32), (1, 4)), (0, 2, 32, 2.75)),
        "cross_text_proj": gaussian(splits[6], (DT, 3, DC), DT ** -0.5, 0.21875, ((0, 32), (2, 4))),
        "cross_text_out": gaussian(splits[7], (DT, DC), (DC // 16) ** -0.5, 0.75, ((0, 32), (1, 4))),
        "cross_text_up": gaussian(splits[8], (DT, FT), DT ** -0.5, 0.21875, ((0, 32), (1, 4))),
        "cross_text_down": gaussian(splits[9], (DT, FT), FT ** -0.5, 0.109375, ((0, 32), (1, 4))),
        "cross_text_head_bias": gaussian(splits[10], (2, DC), 0.2, 1.0, ((1, 4),)),
        "cross_text_up_bias": gaussian(splits[11], (1, FT), 0.2, 1.0, ((1, 4),)),
        "cross_text_bias": gaussian(splits[12], (4, DT), 0.2, 1.0),
        "cross_text_gain": jnp.clip(1.0 + 0.1 * jax.random.normal(splits[13], (2, DT), jnp.float32), 0.5, 1.5).astype(jnp.bfloat16),
        "cross_image_proj": gaussian(splits[14], (DI, 3, DC), DI ** -0.5, 0.1875, ((0, 32), (2, 4))),
        "cross_image_out": gaussian(splits[15], (DI, DC), (DC // 16) ** -0.5, 0.75, ((0, 32), (1, 4))),
        "cross_image_up": gaussian(splits[16], (DI, FI), DI ** -0.5, 0.1875, ((0, 32), (1, 4))),
        "cross_image_down": gaussian(splits[17], (DI, FI), FI ** -0.5, 0.1875, ((0, 32), (1, 4))),
        "cross_image_head_bias": gaussian(splits[18], (2, DC), 0.2, 1.0, ((1, 4),)),
        "cross_image_up_bias": gaussian(splits[19], (1, FI), 0.2, 1.0, ((1, 4),)),
        "cross_image_bias": gaussian(splits[20], (4, DI), 0.2, 1.0),
        "cross_image_gain": jnp.clip(1.0 + 0.1 * jax.random.normal(splits[21], (2, DI), jnp.float32), 0.5, 1.5).astype(jnp.bfloat16),
        "self_text_proj": gaussian(splits[22], (DT, 3, DT), DT ** -0.5, 0.21875, ((0, 32), (2, 4))),
        "self_text_out": gaussian(splits[23], (DT, DT), (DT // 16) ** -0.5, 0.875, ((0, 32), (1, 4))),
        "self_text_up": gaussian(splits[24], (DT, FT), DT ** -0.5, 0.21875, ((0, 32), (1, 4))),
        "self_text_down": gaussian(splits[25], (DT, FT), FT ** -0.5, 0.109375, ((0, 32), (1, 4))),
        "self_text_head_bias": gaussian(splits[26], (2, DT), 0.2, 1.0, ((1, 4),)),
        "self_text_up_bias": gaussian(splits[27], (1, FT), 0.2, 1.0, ((1, 4),)),
        "self_text_bias": gaussian(splits[28], (4, DT), 0.2, 1.0),
        "self_text_gain": jnp.clip(1.0 + 0.1 * jax.random.normal(splits[29], (2, DT), jnp.float32), 0.5, 1.5).astype(jnp.bfloat16),
        "self_image_proj": gaussian(splits[30], (DI, 3, DI), DI ** -0.5, 0.1875, ((0, 32), (2, 4))),
        "self_image_out": gaussian(splits[31], (DI, DI), (DI // 16) ** -0.5, 0.75, ((0, 32), (1, 4))),
        "self_image_up": gaussian(splits[32], (DI, FI), DI ** -0.5, 0.1875, ((0, 32), (1, 4))),
        "self_image_down": gaussian(splits[33], (DI, FI), FI ** -0.5, 0.1875, ((0, 32), (1, 4))),
        "self_image_head_bias": gaussian(splits[34], (2, DI), 0.2, 1.0, ((1, 4),)),
        "self_image_up_bias": gaussian(splits[35], (1, FI), 0.2, 1.0, ((1, 4),)),
        "self_image_bias": gaussian(splits[36], (4, DI), 0.2, 1.0),
        "self_image_gain": jnp.clip(1.0 + 0.1 * jax.random.normal(splits[37], (2, DI), jnp.float32), 0.5, 1.5).astype(jnp.bfloat16),
    }


epsilon = 1e-05
masked_value = -1000000000.0
highest = lax.Precision.HIGHEST

@jax.custom_vjp
def low(v):
    return lax.optimization_barrier(v.astype(jnp.bfloat16)).astype(jnp.float32)

@jax.custom_vjp
def low_back(v):
    return v

def low_keep(v):
    return (low(v), None)

def low_pass(kept, grad):
    return (grad,)

def back_keep(v):
    return (v, None)

def back_low(kept, grad):
    return (low(grad),)
low.defvjp(low_keep, low_pass)
low_back.defvjp(back_keep, back_low)

def segments(lengths, positions_total):
    boundary = jnp.cumsum(lengths, axis=-1)
    position = jnp.arange(positions_total, dtype=jnp.int32)
    return lax.optimization_barrier(jnp.sum((position[None, :, None] >= boundary[:, None, :]).astype(jnp.int32), axis=-1))

def layer_norm(summed, gain_vec, shift_vec):
    centre = lax.optimization_barrier(jnp.mean(summed, axis=-1, keepdims=True))
    spread = lax.optimization_barrier(jnp.mean(jnp.square(summed - centre), axis=-1, keepdims=True))
    return (summed - centre) * lax.rsqrt(spread + epsilon) * gain_vec + shift_vec

def project(inputs, proj_weight, head_bias):
    offset = jnp.stack([head_bias[0], jnp.zeros_like(head_bias[0]), head_bias[1]])
    result = jnp.einsum('btd,dca->btca', low(inputs), proj_weight, precision=highest) + offset
    return low(low_back(result))

def attend(queries, keys_in, values_in, allowed, head_size):
    batch_size, query_len, inner_width = queries.shape
    heads_count = inner_width // head_size
    query_heads = queries.reshape(batch_size, query_len, heads_count, head_size)
    key_heads = keys_in.reshape(keys_in.shape[0], keys_in.shape[1], heads_count, head_size)
    value_heads = values_in.reshape(values_in.shape[0], values_in.shape[1], heads_count, head_size)
    raw_scores = low_back(jnp.einsum('bqhd,bkhd->bhqk', query_heads, key_heads, precision=highest))
    scores = jnp.where(allowed[:, None], raw_scores * head_size ** (-0.5), masked_value)
    largest = lax.optimization_barrier(jnp.max(scores, axis=-1, keepdims=True))
    shifted = jnp.exp(scores - largest)
    probability = shifted / lax.optimization_barrier(jnp.sum(shifted, axis=-1, keepdims=True))
    mixed = jnp.einsum('bhqk,bkhd->bqhd', low(probability), value_heads, precision=highest)
    return low(low_back(mixed.reshape(batch_size, query_len, inner_width)))

def finish(inputs, mixed, params):
    out_weight = params[1]
    up_weight = params[2]
    down_weight = params[3]
    up_bias = params[5]
    bias_rows = params[6]
    gain_rows = params[7]
    branch = low_back(jnp.einsum('bta,da->btd', mixed, out_weight, precision=highest) + bias_rows[0])
    normed = layer_norm(inputs + branch, gain_rows[0], bias_rows[2])
    upward = low_back(jnp.einsum('btd,df->btf', low(normed), up_weight, precision=highest) + up_bias[0])
    active = low(jax.nn.gelu(upward))
    second = low_back(jnp.einsum('btf,df->btd', active, down_weight, precision=highest) + bias_rows[1])
    return layer_norm(normed + second, gain_rows[1], bias_rows[3])

def forward(text_value, image_value, text_seg, image_seg, weight_tree):
    cross_text, cross_image, self_text, self_image = weight_tree
    text_proj = project(text_value, cross_text[0], cross_text[4])
    image_proj = project(image_value, cross_image[0], cross_image[4])
    text_mask = text_seg[:, :, None] == image_seg[:, None, :]
    image_mask = image_seg[:, :, None] == text_seg[:, None, :]
    cross_head = DC // HEADS_CROSS
    text_mixed = attend(text_proj[:, :, 0], image_proj[:, :, 1], image_proj[:, :, 2], text_mask, cross_head)
    image_mixed = attend(image_proj[:, :, 0], text_proj[:, :, 1], text_proj[:, :, 2], image_mask, cross_head)
    text_mid = finish(text_value, text_mixed, cross_text)
    image_mid = finish(image_value, image_mixed, cross_image)
    text_self = project(text_mid, self_text[0], self_text[4])
    image_self = project(image_mid, self_image[0], self_image[4])
    text_own = text_seg[:, :, None] == text_seg[:, None, :]
    image_own = image_seg[:, :, None] == image_seg[:, None, :]
    text_smix = attend(text_self[:, :, 0], text_self[:, :, 1], text_self[:, :, 2], text_own, DT // HEADS_TEXT)
    image_smix = attend(image_self[:, :, 0], image_self[:, :, 1], image_self[:, :, 2], image_own, DI // HEADS_IMAGE)
    text_final = finish(text_mid, text_smix, self_text)
    image_final = finish(image_mid, image_smix, self_image)
    return (text_final, image_final)

def to_float(leaf_array):
    return leaf_array.astype(jnp.float32)

def reference(text_in, image_in, text_lengths, image_lengths, text_cotangent, image_cotangent, cross_text_proj, cross_text_out, cross_text_up, cross_text_down, cross_text_head_bias, cross_text_up_bias, cross_text_bias, cross_text_gain, cross_image_proj, cross_image_out, cross_image_up, cross_image_down, cross_image_head_bias, cross_image_up_bias, cross_image_bias, cross_image_gain, self_text_proj, self_text_out, self_text_up, self_text_down, self_text_head_bias, self_text_up_bias, self_text_bias, self_text_gain, self_image_proj, self_image_out, self_image_up, self_image_down, self_image_head_bias, self_image_up_bias, self_image_bias, self_image_gain):
    weight_tree = jax.tree.map(to_float, ((cross_text_proj, cross_text_out, cross_text_up, cross_text_down, cross_text_head_bias, cross_text_up_bias, cross_text_bias, cross_text_gain), (cross_image_proj, cross_image_out, cross_image_up, cross_image_down, cross_image_head_bias, cross_image_up_bias, cross_image_bias, cross_image_gain), (self_text_proj, self_text_out, self_text_up, self_text_down, self_text_head_bias, self_text_up_bias, self_text_bias, self_text_gain), (self_image_proj, self_image_out, self_image_up, self_image_down, self_image_head_bias, self_image_up_bias, self_image_bias, self_image_gain)))
    text_seg = segments(text_lengths, LT)
    image_seg = segments(image_lengths, LI)
    group_count = text_in.shape[0] // ROWS_DEV

    def grouped(full_array):
        return full_array.reshape((group_count, ROWS_DEV) + full_array.shape[1:])
    stacked = (grouped(text_in), grouped(image_in), grouped(text_seg), grouped(image_seg), grouped(text_cotangent), grouped(image_cotangent))
    zero_grads = jax.tree.map(jnp.zeros_like, weight_tree)

    def group_step(running, group_item):
        text_part, image_part, text_part_seg, image_part_seg, text_part_cot, image_part_cot = group_item

        def forward_group(text_value, image_value, weights_now):
            return forward(text_value, image_value, text_part_seg, image_part_seg, weights_now)
        outputs, pullback = jax.vjp(forward_group, text_part.astype(jnp.float32), image_part.astype(jnp.float32), weight_tree)
        text_back, image_back, weight_back = pullback((text_part_cot.astype(jnp.float32), image_part_cot.astype(jnp.float32)))
        running = jax.tree.map(jnp.add, running, weight_back)
        return (running, (outputs[0].astype(jnp.bfloat16), outputs[1].astype(jnp.bfloat16), text_back.astype(jnp.bfloat16), image_back.astype(jnp.bfloat16)))
    totals, per_group = lax.scan(group_step, zero_grads, stacked)
    text_out = per_group[0].reshape(text_in.shape)
    image_out = per_group[1].reshape(image_in.shape)
    text_grad = per_group[2].reshape(text_in.shape)
    image_grad = per_group[3].reshape(image_in.shape)
    return (text_out, image_out, text_grad, image_grad, totals[0][0], totals[0][1], totals[0][2], totals[0][3], totals[0][4], totals[0][5], totals[0][6], totals[0][7], totals[1][0], totals[1][1], totals[1][2], totals[1][3], totals[1][4], totals[1][5], totals[1][6], totals[1][7], totals[2][0], totals[2][1], totals[2][2], totals[2][3], totals[2][4], totals[2][5], totals[2][6], totals[2][7], totals[3][0], totals[3][1], totals[3][2], totals[3][3], totals[3][4], totals[3][5], totals[3][6], totals[3][7])
```

```python
import jax
import jax.numpy as jnp
from jax import lax
from jax.experimental import pallas as pl
from jax.experimental.pallas import tpu as pltpu
from jax.sharding import PartitionSpec as P

DT = 768
DI = 1024
DC = 1024
HEADS_CROSS = 8
HEADS_TEXT = 12
HEADS_IMAGE = 8


epsilon = 1e-05
masked_value = -1000000000.0


MESH = pl.DeviceIdType.MESH
VMEM = pltpu.VMEM
DMA = pltpu.SemaphoreType.DMA


class Place:
    def __init__(self):
        r = lax.axis_index("rows")
        s = lax.axis_index("seq")
        self.r, self.s = r, s
        self.x, self.z, self.y = r // 8, (r // 4) % 2, r % 4
        self.zh, self.c = s // 2, s % 2

    def dev(self, x, z, y):
        return ((x * 2 + z) * 4 + y, self.s)

    def along(self, axis, step):
        x, z, y = self.x, self.z, self.y
        if axis == "x":
            return self.dev((x + step) % 4, z, y)
        if axis == "y":
            return self.dev(x, z, (y + step) % 4)
        return self.dev(x, 1 - z, y)


def greet(devices):
    barrier = pltpu.get_barrier_semaphore()
    for device in devices:
        pl.semaphore_signal(barrier, inc=1, device_id=device, device_id_type=MESH)
    pl.semaphore_wait(barrier, len(devices))


def push(src, dst, sems, k, device):
    copy = pltpu.make_async_remote_copy(
        src_ref=src, dst_ref=dst, send_sem=sems.at[0, k], recv_sem=sems.at[1, k],
        device_id=device, device_id_type=MESH)
    copy.start()
    return copy


def gather_steps(me, own, buf, sems, order):
    x, z, y = me.x, me.z, me.y
    sent = []
    first = push(own, buf.at[x, z, y], sems, 0, me.along("z", 1))
    local = pltpu.make_async_copy(own, buf.at[x, z, y], sems.at[0, 9])
    local.start()
    yield
    local.wait()
    first.wait()
    k = 1
    for stage, axis in enumerate(order):
        if axis == "x":
            def view(step, half):
                at = (x + step) % 4
                if stage == 0:
                    return buf.at[at, :, y] if half is None else buf.at[at, half, y]
                return buf.at[at] if half is None else buf.at[at, :, pl.ds(2 * half, 2)]
        else:
            def view(step, half):
                at = (y + step) % 4
                if stage == 0:
                    return buf.at[x, :, at] if half is None else buf.at[x, half, at]
                return buf.at[:, :, at] if half is None else buf.at[pl.ds(2 * half, 2), :, at]
        right, left = me.along(axis, 1), me.along(axis, 3)
        to_right = push(view(0, None), view(0, None), sems, k, right)
        to_left = push(view(0, None), view(0, None), sems, k + 1, left)
        yield
        to_right.wait_recv()
        on_right = push(view(3, 0), view(3, 0), sems, k + 2, right)
        to_left.wait_recv()
        on_left = push(view(1, 1), view(1, 1), sems, k + 3, left)
        yield
        on_right.wait_recv()
        on_left.wait_recv()
        sent += [to_right, to_left, on_right, on_left]
        k += 4
    for copy in sent:
        copy.wait_send()


def run_together(steps):
    steps = list(steps)
    while steps:
        alive = []
        for step in steps:
            try:
                next(step)
                alive.append(step)
            except StopIteration:
                pass
        steps = alive


def gather_kernel(orders, *refs):
    n = len(orders)
    owns, bufs, sems = refs[:n], refs[n:2 * n], refs[2 * n:]
    me = Place()
    greet([me.along("z", 1), me.along("x", 1), me.along("x", 3), me.along("y", 1), me.along("y", 3)])
    run_together(gather_steps(me, owns[i], bufs[i], sems[i], orders[i]) for i in range(n))


def gather_all(packs, orders, collective_id=0):
    return pl.pallas_call(
        lambda *refs: gather_kernel(orders, *refs),
        out_shape=[jax.ShapeDtypeStruct((4, 2, 4) + p.shape, p.dtype) for p in packs],
        in_specs=[pl.BlockSpec(memory_space=pl.ANY)] * len(packs),
        out_specs=[pl.BlockSpec(memory_space=pl.ANY)] * len(packs),
        scratch_shapes=[DMA((2, 10))] * len(packs),
        compiler_params=pltpu.CompilerParams(collective_id=collective_id, has_side_effects=True),
    )(*packs)


def add_slabs(me, dst, src, count):
    def one(i, carry):
        at = dst(i)
        at[...] = (at[...].astype(jnp.float32) + src(i)[...].astype(jnp.float32)).astype(at.dtype)
        return carry
    lax.fori_loop(0, count, one, 0)


def reduce_steps(me, buf, out, halves, chunks, small_halves, small_chunks, last, sems, order):
    x, z, y = me.x, me.z, me.y
    sent = []
    k = 0
    for stage, axis in enumerate(order):
        half_in, chunk_in = (halves, chunks) if stage == 0 else (small_halves, small_chunks)
        place = x if axis == "x" else y
        if axis == "x":
            def view(step, half=None):
                at = (x + step) % 4
                if stage == 0:
                    return buf.at[at] if half is None else buf.at[at, :, pl.ds(2 * half, 2)]
                return buf.at[at, :, y] if half is None else buf.at[at, half, y]
        else:
            def view(step, half=None):
                at = (y + step) % 4
                if stage == 0:
                    return buf.at[:, :, at] if half is None else buf.at[pl.ds(2 * half, 2), :, at]
                return buf.at[x, :, at] if half is None else buf.at[x, half, at]
        right, left = me.along(axis, 1), me.along(axis, 3)
        a = push(view(2, 0), half_in.at[0], sems, k, right)
        b = push(view(2, 1), half_in.at[1], sems, k + 1, left)
        yield
        if stage == 0:
            def half_slab(step, half):
                at = (place + step) % 4
                if axis == "x":
                    return lambda i: buf.at[at, i // 2, 2 * half + i % 2]
                return lambda i: buf.at[2 * half + i // 2, i % 2, at]

            def full_slab(i):
                return buf.at[x, i // 4, i % 4] if axis == "x" else buf.at[i // 2, i % 2, y]
            n_half, n_full = 4, 8
        else:
            def half_slab(step, half):
                at = (place + step) % 4
                return lambda i: buf.at[at, half, y] if axis == "x" else buf.at[x, half, at]

            def full_slab(i):
                return buf.at[x, i, y]
            n_half, n_full = 1, 2

        def in_slab(ref, d):
            if stage == 1:
                return (lambda i: ref.at[d]) if ref is half_in else (lambda i: ref.at[d, i])
            wide = ref.shape[2]
            return lambda i: ref.at[d, i // wide, i % wide]
        a.wait_recv()
        add_slabs(me, half_slab(1, 0), in_slab(half_in, 0), n_half)
        c = push(view(1), chunk_in.at[0], sems, k + 2, right)
        b.wait_recv()
        add_slabs(me, half_slab(3, 1), in_slab(half_in, 1), n_half)
        d = push(view(3), chunk_in.at[1], sems, k + 3, left)
        yield
        c.wait_recv()
        add_slabs(me, full_slab, in_slab(chunk_in, 0), n_full)
        d.wait_recv()
        add_slabs(me, full_slab, in_slab(chunk_in, 1), n_full)
        sent += [a, b, c, d]
        k += 4
    e = push(buf.at[x, 1 - z, y], last, sems, k, me.along("z", 1))
    yield
    e.wait_recv()
    out[...] = buf[x, z, y].astype(jnp.float32) + last[...].astype(jnp.float32)
    sent.append(e)
    for copy in sent:
        copy.wait_send()


def reduce_scratch(order, rows, cols):
    lead = (2, 4) if order[0] == "x" else (4, 2)
    bf = jnp.bfloat16
    return [VMEM((2, 2, 2, rows, cols), bf), VMEM((2,) + lead + (rows, cols), bf),
            VMEM((2, rows, cols), bf), VMEM((2, 2, rows, cols), bf), VMEM((rows, cols), bf), DMA((2, 9))]


def reduce_kernel(orders, *refs):
    n = len(orders)
    ins, outs, scratch = refs[:n], refs[n:2 * n], refs[2 * n:]
    me = Place()
    copies = []
    for i in range(n):
        copies.append(pltpu.make_async_copy(ins[i], scratch[7 * i], scratch[7 * i + 6].at[0, 0]))
        copies[-1].start()
    greet([me.along("z", 1), me.along("x", 1), me.along("x", 3), me.along("y", 1), me.along("y", 3)])
    for copy in copies:
        copy.wait()
    run_together(reduce_steps(me, scratch[7 * i], outs[i], *scratch[7 * i + 1:7 * i + 7], orders[i]) for i in range(n))


def reduce_all(packs, orders, collective_id=1):
    scratch = []
    for p, order in zip(packs, orders):
        scratch += [VMEM(p.shape, p.dtype)] + reduce_scratch(order, p.shape[3], p.shape[4])
    return pl.pallas_call(
        lambda *refs: reduce_kernel(orders, *refs),
        out_shape=[jax.ShapeDtypeStruct(p.shape[3:], jnp.float32) for p in packs],
        in_specs=[pl.BlockSpec(memory_space=pl.ANY)] * len(packs),
        out_specs=[pl.BlockSpec(memory_space=pltpu.VMEM)] * len(packs),
        scratch_shapes=scratch,
        compiler_params=pltpu.CompilerParams(collective_id=collective_id, has_side_effects=True,
                                             vmem_limit_bytes=60 * 1024 * 1024),
    )(*packs)


def segments(lengths, positions_total):
    boundary = jnp.cumsum(lengths, axis=-1)
    position = jnp.arange(positions_total, dtype=jnp.int32)
    return jnp.sum((position[None, :, None] >= boundary[:, None, :]).astype(jnp.int32), axis=-1)


def layer_norm(summed, gain_vec, shift_vec):
    centre = jnp.mean(summed, axis=-1, keepdims=True)
    spread = jnp.mean(jnp.square(summed - centre), axis=-1, keepdims=True)
    return (summed - centre) * lax.rsqrt(spread + epsilon) * gain_vec + shift_vec


def spread_tokens(text_part, image_part):
    return (
        lax.all_gather(text_part, "seq", axis=1, tiled=True),
        lax.all_gather(image_part, "seq", axis=1, tiled=True),
    )


def tokens_from_partials(text_part, image_part):
    return (
        lax.psum_scatter(
            text_part.astype(jnp.bfloat16), "seq", scatter_dimension=1, tiled=True
        ).astype(jnp.float32),
        lax.psum_scatter(
            image_part.astype(jnp.bfloat16), "seq", scatter_dimension=1, tiled=True
        ).astype(jnp.float32),
    )


def spread_gradients(text_part, image_part):
    return (
        lax.all_gather(text_part, "seq", axis=1, tiled=True),
        lax.all_gather(image_part, "seq", axis=1, tiled=True),
    )


def gradients_from_partials(text_part, image_part):
    return (
        lax.psum_scatter(
            text_part.astype(jnp.bfloat16), "seq", scatter_dimension=1, tiled=True
        ).astype(jnp.float32),
        lax.psum_scatter(
            image_part.astype(jnp.bfloat16), "seq", scatter_dimension=1, tiled=True
        ).astype(jnp.float32),
    )


def heads_of(values_flat, head_size):
    return values_flat.reshape(
        values_flat.shape[0], values_flat.shape[1], values_flat.shape[2] // head_size, head_size
    )


def project_local(inputs_low, weights):
    head_bias = weights[4].astype(jnp.float32)
    offset = jnp.stack([head_bias[0], jnp.zeros_like(head_bias[0]), head_bias[1]])
    result = (
        jnp.einsum("rtd,dca->rtca", inputs_low, weights[0], preferred_element_type=jnp.float32)
        + offset
    )
    return result.astype(jnp.bfloat16)


def stream_sources(projected, crossing):
    partner = [1, 0] if crossing else [0, 1]
    sources = []
    for stream in range(2):
        key_source = projected[partner[stream]]
        sources.append((projected[stream][:, :, 0], key_source[:, :, 1], key_source[:, :, 2]))
    return sources


def attend_local(queries, keys_in, values_in, allowed, head_size):
    query_heads = heads_of(queries, head_size)
    key_heads = heads_of(keys_in, head_size)
    value_heads = heads_of(values_in, head_size)
    scaling = head_size ** (-0.5)
    raw_scores = jnp.einsum(
        "bqhd,bkhd->bhqk", query_heads, key_heads, preferred_element_type=jnp.float32
    )
    scores = jnp.where(allowed[:, None], raw_scores * scaling, masked_value)
    largest = jnp.max(scores, axis=-1, keepdims=True)
    shifted = jnp.exp(scores - largest)
    total_mass = jnp.sum(shifted, axis=-1, keepdims=True)
    probability = (shifted / total_mass).astype(jnp.bfloat16)
    mixed = jnp.einsum(
        "bhqk,bkhd->bqhd", probability, value_heads, preferred_element_type=jnp.float32
    )
    return (mixed.reshape(queries.shape).astype(jnp.bfloat16), largest + jnp.log(total_mass))


def attend_back(queries, keys_in, values_in, allowed, logsum, grad_mixed, head_size):
    query_heads = heads_of(queries, head_size)
    key_heads = heads_of(keys_in, head_size)
    value_heads = heads_of(values_in, head_size)
    scaling = head_size ** (-0.5)
    raw_scores = jnp.einsum(
        "bqhd,bkhd->bhqk", query_heads, key_heads, preferred_element_type=jnp.float32
    )
    scores = jnp.where(allowed[:, None], raw_scores * scaling, masked_value)
    probability = jnp.exp(scores - logsum)
    grad_heads = heads_of(grad_mixed, head_size)
    grad_prob = jnp.einsum(
        "bqhd,bkhd->bhqk", grad_heads, value_heads, preferred_element_type=jnp.float32
    )
    grad_values = jnp.einsum(
        "bhqk,bqhd->bkhd",
        probability.astype(jnp.bfloat16),
        grad_heads,
        preferred_element_type=jnp.float32,
    )
    row_inner = jnp.sum(grad_prob * probability, axis=-1, keepdims=True)
    grad_scores = (probability * (grad_prob - row_inner) * scaling).astype(jnp.bfloat16)
    grad_queries = jnp.einsum(
        "bhqk,bkhd->bqhd", grad_scores, key_heads, preferred_element_type=jnp.float32
    )
    grad_keys = jnp.einsum(
        "bhqk,bqhd->bkhd", grad_scores, query_heads, preferred_element_type=jnp.float32
    )
    return (
        grad_queries.reshape(queries.shape).astype(jnp.bfloat16),
        grad_keys.reshape(keys_in.shape).astype(jnp.bfloat16),
        grad_values.reshape(values_in.shape).astype(jnp.bfloat16),
    )


def mlp_forward(normed_low, up_weight, down_weight, up_bias):
    upward = jnp.einsum(
        "rtd,df->rtf", normed_low, up_weight, preferred_element_type=jnp.float32
    ) + up_bias[0].astype(jnp.float32)
    active = jax.nn.gelu(upward).astype(jnp.bfloat16)
    partial_sum = jnp.einsum("rtf,df->rtd", active, down_weight, preferred_element_type=jnp.float32)
    return (upward, active, partial_sum)


def mlp_backward(grad_low, normed_low, upward, active, up_weight, down_weight):
    grad_down = jnp.einsum("rtd,rtf->df", grad_low, active, preferred_element_type=jnp.float32)
    grad_active = jnp.einsum(
        "rtd,df->rtf", grad_low, down_weight, preferred_element_type=jnp.float32
    )
    unused, gelu_pullback = jax.vjp(jax.nn.gelu, upward)
    grad_upward = gelu_pullback(grad_active)[0].astype(jnp.bfloat16)
    grad_up = jnp.einsum("rtd,rtf->df", normed_low, grad_upward, preferred_element_type=jnp.float32)
    up_bias_grad = jnp.sum(grad_upward, axis=(0, 1), dtype=jnp.float32)[None]
    partial_sum = jnp.einsum(
        "rtf,df->rtd", grad_upward, up_weight, preferred_element_type=jnp.float32
    )
    return (grad_up, grad_down, up_bias_grad, partial_sum)


def forward_block(inputs, weights, mask_pair, head_sizes, crossing):
    lowered = spread_tokens(inputs[0].astype(jnp.bfloat16), inputs[1].astype(jnp.bfloat16))
    projected = [project_local(lowered[stream], weights[stream]) for stream in range(2)]
    sources = stream_sources(projected, crossing)
    attended = [
        attend_local(
            sources[stream][0],
            sources[stream][1],
            sources[stream][2],
            mask_pair[stream],
            head_sizes[stream],
        )
        for stream in range(2)
    ]
    partials = [
        jnp.einsum(
            "rta,da->rtd",
            attended[stream][0],
            weights[stream][1],
            preferred_element_type=jnp.float32,
        )
        for stream in range(2)
    ]
    summed = tokens_from_partials(partials[0], partials[1])
    first_sums = []
    normed_rows = []
    for stream in range(2):
        bias_rows = weights[stream][6].astype(jnp.float32)
        gain_rows = weights[stream][7].astype(jnp.float32)
        first_sum = inputs[stream] + summed[stream] + bias_rows[0]
        first_sums.append(first_sum)
        normed_rows.append(layer_norm(first_sum, gain_rows[0], bias_rows[2]))
    normed_low = [normed_rows[stream].astype(jnp.bfloat16) for stream in range(2)]
    widened = spread_tokens(normed_low[0], normed_low[1])
    feeding = [(weights[stream][2], weights[stream][3], weights[stream][5]) for stream in range(2)]
    lifted = [
        mlp_forward(widened[stream], feeding[stream][0], feeding[stream][1], feeding[stream][2])
        for stream in range(2)
    ]
    down_sums = tokens_from_partials(lifted[0][2], lifted[1][2])
    results = []
    stored = []
    for stream in range(2):
        bias_rows = weights[stream][6].astype(jnp.float32)
        gain_rows = weights[stream][7].astype(jnp.float32)
        second_sum = normed_rows[stream] + down_sums[stream] + bias_rows[1]
        results.append(layer_norm(second_sum, gain_rows[1], bias_rows[3]))
        stored.append(
            (
                lowered[stream],
                projected[stream],
                attended[stream][1],
                attended[stream][0],
                first_sums[stream],
                widened[stream],
                lifted[stream][0],
                lifted[stream][1],
                second_sum,
                feeding[stream],
            )
        )
    return (results, stored)


def backward_block(incoming, stored, weights, mask_pair, head_sizes, crossing):
    grad_seconds = []
    second_lows = []
    down_bias_grads = []
    second_gain_grads = []
    second_shift_grads = []
    for stream in range(2):
        bias_rows = weights[stream][6].astype(jnp.float32)
        gain_rows = weights[stream][7].astype(jnp.float32)
        unused, norm_pullback = jax.vjp(layer_norm, stored[stream][8], gain_rows[1], bias_rows[3])
        grad_second, gain_grad, shift_grad = norm_pullback(incoming[stream])
        second_low = grad_second.astype(jnp.bfloat16)
        grad_seconds.append(grad_second)
        second_lows.append(second_low)
        down_bias_grads.append(jnp.sum(second_low, axis=(0, 1), dtype=jnp.float32))
        second_gain_grads.append(gain_grad)
        second_shift_grads.append(shift_grad)
    widened = spread_gradients(second_lows[0], second_lows[1])
    backed = [
        mlp_backward(
            widened[stream],
            stored[stream][5],
            stored[stream][6],
            stored[stream][7],
            stored[stream][9][0],
            stored[stream][9][1],
        )
        for stream in range(2)
    ]
    returned = gradients_from_partials(backed[0][3], backed[1][3])
    mlp_totals = [(backed[stream][0], backed[stream][1], backed[stream][2]) for stream in range(2)]
    grad_firsts = []
    first_lows = []
    out_bias_grads = []
    first_gain_grads = []
    first_shift_grads = []
    for stream in range(2):
        bias_rows = weights[stream][6].astype(jnp.float32)
        gain_rows = weights[stream][7].astype(jnp.float32)
        grad_normed = grad_seconds[stream] + returned[stream]
        unused, norm_pullback = jax.vjp(layer_norm, stored[stream][4], gain_rows[0], bias_rows[2])
        grad_first, gain_grad, shift_grad = norm_pullback(grad_normed)
        first_low = grad_first.astype(jnp.bfloat16)
        grad_firsts.append(grad_first)
        first_lows.append(first_low)
        out_bias_grads.append(jnp.sum(first_low, axis=(0, 1), dtype=jnp.float32))
        first_gain_grads.append(gain_grad)
        first_shift_grads.append(shift_grad)
    branch_wide = spread_gradients(first_lows[0], first_lows[1])
    out_grads = [
        jnp.einsum(
            "rtd,rta->da",
            branch_wide[stream],
            stored[stream][3],
            preferred_element_type=jnp.float32,
        )
        for stream in range(2)
    ]
    mixed_grads = [
        jnp.einsum(
            "rtd,da->rta",
            branch_wide[stream],
            weights[stream][1],
            preferred_element_type=jnp.float32,
        ).astype(jnp.bfloat16)
        for stream in range(2)
    ]
    sources = stream_sources([stored[0][1], stored[1][1]], crossing)
    attention_back = [
        attend_back(
            sources[stream][0],
            sources[stream][1],
            sources[stream][2],
            mask_pair[stream],
            stored[stream][2],
            mixed_grads[stream],
            head_sizes[stream],
        )
        for stream in range(2)
    ]
    partner = [1, 0] if crossing else [0, 1]
    proj_grads = [
        jnp.stack(
            (
                attention_back[stream][0],
                attention_back[partner[stream]][1],
                attention_back[partner[stream]][2],
            ),
            axis=2,
        )
        for stream in range(2)
    ]
    input_partials = [
        jnp.einsum(
            "rtca,dca->rtd",
            proj_grads[stream],
            weights[stream][0],
            preferred_element_type=jnp.float32,
        )
        for stream in range(2)
    ]
    input_returned = gradients_from_partials(input_partials[0], input_partials[1])
    next_grads = []
    matrices = []
    columns = []
    vectors = []
    for stream in range(2):
        next_grads.append(grad_firsts[stream] + input_returned[stream])
        proj_weight_grad = jnp.einsum(
            "rtd,rtca->dca",
            stored[stream][0],
            proj_grads[stream],
            preferred_element_type=jnp.float32,
        )
        head_bias_grad = jnp.stack(
            [
                jnp.sum(proj_grads[stream][:, :, 0], axis=(0, 1), dtype=jnp.float32),
                jnp.sum(proj_grads[stream][:, :, 2], axis=(0, 1), dtype=jnp.float32),
            ]
        )
        matrices.append(
            (proj_weight_grad, out_grads[stream], mlp_totals[stream][0], mlp_totals[stream][1])
        )
        columns.append((head_bias_grad, mlp_totals[stream][2]))
        vectors.append(
            (
                jnp.stack(
                    [
                        out_bias_grads[stream],
                        down_bias_grads[stream],
                        first_shift_grads[stream],
                        second_shift_grads[stream],
                    ]
                ),
                jnp.stack([first_gain_grads[stream], second_gain_grads[stream]]),
            )
        )
    return (next_grads, matrices, columns, vectors)


def pack_shard(proj, out, up, down):
    return jnp.concatenate([proj.reshape(proj.shape[0], -1), out, up, down], axis=1)


def cuts_of(proj, out, up):
    a = proj.shape[2]
    return (3 * a, 4 * a, 4 * a + up.shape[1])


def unpack_whole(gathered, proj, out, up, down):
    whole = gathered.reshape(-1, gathered.shape[-1])
    a, b, c = cuts_of(proj, out, up)
    return (whole[:, :a].reshape(-1, 3, proj.shape[2]), whole[:, a:b], whole[:, b:c], whole[:, c:])


def pack_whole(mats):
    whole = jnp.concatenate(
        [mats[0].reshape(mats[0].shape[0], -1), mats[1], mats[2], mats[3]], axis=1
    ).astype(jnp.bfloat16)
    return whole.reshape(4, 2, 4, whole.shape[0] // 32, whole.shape[1])


def unpack_shard(total, proj, out, up):
    a, b, c = cuts_of(proj, out, up)
    return (total[:, :a].reshape(proj.shape), total[:, a:b], total[:, b:c], total[:, c:])


def on_device(
    text_in,
    image_in,
    text_lengths,
    image_lengths,
    text_cotangent,
    image_cotangent,
    cross_text_proj,
    cross_text_out,
    cross_text_up,
    cross_text_down,
    cross_text_head_bias,
    cross_text_up_bias,
    cross_text_bias,
    cross_text_gain,
    cross_image_proj,
    cross_image_out,
    cross_image_up,
    cross_image_down,
    cross_image_head_bias,
    cross_image_up_bias,
    cross_image_bias,
    cross_image_gain,
    self_text_proj,
    self_text_out,
    self_text_up,
    self_text_down,
    self_text_head_bias,
    self_text_up_bias,
    self_text_bias,
    self_text_gain,
    self_image_proj,
    self_image_out,
    self_image_up,
    self_image_down,
    self_image_head_bias,
    self_image_up_bias,
    self_image_bias,
    self_image_gain,
):
    seq_count = lax.axis_size("seq")
    text_seg = segments(text_lengths, text_in.shape[1] * seq_count)
    image_seg = segments(image_lengths, image_in.shape[1] * seq_count)
    cross_masks = (
        text_seg[:, :, None] == image_seg[:, None, :],
        image_seg[:, :, None] == text_seg[:, None, :],
    )
    own_masks = (
        text_seg[:, :, None] == text_seg[:, None, :],
        image_seg[:, :, None] == image_seg[:, None, :],
    )
    cross_heads = (DC // HEADS_CROSS, DC // HEADS_CROSS)
    self_heads = (DT // HEADS_TEXT, DI // HEADS_IMAGE)
    packs = [
        pack_shard(cross_text_proj, cross_text_out, cross_text_up, cross_text_down),
        pack_shard(cross_image_proj, cross_image_out, cross_image_up, cross_image_down),
        pack_shard(self_text_proj, self_text_out, self_text_up, self_text_down),
        pack_shard(self_image_proj, self_image_out, self_image_up, self_image_down),
    ]
    gathered = gather_all(packs, ["xy", "yx", "xy", "yx"])
    cross_fetched = (
        unpack_whole(gathered[0], cross_text_proj, cross_text_out, cross_text_up, cross_text_down)
        + unpack_whole(gathered[1], cross_image_proj, cross_image_out, cross_image_up, cross_image_down)
    )
    cross_blocks = [
        (
            cross_fetched[0],
            cross_fetched[1],
            cross_fetched[2],
            cross_fetched[3],
            cross_text_head_bias,
            cross_text_up_bias,
            cross_text_bias,
            cross_text_gain,
        ),
        (
            cross_fetched[4],
            cross_fetched[5],
            cross_fetched[6],
            cross_fetched[7],
            cross_image_head_bias,
            cross_image_up_bias,
            cross_image_bias,
            cross_image_gain,
        ),
    ]
    middle, cross_stored = forward_block(
        (text_in.astype(jnp.float32), image_in.astype(jnp.float32)),
        cross_blocks,
        cross_masks,
        cross_heads,
        True,
    )
    self_fetched = (
        unpack_whole(gathered[2], self_text_proj, self_text_out, self_text_up, self_text_down)
        + unpack_whole(gathered[3], self_image_proj, self_image_out, self_image_up, self_image_down)
    )
    self_blocks = [
        (
            self_fetched[0],
            self_fetched[1],
            self_fetched[2],
            self_fetched[3],
            self_text_head_bias,
            self_text_up_bias,
            self_text_bias,
            self_text_gain,
        ),
        (
            self_fetched[4],
            self_fetched[5],
            self_fetched[6],
            self_fetched[7],
            self_image_head_bias,
            self_image_up_bias,
            self_image_bias,
            self_image_gain,
        ),
    ]
    final, self_stored = forward_block(
        (middle[0], middle[1]), self_blocks, own_masks, self_heads, False
    )
    self_back = backward_block(
        (text_cotangent.astype(jnp.float32), image_cotangent.astype(jnp.float32)),
        self_stored,
        self_blocks,
        own_masks,
        self_heads,
        False,
    )
    self_mats = self_back[1]
    cross_back = backward_block(
        (self_back[0][0], self_back[0][1]),
        cross_stored,
        cross_blocks,
        cross_masks,
        cross_heads,
        True,
    )
    cross_mats = cross_back[1]
    totals = reduce_all(
        [pack_whole(cross_mats[0]), pack_whole(cross_mats[1]), pack_whole(self_mats[0]), pack_whole(self_mats[1])],
        ["yx", "xy", "yx", "xy"],
    )
    cross_sums = (
        unpack_shard(totals[0], cross_text_proj, cross_text_out, cross_text_up)
        + unpack_shard(totals[1], cross_image_proj, cross_image_out, cross_image_up)
    )
    self_sums = (
        unpack_shard(totals[2], self_text_proj, self_text_out, self_text_up)
        + unpack_shard(totals[3], self_image_proj, self_image_out, self_image_up)
    )
    cross_cols = cross_back[2]
    self_cols = self_back[2]
    column_totals = lax.psum(
        (
            cross_cols[0][0],
            cross_cols[0][1],
            cross_cols[1][0],
            cross_cols[1][1],
            self_cols[0][0],
            self_cols[0][1],
            self_cols[1][0],
            self_cols[1][1],
        ),
        "rows",
    )
    cross_vecs = cross_back[3]
    self_vecs = self_back[3]
    vector_totals = lax.psum(
        (
            cross_vecs[0][0],
            cross_vecs[0][1],
            cross_vecs[1][0],
            cross_vecs[1][1],
            self_vecs[0][0],
            self_vecs[0][1],
            self_vecs[1][0],
            self_vecs[1][1],
        ),
        ("rows", "seq"),
    )
    text_grad = cross_back[0][0].astype(jnp.bfloat16)
    image_grad = cross_back[0][1].astype(jnp.bfloat16)
    return (
        final[0].astype(jnp.bfloat16),
        final[1].astype(jnp.bfloat16),
        text_grad,
        image_grad,
        cross_sums[0],
        cross_sums[1],
        cross_sums[2],
        cross_sums[3],
        column_totals[0],
        column_totals[1],
        vector_totals[0],
        vector_totals[1],
        cross_sums[4],
        cross_sums[5],
        cross_sums[6],
        cross_sums[7],
        column_totals[2],
        column_totals[3],
        vector_totals[2],
        vector_totals[3],
        self_sums[0],
        self_sums[1],
        self_sums[2],
        self_sums[3],
        column_totals[4],
        column_totals[5],
        vector_totals[4],
        vector_totals[5],
        self_sums[4],
        self_sums[5],
        self_sums[6],
        self_sums[7],
        column_totals[6],
        column_totals[7],
        vector_totals[6],
        vector_totals[7],
    )


def solution(mesh):
    placed = (
        P("rows", "seq", None),
        P("rows", "seq", None),
        P("rows", None),
        P("rows", None),
        P("rows", "seq", None),
        P("rows", "seq", None),
        P("rows", None, "seq"),
        P("rows", "seq"),
        P("rows", "seq"),
        P("rows", "seq"),
        P(None, "seq"),
        P(None, "seq"),
        P(),
        P(),
        P("rows", None, "seq"),
        P("rows", "seq"),
        P("rows", "seq"),
        P("rows", "seq"),
        P(None, "seq"),
        P(None, "seq"),
        P(),
        P(),
        P("rows", None, "seq"),
        P("rows", "seq"),
        P("rows", "seq"),
        P("rows", "seq"),
        P(None, "seq"),
        P(None, "seq"),
        P(),
        P(),
        P("rows", None, "seq"),
        P("rows", "seq"),
        P("rows", "seq"),
        P("rows", "seq"),
        P(None, "seq"),
        P(None, "seq"),
        P(),
        P(),
    )
    return jax.shard_map(
        on_device,
        mesh=mesh,
        in_specs=placed,
        out_specs=(
            P("rows", "seq", None),
            P("rows", "seq", None),
            P("rows", "seq", None),
            P("rows", "seq", None),
            P("rows", None, "seq"),
            P("rows", "seq"),
            P("rows", "seq"),
            P("rows", "seq"),
            P(None, "seq"),
            P(None, "seq"),
            P(),
            P(),
            P("rows", None, "seq"),
            P("rows", "seq"),
            P("rows", "seq"),
            P("rows", "seq"),
            P(None, "seq"),
            P(None, "seq"),
            P(),
            P(),
            P("rows", None, "seq"),
            P("rows", "seq"),
            P("rows", "seq"),
            P("rows", "seq"),
            P(None, "seq"),
            P(None, "seq"),
            P(),
            P(),
            P("rows", None, "seq"),
            P("rows", "seq"),
            P("rows", "seq"),
            P("rows", "seq"),
            P(None, "seq"),
            P(None, "seq"),
            P(),
            P(),
        ),
        check_vma=False,
    )
```

```python
import jax
import jax.numpy as jnp
from jax import lax
from jax.experimental import pallas as pl
from jax.experimental.pallas import tpu as pltpu
from jax.sharding import PartitionSpec as P

MESH = pl.DeviceIdType.MESH
VMEM = pltpu.VMEM
DMA = pltpu.SemaphoreType.DMA


class Place:
    def __init__(self):
        r = lax.axis_index("rows")
        s = lax.axis_index("seq")
        self.r, self.s = r, s
        self.x, self.z, self.y = r // 8, (r // 4) % 2, r % 4
        self.zh, self.c = s // 2, s % 2

    def dev(self, x, z, y):
        return ((x * 2 + z) * 4 + y, self.s)

    def along(self, axis, step):
        x, z, y = self.x, self.z, self.y
        if axis == "x":
            return self.dev((x + step) % 4, z, y)
        if axis == "y":
            return self.dev(x, z, (y + step) % 4)
        return self.dev(x, 1 - z, y)


def greet(devices):
    barrier = pltpu.get_barrier_semaphore()
    for device in devices:
        pl.semaphore_signal(barrier, inc=1, device_id=device, device_id_type=MESH)
    pl.semaphore_wait(barrier, len(devices))


def push(src, dst, sems, k, device):
    copy = pltpu.make_async_remote_copy(
        src_ref=src, dst_ref=dst, send_sem=sems.at[0, k], recv_sem=sems.at[1, k],
        device_id=device, device_id_type=MESH)
    copy.start()
    return copy


def gather_steps(me, own, buf, sems, order):
    x, z, y = me.x, me.z, me.y
    sent = []
    first = push(own, buf.at[x, z, y], sems, 0, me.along("z", 1))
    local = pltpu.make_async_copy(own, buf.at[x, z, y], sems.at[0, 9])
    local.start()
    yield
    local.wait()
    first.wait()
    k = 1
    for stage, axis in enumerate(order):
        if axis == "x":
            def view(step, half):
                at = (x + step) % 4
                if stage == 0:
                    return buf.at[at, :, y] if half is None else buf.at[at, half, y]
                return buf.at[at] if half is None else buf.at[at, :, pl.ds(2 * half, 2)]
        else:
            def view(step, half):
                at = (y + step) % 4
                if stage == 0:
                    return buf.at[x, :, at] if half is None else buf.at[x, half, at]
                return buf.at[:, :, at] if half is None else buf.at[pl.ds(2 * half, 2), :, at]
        right, left = me.along(axis, 1), me.along(axis, 3)
        to_right = push(view(0, None), view(0, None), sems, k, right)
        to_left = push(view(0, None), view(0, None), sems, k + 1, left)
        yield
        to_right.wait_recv()
        on_right = push(view(3, 0), view(3, 0), sems, k + 2, right)
        to_left.wait_recv()
        on_left = push(view(1, 1), view(1, 1), sems, k + 3, left)
        yield
        on_right.wait_recv()
        on_left.wait_recv()
        sent += [to_right, to_left, on_right, on_left]
        k += 4
    for copy in sent:
        copy.wait_send()


def run_together(steps):
    steps = list(steps)
    while steps:
        alive = []
        for step in steps:
            try:
                next(step)
                alive.append(step)
            except StopIteration:
                pass
        steps = alive


class Bag:
    pass


def call(kernel, inputs, outs, scratch, collective_id=None, hbm=()):
    names = list(inputs) + list(outs) + list(scratch)

    def body(*refs):
        bag = Bag()
        for name, ref in zip(names, refs):
            setattr(bag, name, ref)
        kernel(bag)

    def space(name):
        return pl.BlockSpec(memory_space=pl.ANY if name in hbm else pltpu.VMEM)
    results = pl.pallas_call(
        body, out_shape=list(outs.values()), in_specs=[space(n) for n in inputs], out_specs=[space(n) for n in outs],
        scratch_shapes=list(scratch.values()),
        compiler_params=pltpu.CompilerParams(collective_id=collective_id, has_side_effects=collective_id is not None,
                                             vmem_limit_bytes=63 * 1024 * 1024),
    )(*inputs.values())
    return dict(zip(outs, results))


class Trade:
    def __init__(self, me, pairs, sems):
        self.me, self.pairs, self.sems = me, pairs, sems

    def copies(self):
        return [pltpu.make_async_remote_copy(
            src_ref=src, dst_ref=dst, send_sem=self.sems.at[0, k], recv_sem=self.sems.at[1, k],
            device_id=self.me.along("z", 1), device_id_type=MESH) for k, (src, dst) in enumerate(self.pairs)]

    def start(self):
        @pl.when(self.me.zh == 1)
        def _():
            for copy in self.copies():
                copy.start()

        @pl.when(self.me.zh == 0)
        def _():
            for src, dst in self.pairs:
                dst[...] = src[...]

    def finish(self):
        @pl.when(self.me.zh == 1)
        def _():
            for copy in self.copies():
                copy.wait()


def near(me):
    return [me.along("z", 1), me.along("x", 1), me.along("x", 3), me.along("y", 1), me.along("y", 3)]


def front_kernel(g):
    me = Place()
    names = [f"{b}{i}" for b in range(2) for i in range(2)]
    for name in names:
        pack, proj = getattr(g, "pack" + name), getattr(g, "proj" + name)
        a = proj.shape[2]
        for c in range(3):
            pack[:, c * a:(c + 1) * a] = proj[c]
        at = 3 * a
        for part in ("out", "up", "down"):
            ref = getattr(g, part + name)
            pack[:, at:at + ref.shape[1]] = ref[...]
            at += ref.shape[1]
    greet(near(me))
    trade = Trade(me, [(g.x0, g.x0_got), (g.x1, g.x1_got), (g.lengths0, g.lengths0_got), (g.lengths1, g.lengths1_got),
                       (g.cot0, g.cot0_got), (g.cot1, g.cot1_got)], g.trade_sems)
    trade.start()
    run_together(gather_steps(me, getattr(g, "pack" + n), getattr(g, "whole" + n), getattr(g, "sems" + n),
                              "yx" if n[1] == "1" else "xy") for n in names)
    trade.finish()
    for name in ("x0", "x1", "cot0", "cot1", "lengths0", "lengths1"):
        getattr(g, name + "_out")[...] = getattr(g, name + "_got")[...]


def front(inputs):
    outs, scratch, hbm = {}, {}, []
    for b in range(2):
        for i in range(2):
            n = f"{b}{i}"
            rows = inputs["up" + n].shape[0]
            cols = 3 * inputs["proj" + n].shape[2] + sum(inputs[p + n].shape[1] for p in ("out", "up", "down"))
            scratch["pack" + n] = VMEM((rows, cols), jnp.bfloat16)
            scratch["sems" + n] = DMA((2, 10))
            outs["whole" + n] = jax.ShapeDtypeStruct((4, 2, 4, rows, cols), jnp.bfloat16)
            hbm.append("whole" + n)
    for name in ("x0", "x1", "cot0", "cot1", "lengths0", "lengths1"):
        scratch[name + "_got"] = VMEM(inputs[name].shape, inputs[name].dtype)
        outs[name + "_out"] = jax.ShapeDtypeStruct(inputs[name].shape, inputs[name].dtype)
    scratch["trade_sems"] = DMA((2, 6))
    return call(front_kernel, inputs, outs, scratch, 0, hbm)


def add_slabs(me, dst, src, count):
    def one(i, carry):
        at = dst(i)
        at[...] = (at[...].astype(jnp.float32) + src(i)[...].astype(jnp.float32)).astype(at.dtype)
        return carry
    lax.fori_loop(0, count, one, 0)


def reduce_steps(me, buf, out, halves, chunks, small_halves, small_chunks, last, sems, order):
    x, z, y = me.x, me.z, me.y
    sent = []
    k = 0
    for stage, axis in enumerate(order):
        half_in, chunk_in = (halves, chunks) if stage == 0 else (small_halves, small_chunks)
        place = x if axis == "x" else y
        if axis == "x":
            def view(step, half=None):
                at = (x + step) % 4
                if stage == 0:
                    return buf.at[at] if half is None else buf.at[at, :, pl.ds(2 * half, 2)]
                return buf.at[at, :, y] if half is None else buf.at[at, half, y]
        else:
            def view(step, half=None):
                at = (y + step) % 4
                if stage == 0:
                    return buf.at[:, :, at] if half is None else buf.at[pl.ds(2 * half, 2), :, at]
                return buf.at[x, :, at] if half is None else buf.at[x, half, at]
        right, left = me.along(axis, 1), me.along(axis, 3)
        a = push(view(2, 0), half_in.at[0], sems, k, right)
        b = push(view(2, 1), half_in.at[1], sems, k + 1, left)
        yield
        if stage == 0:
            def half_slab(step, half):
                at = (place + step) % 4
                if axis == "x":
                    return lambda i: buf.at[at, i // 2, 2 * half + i % 2]
                return lambda i: buf.at[2 * half + i // 2, i % 2, at]

            def full_slab(i):
                return buf.at[x, i // 4, i % 4] if axis == "x" else buf.at[i // 2, i % 2, y]
            n_half, n_full = 4, 8
        else:
            def half_slab(step, half):
                at = (place + step) % 4
                return lambda i: buf.at[at, half, y] if axis == "x" else buf.at[x, half, at]

            def full_slab(i):
                return buf.at[x, i, y]
            n_half, n_full = 1, 2

        def in_slab(ref, d):
            if stage == 1:
                return (lambda i: ref.at[d]) if ref is half_in else (lambda i: ref.at[d, i])
            wide = ref.shape[2]
            return lambda i: ref.at[d, i // wide, i % wide]
        a.wait_recv()
        add_slabs(me, half_slab(1, 0), in_slab(half_in, 0), n_half)
        c = push(view(1), chunk_in.at[0], sems, k + 2, right)
        b.wait_recv()
        add_slabs(me, half_slab(3, 1), in_slab(half_in, 1), n_half)
        d = push(view(3), chunk_in.at[1], sems, k + 3, left)
        yield
        c.wait_recv()
        add_slabs(me, full_slab, in_slab(chunk_in, 0), n_full)
        d.wait_recv()
        add_slabs(me, full_slab, in_slab(chunk_in, 1), n_full)
        sent += [a, b, c, d]
        k += 4
    e = push(buf.at[x, 1 - z, y], last, sems, k, me.along("z", 1))
    yield
    e.wait_recv()
    out[...] = buf[x, z, y].astype(jnp.float32) + last[...].astype(jnp.float32)
    sent.append(e)
    for copy in sent:
        copy.wait_send()


def reduce_scratch(order, rows, cols):
    lead = (2, 4) if order[0] == "x" else (4, 2)
    bf = jnp.bfloat16
    return [VMEM((2, 2, 2, rows, cols), bf), VMEM((2,) + lead + (rows, cols), bf),
            VMEM((2, rows, cols), bf), VMEM((2, 2, rows, cols), bf), VMEM((rows, cols), bf), DMA((2, 9))]


def total_steps(me, team, vecs, cols, got, slots, small, vec_out, col_out, sems):
    wide = vecs.shape[1] // 4

    def quarter(k):
        return pl.ds(pl.multiple_of(k * wide, 128), wide)
    mates = ((team.sib, team.sib_slab), (team.mate, team.mate_slab), (team.far, team.far_slab))
    sent = [push(vecs.at[:, quarter(slab)], got.at[k], sems, k, device) for k, (device, slab) in enumerate(mates)]
    yield
    for copy in sent:
        copy.wait_recv()
    small[:, :wide] = vecs[:, quarter(team.own)] + got[0] + got[1] + got[2]
    small[:, wide:] = cols[...]
    k = 3
    for stage, (axis, place, count) in enumerate((("x", me.x, 4), ("y", me.y, 4), ("z", me.z, 2))):
        slots[stage, place] = small[...]
        copies = [push(slots.at[stage, place], slots.at[stage, place], sems, k + n, me.along(axis, n + 1))
                  for n in range(count - 1)]
        k += count - 1
        yield
        for copy in copies:
            copy.wait_recv()
        total = slots[stage, 0] + slots[stage, 1]
        if count == 4:
            total = total + slots[stage, 2] + slots[stage, 3]
        small[...] = total
        sent += copies
    col_out[...] = small[:, wide:]
    vec_out[:, quarter(team.own)] = small[:, :wide]
    last = [push(vec_out.at[:, quarter(team.own)], vec_out.at[:, quarter(team.own)], sems, k + n, device)
            for n, (device, slab) in enumerate(mates)]
    yield
    for copy in last:
        copy.wait_recv()
    for copy in sent + last:
        copy.wait_send()


def back_kernel(g):
    me = Place()
    team = Team(me)
    names = [f"{b}{i}" for b in range(2) for i in range(2)]
    loads = []
    for k, n in enumerate(names):
        loads.append(pltpu.make_async_copy(getattr(g, "dw" + n), getattr(g, "held" + n), g.load_sems.at[k]))
        loads[-1].start()
    greet(near(me) + [me.along("x", 2), me.along("y", 2), team.sib, team.mate, team.far])
    trade = Trade(me, [(g.out0, g.out0_got), (g.out1, g.out1_got), (g.grad0, g.grad0_got), (g.grad1, g.grad1_got)],
                  g.trade_sems)
    trade.start()
    for copy in loads:
        copy.wait()
    steps = []
    for n in names:
        steps.append(reduce_steps(me, getattr(g, "held" + n), getattr(g, "sum" + n),
                                  *[getattr(g, f"scratch{n}_{k}") for k in range(6)], "xy" if n[1] == "1" else "yx"))
    steps.append(total_steps(me, team, g.vecs, g.cols, g.vec_got, g.slots, g.small, g.vec_sum, g.cols_sum, g.total_sems))
    run_together(steps)
    trade.finish()
    g.vecs_out[...] = g.vec_sum[...]
    for name in ("out0", "out1", "grad0", "grad1"):
        getattr(g, name + "_done")[...] = getattr(g, name + "_got")[...]


def back(inputs):
    outs, scratch, hbm = {}, {}, []
    for b in range(2):
        for i in range(2):
            n = f"{b}{i}"
            shape = inputs["dw" + n].shape
            hbm.append("dw" + n)
            scratch["held" + n] = VMEM(shape, jnp.bfloat16)
            for k, s in enumerate(reduce_scratch("xy" if i else "yx", shape[3], shape[4])):
                scratch[f"scratch{n}_{k}"] = s
            outs["sum" + n] = jax.ShapeDtypeStruct(shape[3:], jnp.float32)
    vec, col = inputs["vecs"].shape, inputs["cols"].shape
    f32 = jnp.float32
    scratch["vec_got"] = VMEM((3, 8, vec[1] // 4), f32)
    scratch["small"] = VMEM((8, vec[1] // 4 + col[1]), f32)
    scratch["slots"] = VMEM((3, 4, 8, vec[1] // 4 + col[1]), f32)
    scratch["vec_sum"] = VMEM(vec, f32)
    scratch["load_sems"] = DMA((4,))
    scratch["trade_sems"] = DMA((2, 4))
    scratch["total_sems"] = DMA((2, 13))
    outs["vecs_out"] = jax.ShapeDtypeStruct(vec, f32)
    outs["cols_sum"] = jax.ShapeDtypeStruct(col, f32)
    for name in ("out0", "out1", "grad0", "grad1"):
        scratch[name + "_got"] = VMEM(inputs[name].shape, inputs[name].dtype)
        outs[name + "_done"] = jax.ShapeDtypeStruct(inputs[name].shape, inputs[name].dtype)
    return call(back_kernel, inputs, outs, scratch, 1, hbm)


def finish_kernel(g):
    for i, count in enumerate((32, 36)):
        for name in ("out", "grad"):
            src, dst = getattr(g, f"{name}{i}"), getattr(g, f"{name}{i}_done")
            if i == 0:
                dst[...] = src[...].reshape(dst.shape)
            else:
                whole = src[...].astype(jnp.float32)
                for b in range(3):
                    dst[b] = whole[b * count:(b + 1) * count].astype(dst.dtype)
    at = 0
    for k, n in enumerate(f"{b}{i}" for b in range(2) for i in range(2)):
        total = getattr(g, "sum" + n)
        proj, out, up, down = [getattr(g, p + n) for p in ("proj", "out", "up", "down")]
        a, f = proj.shape[2], up.shape[1]
        for c in range(3):
            proj[c] = total[:, c * a:(c + 1) * a]
        out[...] = total[:, 3 * a:4 * a]
        up[...] = total[:, 4 * a:4 * a + f]
        down[...] = total[:, 4 * a + f:]
        head_bias, up_bias, bias, gain = [getattr(g, p + n) for p in ("head_bias", "up_bias", "bias", "gain")]
        head_bias[0:1] = g.cols[2 * k:2 * k + 1, :a]
        head_bias[1:2] = g.cols[2 * k:2 * k + 1, 2 * a:3 * a]
        up_bias[...] = g.cols[2 * k + 1:2 * k + 2, :f]
        width = bias.shape[1]
        bias[...] = g.vecs[0:4, at:at + width]
        gain[...] = g.vecs[4:6, at:at + width]
        at += width


F32, BF16 = jnp.float32, jnp.bfloat16
NN, NT, TN = ((1,), (0,)), ((1,), (1,)), ((0,), (0,))
EPS = 1e-05
MASKED = -1000000000.0


class Shape:
    def __init__(self, part, width, inner, hidden, head):
        self.part, self.width, self.inner, self.hidden, self.head = part, width, inner, hidden, head
        self.tokens = 4 * part
        self.out_at = 3 * inner
        self.up_at = 4 * inner
        self.down_at = 4 * inner + hidden
        self.columns = 4 * inner + 2 * hidden


def dot(a, b, dims):
    return lax.dot_general(a, b, (dims, ((), ())), preferred_element_type=F32)


def loop(count, body):
    def step(i, carry):
        body(i)
        return carry
    lax.fori_loop(0, count, step, 0)


def lanes(i, size=256, base=0):
    return pl.ds(pl.multiple_of(base + i * size, 128), size)


def rows16(i):
    return pl.ds(pl.multiple_of(i * 16, 16), 16)


class Team:
    def __init__(self, me):
        self.me = me
        self.own = me.s
        self.sib_slab = me.zh * 2 + 1 - me.c
        self.mate_slab = (1 - me.zh) * 2 + me.c
        self.far_slab = (1 - me.zh) * 2 + 1 - me.c
        self.sib = (me.r, self.sib_slab)
        self.far = ((me.x * 2 + 1 - me.z) * 4 + me.y, self.far_slab)
        self.mate = ((me.x * 2 + 1 - me.z) * 4 + me.y, self.mate_slab)


class Wire:
    def __init__(self, team, part, from_sib, from_mate, sems):
        self.team, self.part, self.from_sib, self.from_mate, self.sems = team, part, from_sib, from_mate, sems

    def gather_start(self, buf):
        t = self.team
        self.buf = buf
        self.over = push(buf.at[t.own], buf.at[t.own], self.sems, 0, t.mate)
        self.beside = push(buf.at[t.own], buf.at[t.own], self.sems, 1, t.sib)

    def gather_mid(self):
        t = self.team
        self.over.wait_recv()
        self.on = push(self.buf.at[t.mate_slab], self.buf.at[t.mate_slab], self.sems, 2, t.sib)

    def gather_end(self):
        self.beside.wait_recv()
        self.on.wait_recv()
        for copy in (self.over, self.beside, self.on):
            copy.wait_send()

    def reduce_start(self):
        t = self.team
        self.a = push(self.part.at[t.far_slab], self.from_sib.at[0], self.sems, 3, t.sib)
        self.b = push(self.part.at[t.sib_slab], self.from_sib.at[1], self.sems, 4, t.sib)

    def reduce_mid(self):
        t = self.team
        self.a.wait_recv()
        part, from_sib = self.part, self.from_sib

        def add(i):
            rows = rows16(i)
            part[t.mate_slab, rows] = (part[t.mate_slab, rows].astype(F32) + from_sib[0, rows].astype(F32)).astype(BF16)
        loop(part.shape[1] // 16, add)
        self.d = push(part.at[t.mate_slab], self.from_mate, self.sems, 5, t.mate)

    def reduce_end(self):
        self.b.wait_recv()
        self.d.wait_recv()
        for copy in (self.a, self.b, self.d):
            copy.wait_send()

    def total(self, rows):
        return (self.part[self.team.own, rows].astype(F32) + self.from_sib[1, rows].astype(F32)
                + self.from_mate[rows].astype(F32))


def normal(value):
    centre = jnp.mean(value, axis=-1, keepdims=True)
    moved = value - centre
    scale = lax.rsqrt(jnp.mean(moved * moved, axis=-1, keepdims=True) + EPS)
    return moved * scale, scale


def flat(ref):
    value = ref[...]
    return value.reshape(value.shape[0] * value.shape[1], value.shape[2])


def project(sh, v):
    whole = flat(v.xf)
    if sh.inner % 256:
        v.qkv[...] = (dot(whole, v.w[:, :3 * sh.inner], NN) + v.offset[...]).astype(BF16)
    else:
        def one(i):
            at = lanes(i)
            v.qkv[:, at] = (dot(whole, v.w[:, at], NN) + v.offset[:, at]).astype(BF16)
        loop(3 * sh.inner // 256, one)


def probabilities(query, key, col_ids, row_ids, scale):
    raw = dot(query, key, NT)
    scores = jnp.where(col_ids == row_ids, raw * scale, MASKED)
    grown = jnp.exp(scores - jnp.max(scores, axis=-1, keepdims=True))
    return grown * (1.0 / jnp.sum(grown, axis=-1, keepdims=True))


def attend(sh, v, kv):
    h, a = sh.head, sh.inner
    row_ids = kv.ids_row[...]
    for n in range(a // h):
        key = kv.qkv[:, a + n * h:a + (n + 1) * h]
        value = kv.qkv[:, 2 * a + n * h:2 * a + (n + 1) * h]

        def one(i):
            rows = pl.ds(pl.multiple_of(i * sh.part, 16), sh.part)
            p = probabilities(v.qkv[rows, n * h:(n + 1) * h], key, v.ids_col[rows], row_ids, h ** -0.5)
            v.mixed[rows, n * h:(n + 1) * h] = dot(p.astype(BF16), value, NN).astype(BF16)
        loop(4, one)


def spread_out(sh, v, left, at, size):
    def one(i):
        rows = lanes(i)
        result = dot(left, v.w[rows, at:at + size], NT)
        v.wire.part[:, :, rows] = result.reshape(4, sh.part, 256).astype(BF16)
    loop(sh.width // 256, one)


def norm_forward(sh, v, base, sums, which, result, low):
    bias = v.bias[pl.ds(which, 1)].astype(F32)
    shift = v.bias[pl.ds(2 + which, 1)].astype(F32)
    gain = v.gain[pl.ds(which, 1)].astype(F32)

    def one(i):
        rows = rows16(i)
        value = base[rows] + v.wire.total(rows) + bias
        sums[rows] = value
        value = normal(value)[0] * gain + shift
        result[rows] = value
        low[rows] = value.astype(BF16)
    loop(sh.part // 16, one)


def feed(sh, v):
    whole = flat(v.nf)
    k = (2.0 / jnp.pi) ** 0.5

    def one(i):
        at = lanes(i)
        u = dot(whole, v.w[:, lanes(i, 256, sh.up_at)], NN) + v.up_bias[:, at].astype(F32)
        square = u * u
        t = jnp.tanh(k * u * (1.0 + 0.044715 * square))
        half = 0.5 * (1.0 + t)
        v.active[:, at] = (u * half).astype(BF16)
        v.slope[:, at] = half + 0.5 * u * (1.0 - t * t) * (k * (1.0 + 3 * 0.044715 * square))
    loop(sh.hidden // 256, one)
    spread_out(sh, v, v.active[...], sh.down_at, sh.hidden)


def norm_backward(sh, v, grad, sums, which, result, low, vec, bias_row):
    gain = v.gain[pl.ds(which, 1)].astype(F32)

    def fold(value):
        return value[:8] + value[8:]

    def one(i, carry):
        rows = rows16(i)
        g = grad(rows)
        n, scale = normal(sums[rows])
        gn = g * gain
        out = scale * (gn - jnp.mean(gn, axis=-1, keepdims=True) - n * jnp.mean(gn * n, axis=-1, keepdims=True))
        rounded = out.astype(BF16)
        result[rows] = out
        low[rows] = rounded
        return (carry[0] + fold(rounded.astype(F32)), carry[1] + fold(g), carry[2] + fold(g * n))
    zero = jnp.zeros((8, sh.width), F32)
    totals = lax.fori_loop(0, sh.part // 16, one, (zero, zero, zero))
    for at, total in zip((bias_row, 2 + which, 4 + which), totals):
        vec[pl.ds(at, 1)] = jnp.sum(total, axis=0, keepdims=True)


def weight_grad(sh, v, left, right, at):
    def one(i):
        cut = lanes(i)
        piece = left[:, :, cut].reshape(sh.tokens, 256)
        v.dw[cut, at:at + right.shape[1]] = dot(piece, right[...], TN).astype(BF16)
    loop(sh.width // 256, one)


def feed_back(sh, v):
    whole = flat(v.gs)

    def one(i):
        at = lanes(i)
        grad = dot(whole, v.w[:, lanes(i, 256, sh.down_at)], NN)
        gu = (grad * v.slope[:, at]).astype(BF16)
        v.gu[:, at] = gu
        v.col_up[:, at] = jnp.sum(gu.astype(F32), axis=0, keepdims=True)
    loop(sh.hidden // 256, one)
    spread_out(sh, v, v.gu[...], sh.up_at, sh.hidden)


def attend_back(sh, v, kv, p_ref, s_ref):
    h, a = sh.head, sh.inner
    width = kv.qkv.shape[0]
    row_ids = kv.ids_row[...]
    scale = h ** -0.5
    for n in range(a // h):
        q_at, k_at, v_at = [slice(c * a + n * h, c * a + (n + 1) * h) for c in range(3)]
        key, value = kv.qkv[:, k_at], kv.qkv[:, v_at]

        def one(i):
            rows = pl.ds(pl.multiple_of(i * sh.part, 16), sh.part)
            p = probabilities(v.qkv[rows, q_at], key, v.ids_col[rows], row_ids, scale)
            gp = dot(v.gm[rows, q_at], value, NT)
            gs = (p * (gp - jnp.sum(gp * p, axis=-1, keepdims=True)) * scale).astype(BF16)
            p_ref[rows, :width] = p.astype(BF16)
            s_ref[rows, :width] = gs
            v.gp[rows, q_at] = dot(gs, key, NN).astype(BF16)
        loop(4, one)
        kv.gp[:, k_at] = dot(s_ref[:sh.tokens, :width], v.qkv[:, q_at], TN).astype(BF16)
        kv.gp[:, v_at] = dot(p_ref[:sh.tokens, :width], v.gm[:, q_at], TN).astype(BF16)


def block_forward(shapes, views, crossing, base, result, low):
    for v in views:
        v.wire.gather_start(v.xf)
    for v in views:
        v.wire.gather_mid()
    for sh, v in zip(shapes, views):
        v.wire.gather_end()
        project(sh, v)
    for i, (sh, v) in enumerate(zip(shapes, views)):
        attend(sh, v, views[1 - i] if crossing else v)
        spread_out(sh, v, v.mixed[...], sh.out_at, sh.inner)
        v.wire.reduce_start()
        if i == 1:
            views[0].wire.reduce_mid()
    views[1].wire.reduce_mid()
    for i, (sh, v) in enumerate(zip(shapes, views)):
        v.wire.reduce_end()
        norm_forward(sh, v, base[i], v.first, 0, v.normed, v.nf.at[v.wire.team.own])
        v.wire.gather_start(v.nf)
    for i, (sh, v) in enumerate(zip(shapes, views)):
        v.wire.gather_mid()
        v.wire.gather_end()
        feed(sh, v)
        v.wire.reduce_start()
        if i == 1:
            views[0].wire.reduce_mid()
    views[1].wire.reduce_mid()
    for i, (sh, v) in enumerate(zip(shapes, views)):
        v.wire.reduce_end()
        norm_forward(sh, v, v.normed, v.second, 1, result[i], low[i])


def block_backward(shapes, views, crossing, grads, results, scratch):
    own = views[0].wire.team.own
    for i, (sh, v) in enumerate(zip(shapes, views)):
        norm_backward(sh, v, grads[i], v.second, 1, v.normed, v.gs.at[own], v.vec, 1)
        v.wire.gather_start(v.gs)
    for i, (sh, v) in enumerate(zip(shapes, views)):
        v.wire.gather_mid()
        v.wire.gather_end()
        feed_back(sh, v)
        v.wire.reduce_start()
        if i == 1:
            views[0].wire.reduce_mid()
    views[1].wire.reduce_mid()
    weight_grad(shapes[0], views[0], views[0].gs, views[0].active, shapes[0].down_at)
    for i, (sh, v) in enumerate(zip(shapes, views)):
        v.wire.reduce_end()
        norm_backward(sh, v, lambda rows, v=v: v.normed[rows] + v.wire.total(rows), v.first, 0, v.normed,
                      v.gb.at[own], v.vec, 0)
        v.wire.gather_start(v.gb)
    weight_grad(shapes[1], views[1], views[1].gs, views[1].active, shapes[1].down_at)
    for v in views:
        v.wire.gather_mid()
    weight_grad(shapes[0], views[0], views[0].nf, views[0].gu, shapes[0].up_at)
    weight_grad(shapes[1], views[1], views[1].nf, views[1].gu, shapes[1].up_at)
    for i, (sh, v) in enumerate(zip(shapes, views)):
        v.wire.gather_end()
        v.gm[...] = dot(flat(v.gb), v.w[:, sh.out_at:sh.out_at + sh.inner], NN).astype(BF16)
    for i, (sh, v) in enumerate(zip(shapes, views)):
        attend_back(sh, v, views[1 - i] if crossing else v, *scratch)
    for i, (sh, v) in enumerate(zip(shapes, views)):
        spread_out(sh, v, v.gp[...], 0, 3 * sh.inner)
        v.wire.reduce_start()
        if i == 1:
            views[0].wire.reduce_mid()
    views[1].wire.reduce_mid()
    for sh, v in zip(shapes, views):
        weight_grad(sh, v, v.gb, v.mixed, sh.out_at)
        weight_grad(sh, v, v.xf, v.gp, 0)
        v.col_proj[:, :3 * sh.inner] = jnp.sum(v.gp[...].astype(F32), axis=0, keepdims=True)
    for i, (sh, v) in enumerate(zip(shapes, views)):
        v.wire.reduce_end()

        def one(j):
            rows = rows16(j)
            results[i](rows, v.normed[rows] + v.wire.total(rows))
        loop(sh.part // 16, one)


SHAPES = ((Shape(96, 768, 256, 768, 128), Shape(112, 1024, 256, 256, 128)),
          (Shape(96, 768, 192, 768, 64), Shape(112, 1024, 256, 256, 128)))


def set_ids(ref, lengths, per_part, part, axis):
    token = lax.broadcasted_iota(jnp.int32, ref.shape, axis)

    def over(value, size, most):
        return sum((value >= k * size).astype(jnp.int32) for k in range(1, most))
    p = over(token, part, 4)
    within = token - part * p
    row = over(within, per_part, 4)
    position = p * per_part + within - per_part * row
    ids = jnp.full(ref.shape, -1, jnp.int32)
    for b in range(3):
        bound = jnp.zeros((1, 1), jnp.int32)
        seg = jnp.full(ref.shape, 4 * b, jnp.int32)
        for j in range(4):
            bound = bound + lengths[b:b + 1, j:j + 1]
            seg = seg + (position >= bound).astype(jnp.int32)
        ids = jnp.where(row == b, seg, ids)
    ref[...] = ids.astype(F32)


def middle_kernel(g):
    me = Place()
    team = Team(me)
    loads = []
    for b in range(2):
        for i in range(2):
            copy = pltpu.make_async_copy(getattr(g, f"w_in{b}{i}"), getattr(g, f"w{b}{i}"), g.load_sem.at[2 * b + i])
            copy.start()
            loads.append(copy)
    greet([team.sib, team.mate])
    wires = [Wire(team, getattr(g, f"part{i}"), getattr(g, f"from_sib{i}"), getattr(g, f"from_mate{i}"),
                  getattr(g, f"sems{i}")) for i in range(2)]
    views = []
    lane = 0
    for b in range(2):
        pair = []
        for i in range(2):
            v = Bag()
            v.wire = wires[i]
            for name in ("w", "head_bias", "up_bias", "bias", "gain", "offset", "xf", "qkv", "mixed", "nf", "slope",
                         "active", "first", "second", "dw", "gm", "gp"):
                setattr(v, name, getattr(g, f"{name}{b}{i}"))
            for name in ("ids_col", "ids_row", "normed", "gs", "gb", "gu"):
                setattr(v, name, getattr(g, f"{name}{i}"))
            sh = SHAPES[b][i]
            k = 2 * (2 * b + i)
            v.vec = g.vecs.at[:, lane:lane + sh.width]
            lane += sh.width
            v.col_proj = g.cols.at[k:k + 1]
            v.col_up = g.cols.at[k + 1:k + 2]
            a = sh.inner
            v.offset[:, :a] = v.head_bias[0:1].astype(F32)
            v.offset[:, a:2 * a] = jnp.zeros((1, a), F32)
            v.offset[:, 2 * a:] = v.head_bias[1:2].astype(F32)
            pair.append(v)
        views.append(pair)
    g.vecs[...] = jnp.zeros_like(g.vecs)
    g.cols[...] = jnp.zeros_like(g.cols)
    for i, per_part in enumerate((32, 36)):
        for axis, name in enumerate(("ids_col", "ids_row")):
            set_ids(getattr(g, f"{name}{i}"), getattr(g, f"lengths{i}"), per_part, SHAPES[0][i].part, axis)
    x_in = (g.x0, g.x1)
    base = (g.base0, g.base1)
    for i in range(2):
        def one(j, i=i):
            rows = rows16(j)
            views[0][i].xf[team.own, rows] = x_in[i][rows]
            base[i][rows] = x_in[i][rows].astype(F32)
        loop(SHAPES[0][i].part // 16, one)
    loads[0].wait()
    loads[1].wait()
    block_forward(SHAPES[0], views[0], True, base, base, [views[1][i].xf.at[team.own] for i in range(2)])
    loads[2].wait()
    loads[3].wait()
    block_forward(SHAPES[1], views[1], False, base, base, (g.out0, g.out1))
    cots = (g.cot0, g.cot1)
    scratch = (g.p_ref, g.s_ref)

    def keep(i):
        def put(rows, value):
            base[i][rows] = value
        return put

    def give(i):
        out = (g.grad0, g.grad1)[i]

        def put(rows, value):
            out[rows] = value.astype(BF16)
        return put
    block_backward(SHAPES[1], views[1], False, [lambda rows, i=i: cots[i][rows].astype(F32) for i in range(2)],
                   [keep(0), keep(1)], scratch)
    saves = []
    for i in range(2):
        saves.append(pltpu.make_async_copy(views[1][i].dw, getattr(g, f"dw_out1{i}"), g.load_sem.at[2 + i]))
        saves[-1].start()
    block_backward(SHAPES[0], views[0], True, [lambda rows, i=i: base[i][rows] for i in range(2)],
                   [give(0), give(1)], scratch)
    for i in range(2):
        saves.append(pltpu.make_async_copy(views[0][i].dw, getattr(g, f"dw_out0{i}"), g.load_sem.at[i]))
        saves[-1].start()
    for copy in saves:
        copy.wait()


def middle(inputs):
    outs, scratch, hbm = {}, {}, []
    for i in range(2):
        sh = SHAPES[0][i]
        outs[f"out{i}"] = jax.ShapeDtypeStruct((sh.part, sh.width), BF16)
        outs[f"grad{i}"] = jax.ShapeDtypeStruct((sh.part, sh.width), BF16)
        scratch[f"base{i}"] = VMEM((sh.part, sh.width), F32)
        scratch[f"normed{i}"] = VMEM((sh.part, sh.width), F32)
        for name in ("gs", "gb"):
            scratch[f"{name}{i}"] = VMEM((4, sh.part, sh.width), BF16)
        scratch[f"gu{i}"] = VMEM((sh.tokens, sh.hidden), BF16)
        scratch[f"part{i}"] = VMEM((4, sh.part, sh.width), BF16)
        scratch[f"from_sib{i}"] = VMEM((2, sh.part, sh.width), BF16)
        scratch[f"from_mate{i}"] = VMEM((sh.part, sh.width), BF16)
        scratch[f"sems{i}"] = DMA((2, 6))
        scratch[f"ids_col{i}"] = VMEM((sh.tokens, 1), F32)
        scratch[f"ids_row{i}"] = VMEM((1, sh.tokens), F32)
    scratch["p_ref"] = VMEM((448, 448), BF16)
    scratch["s_ref"] = VMEM((448, 448), BF16)
    scratch["load_sem"] = DMA((4,))
    outs["vecs"] = jax.ShapeDtypeStruct((8, 2 * (768 + 1024)), F32)
    outs["cols"] = jax.ShapeDtypeStruct((8, 768), F32)
    for b in range(2):
        for i in range(2):
            sh = SHAPES[b][i]
            outs[f"dw_out{b}{i}"] = jax.ShapeDtypeStruct((sh.width, sh.columns), BF16)
            hbm += [f"dw_out{b}{i}", f"w_in{b}{i}"]
            scratch[f"offset{b}{i}"] = VMEM((1, 3 * sh.inner), F32)
            for name, shape, kind in (
                    ("w", (sh.width, sh.columns), BF16), ("dw", (sh.width, sh.columns), BF16),
                    ("xf", (4, sh.part, sh.width), BF16), ("nf", (4, sh.part, sh.width), BF16),
                    ("qkv", (sh.tokens, 3 * sh.inner), BF16), ("gp", (sh.tokens, 3 * sh.inner), BF16),
                    ("mixed", (sh.tokens, sh.inner), BF16), ("gm", (sh.tokens, sh.inner), BF16),
                    ("slope", (sh.tokens, sh.hidden), F32),
                    ("active", (sh.tokens, sh.hidden), BF16), ("first", (sh.part, sh.width), F32),
                    ("second", (sh.part, sh.width), F32)):
                scratch[f"{name}{b}{i}"] = VMEM(shape, kind)
    return call(middle_kernel, inputs, outs, scratch, 2, hbm)


def on_device(*args):
    text_in, image_in, text_lengths, image_lengths, text_cot, image_cot = args[:6]
    matrix_names = ("proj", "out", "up", "down")
    small_names = ("head_bias", "up_bias", "bias", "gain")

    def rows_of(value):
        value = value.reshape(-1, value.shape[-1])
        return jnp.pad(value, ((0, -value.shape[0] % 16), (0, 0)))
    tensors = {}
    for b in range(2):
        for i in range(2):
            at = 6 + 16 * b + 8 * i
            for name, value in zip(matrix_names + small_names, args[at:at + 8]):
                tensors[f"{name}{b}{i}"] = value.transpose(1, 0, 2) if name == "proj" else value
    names = [f"{b}{i}" for b in range(2) for i in range(2)]
    first = {"x0": rows_of(text_in), "x1": rows_of(image_in), "cot0": rows_of(text_cot), "cot1": rows_of(image_cot),
             "lengths0": text_lengths, "lengths1": image_lengths}
    moved = list(first)
    for n in names:
        for p in matrix_names:
            first[p + n] = tensors[p + n]
    got = front(first)
    inputs = {name: got[name + "_out"] for name in moved}
    for n in names:
        whole = got["whole" + n]
        inputs["w_in" + n] = whole.reshape(-1, whole.shape[-1])
        for p in small_names:
            inputs[p + n] = tensors[p + n]
    done = middle(inputs)
    last = {name: done[name] for name in ("vecs", "cols", "out0", "out1", "grad0", "grad1")}
    for n in names:
        whole = done["dw_out" + n]
        last["dw" + n] = whole.reshape(4, 2, 4, whole.shape[0] // 32, whole.shape[1])
    sums = back(last)
    ends = {"vecs": sums["vecs_out"], "cols": sums["cols_sum"]}
    outs = {}
    for name, like in (("out0", text_in), ("out1", image_in), ("grad0", text_in), ("grad1", image_in)):
        ends[name] = sums[name + "_done"]
        outs[name + "_done"] = jax.ShapeDtypeStruct(like.shape, like.dtype)
    for n in names:
        ends["sum" + n] = sums["sum" + n]
        for p in matrix_names + small_names:
            outs[p + n] = jax.ShapeDtypeStruct(tensors[p + n].shape, jnp.float32)
    return tuple(value.transpose(1, 0, 2) if name.startswith("proj") else value
                 for name, value in call(finish_kernel, ends, outs, {}).items())


def solution(mesh):
    kinds = [P("rows", None, "seq"), P("rows", "seq"), P("rows", "seq"), P("rows", "seq"), P(None, "seq"),
             P(None, "seq"), P(), P()] * 4
    position = P("rows", "seq", None)
    return jax.shard_map(
        on_device, mesh=mesh,
        in_specs=tuple([position, position, P("rows", None), P("rows", None), position, position] + kinds),
        out_specs=tuple([position] * 4 + kinds), check_vma=False)
```

```python
import jax
import jax.numpy as jnp
from jax import lax
from jax.experimental import pallas as pl
from jax.experimental.pallas import tpu as pltpu
from jax.sharding import PartitionSpec as P

MESH = pl.DeviceIdType.MESH
VMEM = pltpu.VMEM
DMA = pltpu.SemaphoreType.DMA
F32, BF16 = jnp.float32, jnp.bfloat16
NN, NT, TN = ((1,), (0,)), ((1,), (1,)), ((0,), (0,))
EPS = 1e-05
MASKED = -1000000000.0
LIMIT = 63 * 1024 * 1024


class Bag:
    pass


RATE = {"x+": 45e3, "x-": 45e3, "y+": 45e3, "y-": 45e3, "z": 45e3, "over": 45e3, "beside": 200e3}
DELAY = {"beside": 1.0}


class Plan:
    def __init__(self):
        self.now = 0.0
        self.free = {}
        self.done = set()

    def post(self, *event):
        self.done.add(event)

    def arrival(self, link, size):
        begin = max(self.now, self.free.get(link, 0.0))
        self.free[link] = begin + size / RATE[link]
        return self.free[link] + DELAY.get(link, 1.5)

    def run(self, tasks):
        waiting = [[rank, n, task, ("at", 0.0)] for n, (rank, task) in enumerate(tasks)]
        while waiting:
            best = None
            for entry in waiting:
                kind, what = entry[3]
                if kind == "event":
                    if what not in self.done:
                        continue
                    due = self.now
                else:
                    due = max(what, self.now)
                key = (due, entry[0], entry[1])
                if best is None or key < best[0]:
                    best = (key, entry)
            assert best is not None, "stuck"
            entry = best[1]
            self.now = best[0][0]
            try:
                need = next(entry[2])
            except StopIteration:
                waiting.remove(entry)
                continue
            if need[0] == "for":
                self.now += need[1]
                need = ("at", self.now)
            entry[3] = need


class Place:
    def __init__(self, plan):
        r = lax.axis_index("rows")
        s = lax.axis_index("seq")
        self.plan = plan
        self.r, self.s = r, s
        self.x, self.z, self.y = r // 8, (r // 4) % 2, r % 4
        self.zh, self.c = s // 2, s % 2
        self.own = s
        self.sib_slab = self.zh * 2 + 1 - self.c
        self.mate_slab = (1 - self.zh) * 2 + self.c
        self.far_slab = (1 - self.zh) * 2 + 1 - self.c
        self.sib = (r, self.sib_slab)
        across = (self.x * 2 + 1 - self.z) * 4 + self.y
        self.mate = (across, self.mate_slab)
        self.far = (across, self.far_slab)

    def along(self, axis, step):
        x, z, y = self.x, self.z, self.y
        if axis == "x":
            x = (x + step) % 4
        elif axis == "y":
            y = (y + step) % 4
        else:
            z = 1 - z
        return ((x * 2 + z) * 4 + y, self.s)

    def push(self, src, dst, sems, k, device, link):
        copy = pltpu.make_async_remote_copy(
            src_ref=src, dst_ref=dst, send_sem=sems.at[0, k], recv_sem=sems.at[1, k],
            device_id=device, device_id_type=MESH)
        copy.start()
        size = src.dtype.itemsize
        for n in src.shape:
            size *= n
        copy.due = self.plan.arrival(link, size)
        return copy


def greet(devices):
    barrier = pltpu.get_barrier_semaphore()
    for device in devices:
        pl.semaphore_signal(barrier, inc=1, device_id=device, device_id_type=MESH)
    pl.semaphore_wait(barrier, len(devices))


def at(copy, *more):
    return ("at", max(c.due for c in (copy,) + more))


def need(*event):
    return ("event", event)


def spent(cost):
    return ("for", cost)


class Trade:
    def __init__(self, me, pairs, sems):
        self.me, self.pairs, self.sems = me, pairs, sems

    def copies(self):
        return [pltpu.make_async_remote_copy(
            src_ref=src, dst_ref=dst, send_sem=self.sems.at[0, k], recv_sem=self.sems.at[1, k],
            device_id=self.me.along("z", 1), device_id_type=MESH) for k, (src, dst) in enumerate(self.pairs)]

    def start(self):
        @pl.when(self.me.zh == 1)
        def _():
            for copy in self.copies():
                copy.start()

        @pl.when(self.me.zh == 0)
        def _():
            for src, dst in self.pairs:
                dst[...] = src[...]

    def finish(self):
        @pl.when(self.me.zh == 1)
        def _():
            for copy in self.copies():
                copy.wait()


def dot(a, b, dims):
    return lax.dot_general(a, b, (dims, ((), ())), preferred_element_type=F32)


def loop(count, body):
    def step(i, carry):
        body(i)
        return carry
    lax.fori_loop(0, count, step, 0)


def lanes(i, size=256, base=0):
    return pl.ds(pl.multiple_of(base + i * size, 128), size)


def span(start, size):
    return pl.ds(pl.multiple_of(start, 16), size)


def add_rows(dst, start, src, first, count):
    def one(i):
        to, come = span(start + 16 * i, 16), span(first + 16 * i, 16)
        total = dst[to].astype(F32)
        for ref in src:
            total = total + ref[come].astype(F32)
        dst[to] = total.astype(dst.dtype)
    loop(count // 16, one)


def add_slabs(dst, src, count):
    def one(i):
        to = dst(i)
        total = to[...].astype(F32)
        for ref in src(i):
            total = total + ref[...].astype(F32)
        to[...] = total.astype(to.dtype)
    loop(count, one)


def middle_of(columns):
    return columns // 256 * 128


def gather_text(me, pieces, w, sems, started, ready):
    columns = w.shape[1]
    cut = middle_of(columns)
    x, z, y = me.x, me.z, me.y
    right, left = me.along("y", 1), me.along("y", 3)
    a = me.push(pieces.at[y], pieces.at[y], sems, 0, right, "y+")
    b = me.push(pieces.at[y], pieces.at[y], sems, 1, left, "y-")
    yield at(a)
    a.wait_recv()
    before = pieces.at[(y + 3) % 4, :, :cut]
    c = me.push(before, before, sems, 2, right, "y+")
    yield at(b)
    b.wait_recv()
    after = pieces.at[(y + 1) % 4, :, cut:]
    d = me.push(after, after, sems, 3, left, "y-")
    yield at(c, d)
    c.wait_recv()
    d.wait_recv()
    base = (x * 2 + z) * 96
    w[span(base, 96)] = pieces[...].astype(F32).reshape(96, columns).astype(BF16)
    yield spent(0.3)
    block = w.at[span(base, 96)]
    e = me.push(block, block, sems, 4, me.along("z", 1), "z")
    yield at(e)
    e.wait_recv()
    right, left = me.along("x", 1), me.along("x", 3)
    block = w.at[span(192 * x, 192)]
    f = me.push(block, block, sems, 5, right, "x+")
    g = me.push(block, block, sems, 6, left, "x-")
    me.plan.post(*started)
    yield at(f)
    f.wait_recv()
    block = w.at[span(192 * ((x + 3) % 4), 96)]
    h = me.push(block, block, sems, 7, right, "x+")
    yield at(g)
    g.wait_recv()
    block = w.at[span(192 * ((x + 1) % 4) + 96, 96)]
    i = me.push(block, block, sems, 8, left, "x-")
    yield at(h, i)
    h.wait_recv()
    i.wait_recv()
    me.plan.post(*ready)
    for copy in (a, b, c, d, e, f, g, h, i):
        copy.wait_send()


def gather_image(me, w, sems, started, ready):
    x, z, y = me.x, me.z, me.y
    e = me.push(w.at[x, z, y], w.at[x, z, y], sems, 0, me.along("z", 1), "z")
    yield at(e)
    e.wait_recv()
    right, left = me.along("x", 1), me.along("x", 3)
    a = me.push(w.at[x, :, y], w.at[x, :, y], sems, 1, right, "x+")
    b = me.push(w.at[x, :, y], w.at[x, :, y], sems, 2, left, "x-")
    yield at(a)
    a.wait_recv()
    block = w.at[(x + 3) % 4, 0, y]
    c = me.push(block, block, sems, 3, right, "x+")
    yield at(b)
    b.wait_recv()
    block = w.at[(x + 1) % 4, 1, y]
    d = me.push(block, block, sems, 4, left, "x-")
    yield at(c, d)
    c.wait_recv()
    d.wait_recv()
    right, left = me.along("y", 1), me.along("y", 3)
    f = me.push(w.at[:, :, y], w.at[:, :, y], sems, 5, right, "y+")
    g = me.push(w.at[:, :, y], w.at[:, :, y], sems, 6, left, "y-")
    me.plan.post(*started)
    yield at(f)
    f.wait_recv()
    block = w.at[0:2, :, (y + 3) % 4]
    h = me.push(block, block, sems, 7, right, "y+")
    yield at(g)
    g.wait_recv()
    block = w.at[2:4, :, (y + 1) % 4]
    i = me.push(block, block, sems, 8, left, "y-")
    yield at(h, i)
    h.wait_recv()
    i.wait_recv()
    me.plan.post(*ready)
    for copy in (a, b, c, d, e, f, g, h, i):
        copy.wait_send()


def reduce_text(me, dw, out, t, sems):
    columns = dw.shape[1]
    cut = middle_of(columns)
    cost = columns / 2000.0
    x, z, y = me.x, me.z, me.y
    right, left = me.along("x", 1), me.along("x", 3)
    far = 192 * ((x + 2) % 4)
    a = me.push(dw.at[span(far, 96)], t.halves.at[0], sems, 0, right, "x+")
    b = me.push(dw.at[span(far + 96, 96)], t.halves.at[1], sems, 1, left, "x-")
    yield at(a)
    a.wait_recv()
    first = 192 * ((x + 1) % 4)
    add_rows(dw, first, [t.halves.at[0]], 0, 96)
    c = me.push(dw.at[span(first, 192)], t.chunks.at[0], sems, 2, right, "x+")
    yield spent(0.4 * cost)
    yield at(b)
    b.wait_recv()
    first = 192 * ((x + 3) % 4)
    add_rows(dw, first + 96, [t.halves.at[1]], 0, 96)
    d = me.push(dw.at[span(first, 192)], t.chunks.at[1], sems, 3, left, "x-")
    yield spent(0.4 * cost)
    yield at(c, d)
    c.wait_recv()
    d.wait_recv()
    add_rows(dw, 192 * x + 96 * (1 - z), [t.chunks.at[0], t.chunks.at[1]], 96 * (1 - z), 96)
    e = me.push(dw.at[span(192 * x + 96 * (1 - z), 96)], t.across, sems, 4, me.along("z", 1), "z")
    add_rows(dw, 192 * x + 96 * z, [t.chunks.at[0], t.chunks.at[1]], 96 * z, 96)
    yield spent(1.2 * cost)
    yield at(e)
    e.wait_recv()
    total = dw[span(192 * x + 96 * z, 96)].astype(F32) + t.across[...].astype(F32)
    t.pieces[...] = total.reshape(4, 24, columns).astype(BF16)
    yield spent(0.4 * cost)
    right, left = me.along("y", 1), me.along("y", 3)
    pieces = t.pieces
    f = me.push(pieces.at[(y + 2) % 4, :, :cut], t.small_halves.at[0, :, :cut], sems, 5, right, "y+")
    g = me.push(pieces.at[(y + 2) % 4, :, cut:], t.small_halves.at[1, :, cut:], sems, 6, left, "y-")
    yield at(f, g)
    f.wait_recv()
    to = (y + 1) % 4
    pieces[to, :, :cut] = (pieces[to, :, :cut].astype(F32) + t.small_halves[0, :, :cut].astype(F32)).astype(BF16)
    h = me.push(pieces.at[to], t.small_chunks.at[0], sems, 7, right, "y+")
    g.wait_recv()
    to = (y + 3) % 4
    pieces[to, :, cut:] = (pieces[to, :, cut:].astype(F32) + t.small_halves[1, :, cut:].astype(F32)).astype(BF16)
    i = me.push(pieces.at[to], t.small_chunks.at[1], sems, 8, left, "y-")
    yield spent(0.2 * cost)
    yield at(h, i)
    h.wait_recv()
    i.wait_recv()
    out[...] = pieces[y].astype(F32) + t.small_chunks[0].astype(F32) + t.small_chunks[1].astype(F32)
    for copy in (a, b, c, d, e, f, g, h, i):
        copy.wait_send()
    yield spent(0.2 * cost)


def reduce_image(me, dw, out, t, sems):
    cost = dw.shape[4] / 1500.0
    x, z, y = me.x, me.z, me.y
    right, left = me.along("y", 1), me.along("y", 3)
    far = (y + 2) % 4
    a = me.push(dw.at[0:2, :, far], t.halves.at[0], sems, 0, right, "y+")
    b = me.push(dw.at[2:4, :, far], t.halves.at[1], sems, 1, left, "y-")
    yield at(a)
    a.wait_recv()
    to = (y + 1) % 4
    add_slabs(lambda i: dw.at[i // 2, i % 2, to], lambda i: [t.halves.at[0, i // 2, i % 2]], 4)
    c = me.push(dw.at[:, :, to], t.chunks.at[0], sems, 2, right, "y+")
    yield spent(0.5 * cost)
    yield at(b)
    b.wait_recv()
    back = (y + 3) % 4
    add_slabs(lambda i: dw.at[2 + i // 2, i % 2, back], lambda i: [t.halves.at[1, i // 2, i % 2]], 4)
    d = me.push(dw.at[:, :, back], t.chunks.at[1], sems, 3, left, "y-")
    yield spent(0.5 * cost)
    yield at(c, d)
    c.wait_recv()
    d.wait_recv()
    add_slabs(lambda i: dw.at[i // 2, i % 2, y], lambda i: [t.chunks.at[n, i // 2, i % 2] for n in range(2)], 8)
    right, left = me.along("x", 1), me.along("x", 3)
    far = (x + 2) % 4
    e = me.push(dw.at[far, 0, y], t.small_halves.at[0], sems, 4, right, "x+")
    f = me.push(dw.at[far, 1, y], t.small_halves.at[1], sems, 5, left, "x-")
    yield spent(1.5 * cost)
    yield at(e, f)
    e.wait_recv()
    to = (x + 1) % 4
    add_slabs(lambda i: dw.at[to, 0, y], lambda i: [t.small_halves.at[0]], 1)
    g = me.push(dw.at[to, :, y], t.small_chunks.at[0], sems, 6, right, "x+")
    f.wait_recv()
    back = (x + 3) % 4
    add_slabs(lambda i: dw.at[back, 1, y], lambda i: [t.small_halves.at[1]], 1)
    h = me.push(dw.at[back, :, y], t.small_chunks.at[1], sems, 7, left, "x-")
    yield spent(0.3 * cost)
    yield at(g, h)
    g.wait_recv()
    h.wait_recv()
    add_slabs(lambda i: dw.at[x, i, y], lambda i: [t.small_chunks.at[n, i] for n in range(2)], 2)
    i = me.push(dw.at[x, 1 - z, y], t.across, sems, 8, me.along("z", 1), "z")
    yield spent(0.3 * cost)
    yield at(i)
    i.wait_recv()
    out[...] = dw[x, z, y].astype(F32) + t.across[...].astype(F32)
    for copy in (a, b, c, d, e, f, g, h, i):
        copy.wait_send()
    yield spent(0.2 * cost)


def total_steps(me, vecs, cols, got, slots, small, vec_out, col_out, sems):
    wide = vecs.shape[1] // 4

    def quarter(k):
        return pl.ds(pl.multiple_of(k * wide, 128), wide)
    mates = ((me.sib, me.sib_slab, "beside"), (me.mate, me.mate_slab, "over"), (me.far, me.far_slab, "over"))
    sent = [me.push(vecs.at[:, quarter(slab)], got.at[k], sems, k, device, link)
            for k, (device, slab, link) in enumerate(mates)]
    yield at(*sent)
    for copy in sent:
        copy.wait_recv()
    small[:, :wide] = vecs[:, quarter(me.own)] + got[0] + got[1] + got[2]
    small[:, wide:] = cols[...]
    k = 3
    for stage, (axis, place, count) in enumerate((("x", me.x, 4), ("y", me.y, 4), ("z", me.z, 2))):
        slots[stage, place] = small[...]
        copies = [me.push(slots.at[stage, place], slots.at[stage, place], sems, k + n, me.along(axis, n + 1),
                          axis + "++-"[n] if count == 4 else "z") for n in range(count - 1)]
        k += count - 1
        yield at(*copies)
        for copy in copies:
            copy.wait_recv()
        total = slots[stage, 0] + slots[stage, 1]
        if count == 4:
            total = total + slots[stage, 2] + slots[stage, 3]
        small[...] = total
        sent += copies
    col_out[...] = small[:, wide:]
    vec_out[:, quarter(me.own)] = small[:, :wide]
    mine = vec_out.at[:, quarter(me.own)]
    last = [me.push(mine, mine, sems, k + n, device, link) for n, (device, slab, link) in enumerate(mates)]
    yield at(*last)
    for copy in last:
        copy.wait_recv()
    for copy in sent + last:
        copy.wait_send()


class Wire:
    def __init__(self, me, part, from_sib, from_mate, sems):
        self.me, self.part, self.from_sib, self.from_mate, self.sems = me, part, from_sib, from_mate, sems

    def gather(self, buf):
        me = self.me
        mine, theirs = buf.at[me.own], buf.at[me.mate_slab]
        over = me.push(mine, mine, self.sems, 0, me.mate, "over")
        beside = me.push(mine, mine, self.sems, 1, me.sib, "beside")
        yield at(over)
        over.wait_recv()
        on = me.push(theirs, theirs, self.sems, 2, me.sib, "beside")
        yield at(beside, on)
        beside.wait_recv()
        on.wait_recv()
        for copy in (over, beside, on):
            copy.wait_send()

    def reduce(self):
        me, part, from_sib = self.me, self.part, self.from_sib
        a = me.push(part.at[me.far_slab], from_sib.at[0], self.sems, 3, me.sib, "beside")
        b = me.push(part.at[me.sib_slab], from_sib.at[1], self.sems, 4, me.sib, "beside")
        yield at(a)
        a.wait_recv()
        for i in range(part.shape[1] // 16):
            rows = pl.ds(16 * i, 16)
            part[me.mate_slab, rows] = (
                part[me.mate_slab, rows].astype(F32) + from_sib[0, rows].astype(F32)).astype(BF16)
        d = me.push(part.at[me.mate_slab], self.from_mate, self.sems, 5, me.mate, "over")
        yield spent(0.3)
        yield at(b, d)
        b.wait_recv()
        d.wait_recv()
        for copy in (a, b, d):
            copy.wait_send()

    def total(self, rows):
        return (self.part[self.me.own, rows].astype(F32) + self.from_sib[1, rows].astype(F32)
                + self.from_mate[rows].astype(F32))


class Shape:
    def __init__(self, stream, part, length, width, inner, hidden, head):
        self.stream, self.part, self.length, self.width = stream, part, length, width
        self.inner, self.hidden, self.head = inner, hidden, head
        self.tokens = 4 * part
        self.count = length // 4
        self.down_at = hidden
        self.out_at = 2 * hidden
        self.proj_columns = -(-3 * inner // 128) * 128
        self.rest_columns = -(-(inner + 2 * hidden) // 128) * 128


SHAPES = ((Shape(0, 96, 128, 768, 256, 768, 128), Shape(1, 112, 144, 1024, 256, 256, 128)),
          (Shape(0, 96, 128, 768, 192, 768, 64), Shape(1, 112, 144, 1024, 256, 256, 128)))
WIDEST = {0: (768, 1792), 1: (768, 768)}


def columns_of(sh, w, cols):
    if sh.stream == 0:
        return w[:, cols]
    return w[:, :, :, :, cols].reshape(sh.width, -1)


def rows_of(sh, w, i, cols):
    if sh.stream == 0:
        return w[lanes(i), cols]
    value = w[i, :, :, :, cols]
    return value.reshape(256, value.shape[-1])


def set_rows(sh, w, i, cols, value):
    if sh.stream == 0:
        w[lanes(i), cols] = value
    else:
        w[i, :, :, :, cols] = value.reshape(2, 4, 32, value.shape[-1])


def normal(value):
    centre = jnp.mean(value, axis=-1, keepdims=True)
    moved = value - centre
    scale = lax.rsqrt(jnp.mean(moved * moved, axis=-1, keepdims=True) + EPS)
    return moved * scale, scale


def flat(ref):
    value = ref[...]
    return value.reshape(value.shape[0] * value.shape[1], value.shape[2])


def by_row(sh, v, value):
    if sh.stream == 0:
        parts = value.reshape(4, 3, 32, value.shape[-1])
        return jnp.concatenate([parts[:, b].reshape(128, -1) for b in range(3)], axis=0)
    return dot(v.to_rows[...], value, NN).astype(BF16)


def put_by_part(sh, ref, b, cols, value):
    for p in range(4):
        ref[p * 96 + 32 * b:p * 96 + 32 * b + 32, cols] = value[32 * p:32 * p + 32]


def project(sh, v):
    whole = flat(v.xf)
    if sh.inner % 256:
        cols = slice(0, 3 * sh.inner)
        v.qkv[...] = by_row(sh, v, (dot(whole, columns_of(sh, v.wp, cols), NN) + v.offset[...]).astype(BF16))
    else:
        def one(i):
            cols = lanes(i)
            v.qkv[:, cols] = by_row(
                sh, v, (dot(whole, columns_of(sh, v.wp, cols), NN) + v.offset[:, cols]).astype(BF16))
        loop(3 * sh.inner // 256, one)


def probabilities(query, key, col_ids, row_ids, scale):
    raw = dot(query, key, NT)
    scores = jnp.where(col_ids == row_ids, raw * scale, MASKED)
    grown = jnp.exp(scores - jnp.max(scores, axis=-1, keepdims=True))
    return grown * (1.0 / jnp.sum(grown, axis=-1, keepdims=True))


def attend(sh, v, kv, key_length):
    h, a = sh.head, sh.inner
    for b in range(3):
        mine = pl.ds(b * sh.length, sh.length)
        theirs = pl.ds(b * key_length, key_length)
        for n in range(a // h):
            q_at, k_at, v_at = [slice(c * a + n * h, c * a + (n + 1) * h) for c in range(3)]
            p = probabilities(v.qkv[mine, q_at], kv.qkv[theirs, k_at], v.ids_col[b], kv.ids_row[b], h ** -0.5)
            result = dot(p.astype(BF16), kv.qkv[theirs, v_at], NN).astype(BF16)
            if sh.stream == 0:
                put_by_part(sh, v.mixed, b, q_at, result)
            else:
                v.mixed_rows[mine, q_at] = result
        yield spent(0.5)
    if sh.stream == 1:
        v.mixed[...] = dot(v.to_parts[...], v.mixed_rows[...], NN).astype(BF16)
        yield spent(0.3)


def spread_out(sh, v, left, w, cols):
    def one(i):
        result = dot(left, rows_of(sh, w, i, cols), NT)
        v.wire.part[:, :, lanes(i)] = result.reshape(4, sh.part, 256).astype(BF16)
    loop(sh.width // 256, one)


def norm_forward(sh, v, base, sums, which, result, low):
    bias = v.bias[which:which + 1].astype(F32)
    shift = v.bias[2 + which:3 + which].astype(F32)
    gain = v.gain[which:which + 1].astype(F32)
    for i in range(sh.part // 16):
        rows = pl.ds(16 * i, 16)
        value = base[rows] + v.wire.total(rows) + bias
        sums[rows] = value
        value = normal(value)[0] * gain + shift
        result[rows] = value
        low[rows] = value.astype(BF16)


def feed(sh, v):
    whole = flat(v.nf)
    k = (2.0 / jnp.pi) ** 0.5

    def one(i):
        cols = lanes(i)
        u = dot(whole, columns_of(sh, v.wr, cols), NN) + v.up_bias[:, cols].astype(F32)
        square = u * u
        t = jnp.tanh(k * u * (1.0 + 0.044715 * square))
        half = 0.5 * (1.0 + t)
        v.active[:, cols] = (u * half).astype(BF16)
        v.slope[:, cols] = (half + 0.5 * u * (1.0 - t * t) * (k * (1.0 + 3 * 0.044715 * square))).astype(BF16)
    loop(sh.hidden // 256, one)


def norm_backward(sh, v, grad, sums, which, result, low, bias_row):
    gain = v.gain[which:which + 1].astype(F32)

    def fold(value):
        return value[:8] + value[8:]
    totals = None
    for i in range(sh.part // 16):
        rows = pl.ds(16 * i, 16)
        g = grad(rows)
        n, scale = normal(sums[rows])
        gn = g * gain
        out = scale * (gn - jnp.mean(gn, axis=-1, keepdims=True) - n * jnp.mean(gn * n, axis=-1, keepdims=True))
        rounded = out.astype(BF16)
        result[rows] = out
        low[rows] = rounded
        terms = (fold(rounded.astype(F32)), fold(g), fold(g * n))
        totals = terms if totals is None else tuple(x + y for x, y in zip(totals, terms))
    for at_row, total in zip((bias_row, 2 + which, 4 + which), totals):
        v.vec[at_row:at_row + 1] = jnp.sum(total, axis=0, keepdims=True)


def weight_grad(sh, left, right, dw, start):
    cols = slice(start, start + right.shape[1])

    def one(i):
        piece = left[:, :, lanes(i)].reshape(sh.tokens, 256)
        set_rows(sh, dw, i, cols, dot(piece, right[...], TN).astype(BF16))
    loop(sh.width // 256, one)


def feed_back(sh, v):
    whole = flat(v.gs)

    def one(i):
        cols = lanes(i)
        grad = dot(whole, columns_of(sh, v.wr, lanes(i, 256, sh.down_at)), NN)
        gu = (grad * v.slope[:, cols].astype(F32)).astype(BF16)
        v.gu[:, cols] = gu
        v.col_up[:, cols] = jnp.sum(gu.astype(F32), axis=0, keepdims=True)
    loop(sh.hidden // 256, one)


def attend_back(sh, v, key_sh, kv):
    h, a = sh.head, sh.inner
    scale = h ** -0.5

    def put(to_sh, to, b, cols, value):
        value = value.astype(BF16)
        if to_sh.stream == 0:
            put_by_part(to_sh, to.gp, b, cols, value)
        else:
            to.gp_rows[pl.ds(b * to_sh.length, to_sh.length), cols] = value
    for b in range(3):
        mine = pl.ds(b * sh.length, sh.length)
        theirs = pl.ds(b * key_sh.length, key_sh.length)
        for n in range(a // h):
            q_at, k_at, v_at = [slice(c * a + n * h, c * a + (n + 1) * h) for c in range(3)]
            query, key, value = v.qkv[mine, q_at], kv.qkv[theirs, k_at], kv.qkv[theirs, v_at]
            grad = v.gm[mine, q_at]
            p = probabilities(query, key, v.ids_col[b], kv.ids_row[b], scale)
            gp = dot(grad, value, NT)
            gs = (p * (gp - jnp.sum(gp * p, axis=-1, keepdims=True)) * scale).astype(BF16)
            put(sh, v, b, q_at, dot(gs, key, NN))
            put(key_sh, kv, b, k_at, dot(gs, query, TN))
            put(key_sh, kv, b, v_at, dot(p.astype(BF16), grad, TN))
        yield spent(1.0)


def set_ids(ref, lengths, axis):
    shape = ref.shape[1:]
    position = lax.broadcasted_iota(jnp.int32, shape, axis)
    for b in range(3):
        bound = jnp.zeros((1, 1), jnp.int32)
        seg = jnp.zeros(shape, jnp.int32)
        for j in range(4):
            bound = bound + lengths[b:b + 1, j:j + 1]
            seg = seg + (position >= bound).astype(jnp.int32)
        ref[b] = seg.astype(F32)


def row_of_part(token):
    def over(value, size, most):
        return sum((value >= k * size).astype(jnp.int32) for k in range(1, most))
    p = over(token, 112, 4)
    within = token - 112 * p
    row = over(within, 36, 4)
    return jnp.where(row < 3, 144 * row + 36 * p + within - 36 * row, -1)


def stream(plan, i, views, base, cot, outs, grads):
    other = 1 - i
    for b in range(2):
        sh, v = SHAPES[b][i], views[b][i]
        key_stream = other if b == 0 else i
        kv = views[b][key_stream]
        own = v.wire.me.own
        yield from v.wire.gather(v.xf)
        yield need("wp", b, i)
        project(sh, v)
        yield spent(1.0)
        plan.post("qkv", b, i)
        yield need("qkv", b, key_stream)
        yield from attend(sh, v, kv, SHAPES[b][key_stream].length)
        yield need("wr", b, i)
        spread_out(sh, v, v.mixed[...], v.wr, slice(sh.out_at, sh.out_at + sh.inner))
        yield spent(0.6)
        yield from v.wire.reduce()
        norm_forward(sh, v, base, v.first, 0, v.normed, v.nf.at[own])
        yield spent(0.7)
        yield from v.wire.gather(v.nf)
        feed(sh, v)
        yield spent(2.0 if i == 0 else 1.0)
        spread_out(sh, v, v.active[...], v.wr, slice(sh.down_at, sh.down_at + sh.hidden))
        yield spent(1.2 if i == 0 else 0.7)
        yield from v.wire.reduce()
        norm_forward(sh, v, v.normed, v.second, 1, base, views[1][i].xf.at[own] if b == 0 else outs)
        yield spent(0.7)
    plan.post("out", i)
    for b in (1, 0):
        sh, v = SHAPES[b][i], views[b][i]
        key_stream = other if b == 0 else i
        key_sh, kv = SHAPES[b][key_stream], views[b][key_stream]
        own = v.wire.me.own
        norm_backward(sh, v, (lambda rows: cot[rows].astype(F32)) if b == 1 else (lambda rows: base[rows]),
                      v.second, 1, v.normed, v.gs.at[own], 1)
        yield spent(1.0)
        yield from v.wire.gather(v.gs)
        plan.post("gs", b, i)
        if b == 0:
            yield need("dwu", 1, i)
        feed_back(sh, v)
        yield spent(1.5 if i == 0 else 0.8)
        plan.post("gu", b, i)
        if b == 0:
            yield need("dwo", 1, i)
        spread_out(sh, v, v.gu[...], v.wr, slice(0, sh.hidden))
        yield spent(1.2 if i == 0 else 0.7)
        yield from v.wire.reduce()
        norm_backward(sh, v, lambda rows, v=v: v.normed[rows] + v.wire.total(rows), v.first, 0, v.normed,
                      v.gb.at[own], 0)
        yield spent(1.0)
        yield from v.wire.gather(v.gb)
        plan.post("gb", b, i)
        v.gm[...] = by_row(sh, v, dot(flat(v.gb), columns_of(sh, v.wr, slice(sh.out_at, sh.out_at + sh.inner)),
                                      NN).astype(BF16))
        yield spent(0.8)
        if b == 0:
            yield need("dwp", 1, 0)
            yield need("dwp", 1, 1)
        yield from attend_back(sh, v, key_sh, kv)
        plan.post("attended", b, i)
        yield need("attended", b, key_stream)
        if i == 1:
            v.gp[...] = dot(v.to_parts[...], v.gp_rows[...], NN).astype(BF16)
            yield spent(0.5)
        plan.post("gp", b, i)
        if b == 1:
            yield need("dwd", 1, i)
        spread_out(sh, v, v.gp[...], v.wp, slice(0, 3 * sh.inner))
        yield spent(1.3)
        yield from v.wire.reduce()
        for j in range(sh.part // 16):
            rows = pl.ds(16 * j, 16)
            value = v.normed[rows] + v.wire.total(rows)
            if b == 1:
                base[rows] = value
            else:
                grads[rows] = value.astype(BF16)
        yield spent(0.3)
    plan.post("grad", i)


def matrix_grads(plan, b, i, v):
    sh = SHAPES[b][i]
    yield need("gs", b, i)
    weight_grad(sh, v.gs, v.active, v.dwr, sh.down_at)
    yield spent(1.6 if i == 0 else 0.9)
    plan.post("dwd", b, i)
    yield need("gu", b, i)
    weight_grad(sh, v.nf, v.gu, v.dwr, 0)
    yield spent(1.6 if i == 0 else 0.9)
    plan.post("dwu", b, i)
    yield need("gb", b, i)
    weight_grad(sh, v.gb, v.mixed, v.dwr, sh.out_at)
    yield spent(0.8)
    plan.post("dwo", b, i)
    plan.post("dwr", b, i)
    yield need("gp", b, i)
    weight_grad(sh, v.xf, v.gp, v.dwp, 0)
    v.col_proj[:, :3 * sh.inner] = jnp.sum(v.gp[...].astype(F32), axis=0, keepdims=True)
    yield spent(2.0)
    plan.post("dwp", b, i)


def sums_of(plan, me, kind, i, views, outs, t, sems, credit):
    neighbours = [me.along("z", 1), me.along("x", 1), me.along("x", 3), me.along("y", 1), me.along("y", 3)]
    for b in (1, 0):
        yield need("dw" + kind, b, i)
        if b == 0:
            pl.semaphore_wait(credit, 5)
        dw = getattr(views[b][i], "dw" + kind)
        if i == 0:
            wide = dw.shape[1]
            cut = Bag()
            cut.halves, cut.chunks, cut.across = t.halves.at[:, :, :wide], t.chunks.at[:, :, :wide], t.across.at[:, :wide]
            cut.pieces = t.pieces.at[:, :, :wide]
            cut.small_halves, cut.small_chunks = t.small_halves.at[:, :, :wide], t.small_chunks.at[:, :, :wide]
            yield from reduce_text(me, dw, outs[b], cut, sems)
        else:
            yield from reduce_image(me, dw, outs[b], t, sems)
        if b == 1:
            for device in neighbours:
                pl.semaphore_signal(credit, inc=1, device_id=device, device_id_type=MESH)
    plan.post("summed", kind, i)


def gathers(plan, me, b, kind, i, v, g, after):
    if after is not None:
        yield need(*after)
    sems = getattr(g, f"gather_sems_{kind}{b}{i}")
    started, ready = ("started", b, kind, i), ("w" + kind, b, i)
    w = getattr(v, "w" + kind)
    if i == 0:
        yield from gather_text(me, getattr(g, f"pieces_{kind}{b}"), w, sems, started, ready)
    else:
        yield from gather_image(me, w, sems, started, ready)


def whole_kernel(g):
    plan = Plan()
    me = Place(plan)
    wires = [Wire(me, getattr(g, f"part{i}"), getattr(g, f"from_sib{i}"), getattr(g, f"from_mate{i}"),
                  getattr(g, f"wire_sems{i}")) for i in range(2)]
    views = []
    lane = 0
    for b in range(2):
        pair = []
        for i in range(2):
            sh = SHAPES[b][i]
            v = Bag()
            v.wire = wires[i]
            for name in ("head_bias", "up_bias", "bias", "gain", "offset", "xf", "qkv", "mixed", "nf", "slope",
                         "active", "first", "second"):
                setattr(v, name, getattr(g, f"{name}{b}{i}"))
            for name in ("ids_col", "ids_row", "normed", "gs", "gb", "gu"):
                setattr(v, name, getattr(g, f"{name}{i}"))
            v.gm, v.gp = (getattr(g, f"gm0{b}"), getattr(g, f"gp0{b}")) if i == 0 else (g.gm1, g.gp1)
            for kind, wide in (("p", sh.proj_columns), ("r", sh.rest_columns)):
                w, dw = getattr(g, f"w{kind}{b}{i}"), getattr(g, f"w{kind}1{i}" if b == 0 else f"dw{kind}{i}")
                setattr(v, "w" + kind, w.at[:, :wide] if i == 0 else w)
                setattr(v, "dw" + kind, dw.at[:, :wide] if i == 0 else dw)
            if i == 1:
                v.mixed_rows, v.gp_rows, v.to_rows, v.to_parts = g.mixed_rows, g.gp_rows, g.to_rows, g.to_parts
            v.vec = g.vecs.at[:, lane:lane + sh.width]
            lane += sh.width
            k = 2 * (2 * b + i)
            v.col_proj = g.cols.at[k:k + 1]
            v.col_up = g.cols.at[k + 1:k + 2]
            pair.append(v)
        views.append(pair)
    for b in range(2):
        for i in range(2):
            sh, v = SHAPES[b][i], views[b][i]
            a, f = sh.inner, sh.hidden
            proj, out, up, down = [getattr(g, f"{p}{b}{i}") for p in ("proj", "out", "up", "down")]
            if i == 0:
                to_p, to_r = getattr(g, f"pieces_p{b}").at[me.y], getattr(g, f"pieces_r{b}").at[me.y]
                if sh.proj_columns > 3 * a:
                    to_p[:, 512:] = jnp.zeros((24, sh.proj_columns - 512), BF16)
                    to_r[:, 1664:] = jnp.zeros((24, sh.rest_columns - 1664), BF16)
            else:
                to_p, to_r = v.wp.at[me.x, me.z, me.y], v.wr.at[me.x, me.z, me.y]
            for c in range(3):
                to_p[:, c * a:(c + 1) * a] = proj[c]
            to_r[:, :f] = up[...]
            to_r[:, f:2 * f] = down[...]
            to_r[:, 2 * f:2 * f + a] = out[...]
    near = [me.along("z", 1), me.along("x", 1), me.along("x", 3), me.along("y", 1), me.along("y", 3)]
    greet(near + [me.along("x", 2), me.along("y", 2), me.sib, me.mate, me.far])
    entry = Trade(me, [(g.x0, g.x_got0), (g.x1, g.x_got1), (g.lengths0, g.lengths_got0), (g.lengths1, g.lengths_got1),
                       (g.cot0, g.cot_got0), (g.cot1, g.cot_got1)], g.entry_sems)
    out_trade = Trade(me, [(g.out0, g.out0_done), (g.out1, g.out1_done)], g.out_sems)
    grad_trade = Trade(me, [(g.grad0, g.grad0_done), (g.grad1, g.grad1_done)], g.grad_sems)
    base = (g.base0, g.base1)

    def opening():
        entry.start()
        for b in range(2):
            for i in range(2):
                v, a = views[b][i], SHAPES[b][i].inner
                v.offset[:, :a] = v.head_bias[0:1].astype(F32)
                v.offset[:, a:2 * a] = jnp.zeros((1, a), F32)
                v.offset[:, 2 * a:] = v.head_bias[1:2].astype(F32)
        g.vecs[...] = jnp.zeros_like(g.vecs)
        g.cols[...] = jnp.zeros_like(g.cols)
        place = lax.broadcasted_iota(jnp.int32, (432, 448), 0)
        token = row_of_part(lax.broadcasted_iota(jnp.int32, (1, 448), 1))
        g.to_rows[...] = (place == token).astype(F32).astype(BF16)
        place = lax.broadcasted_iota(jnp.int32, (448, 432), 1)
        token = row_of_part(lax.broadcasted_iota(jnp.int32, (448, 1), 0))
        g.to_parts[...] = (place == token).astype(F32).astype(BF16)
        for kind, start in (("p", 512), ("r", 1664)):
            dw = getattr(g, f"dw{kind}0")
            stop = SHAPES[1][0].proj_columns if kind == "p" else SHAPES[1][0].rest_columns
            dw[:, start:stop] = jnp.zeros((768, stop - start), BF16)
        yield spent(2.0)
        entry.finish()
        for i in range(2):
            set_ids(getattr(g, f"ids_col{i}"), getattr(g, f"lengths_got{i}"), 0)
            set_ids(getattr(g, f"ids_row{i}"), getattr(g, f"lengths_got{i}"), 1)
        for i, got in enumerate((g.x_got0, g.x_got1)):
            views[0][i].xf[me.own] = got[...]
            base[i][...] = got[...].astype(F32)
        yield spent(1.0)
        for i in range(2):
            plan.post("x", i)

    def begun(i):
        yield need("x", i)
        yield from stream(plan, i, views, base[i], (g.cot_got0, g.cot_got1)[i], (g.out0, g.out1)[i],
                          (g.grad0, g.grad1)[i])

    def closing():
        yield need("out", 0)
        yield need("out", 1)
        out_trade.start()
        yield need("grad", 0)
        yield need("grad", 1)
        grad_trade.start()

    def vectors():
        for b in range(2):
            for i in range(2):
                yield need("dwp", b, i)
        yield from total_steps(me, g.vecs, g.cols, g.vec_got, g.slots, g.small, g.vec_sum, g.cols_out, g.total_sems)

    tasks = []
    before = None
    for b in range(2):
        for kind in ("p", "r"):
            for i in (1, 0):
                after = None if before is None else ("started", before[0], before[1], i)
                tasks.append((0, gathers(plan, me, b, kind, i, views[b][i], g, after)))
            before = (b, kind)
    tasks.append((0, opening()))
    for i in (1, 0):
        tasks.append((1, begun(i)))
    tasks.append((1, closing()))
    tasks.append((2, vectors()))
    for i in range(2):
        for kind in ("r", "p"):
            t = Bag()
            for name in ("halves", "chunks", "across", "small_halves", "small_chunks") + (("pieces",) if i == 0 else ()):
                setattr(t, name, getattr(g, f"{name}_{kind}{i}"))
            outs = [getattr(g, f"sum_{kind}{b}{i}") for b in range(2)]
            tasks.append((2, sums_of(plan, me, kind, i, views, outs, t, getattr(g, f"reduce_sems_{kind}{i}"),
                                     getattr(g, f"credit_{kind}{i}"))))
    for b in (1, 0):
        for i in (1, 0):
            tasks.append((3, matrix_grads(plan, b, i, views[b][i])))
    plan.run(tasks)
    out_trade.finish()
    grad_trade.finish()
    g.vecs_out[...] = g.vec_sum[...]
    for name in ("out0", "out1", "grad0", "grad1"):
        getattr(g, name + "_end")[...] = getattr(g, name + "_done")[...]


def call(kernel, inputs, outs, scratch, collective_id=None):
    names = list(inputs) + list(outs) + list(scratch)

    def body(*refs):
        bag = Bag()
        for name, ref in zip(names, refs):
            setattr(bag, name, ref)
        kernel(bag)
    vm = pl.BlockSpec(memory_space=pltpu.VMEM)
    results = pl.pallas_call(
        body, out_shape=list(outs.values()), in_specs=[vm] * len(inputs), out_specs=[vm] * len(outs),
        scratch_shapes=list(scratch.values()),
        compiler_params=pltpu.CompilerParams(collective_id=collective_id, has_side_effects=collective_id is not None,
                                             vmem_limit_bytes=LIMIT),
    )(*inputs.values())
    return dict(zip(outs, results))


def whole(inputs):
    outs, scratch = {}, {}
    for i in range(2):
        sh = SHAPES[0][i]
        slab = (sh.part, sh.width)
        for name in ("x_got", "cot_got"):
            scratch[f"{name}{i}"] = VMEM(slab, BF16)
        scratch[f"lengths_got{i}"] = VMEM((3, 4), jnp.int32)
        for name in ("out", "grad"):
            scratch[f"{name}{i}"] = VMEM(slab, BF16)
            scratch[f"{name}{i}_done"] = VMEM(slab, BF16)
            outs[f"{name}{i}_end"] = jax.ShapeDtypeStruct(slab, BF16)
        scratch[f"base{i}"] = VMEM(slab, F32)
        scratch[f"normed{i}"] = VMEM(slab, F32)
        for name in ("gs", "gb", "part"):
            scratch[f"{name}{i}"] = VMEM((4,) + slab, BF16)
        scratch[f"gu{i}"] = VMEM((sh.tokens, sh.hidden), BF16)
        scratch[f"from_sib{i}"] = VMEM((2,) + slab, BF16)
        scratch[f"from_mate{i}"] = VMEM(slab, BF16)
        scratch[f"wire_sems{i}"] = DMA((2, 6))
        scratch[f"ids_col{i}"] = VMEM((3, sh.length, 1), F32)
        scratch[f"ids_row{i}"] = VMEM((3, 1, sh.length), F32)
        for kind, wide in zip("pr", WIDEST[i]):
            matrix = (768, wide) if i == 0 else (4, 2, 4, 32, wide)
            scratch[f"dw{kind}{i}"] = VMEM(matrix, BF16)
            for b in range(2):
                scratch[f"w{kind}{b}{i}"] = VMEM(matrix, BF16)
                scratch[f"gather_sems_{kind}{b}{i}"] = DMA((2, 9))
                cols = SHAPES[b][i].proj_columns if kind == "p" else SHAPES[b][i].rest_columns
                if i == 0:
                    scratch[f"pieces_{kind}{b}"] = VMEM((4, 24, cols), BF16)
                outs[f"sum_{kind}{b}{i}"] = jax.ShapeDtypeStruct((24 if i == 0 else 32, cols), F32)
            scratch[f"reduce_sems_{kind}{i}"] = DMA((2, 9))
            scratch[f"credit_{kind}{i}"] = pltpu.SemaphoreType.REGULAR
            if i == 0:
                sizes = {"halves": (2, 96, wide), "chunks": (2, 192, wide), "across": (96, wide),
                         "pieces": (4, 24, wide), "small_halves": (2, 24, wide), "small_chunks": (2, 24, wide)}
            else:
                sizes = {"halves": (2, 2, 2, 32, wide), "chunks": (2, 4, 2, 32, wide), "across": (32, wide),
                         "small_halves": (2, 32, wide), "small_chunks": (2, 2, 32, wide)}
            for name, size in sizes.items():
                scratch[f"{name}_{kind}{i}"] = VMEM(size, BF16)
    scratch["mixed_rows"] = VMEM((432, 256), BF16)
    scratch["gp_rows"] = VMEM((432, 768), BF16)
    scratch["gm1"] = VMEM((432, 256), BF16)
    scratch["gp1"] = VMEM((448, 768), BF16)
    for b in range(2):
        scratch[f"gm0{b}"] = VMEM((384, SHAPES[b][0].inner), BF16)
        scratch[f"gp0{b}"] = VMEM((384, 3 * SHAPES[b][0].inner), BF16)
    scratch["to_rows"] = VMEM((432, 448), BF16)
    scratch["to_parts"] = VMEM((448, 432), BF16)
    scratch["entry_sems"] = DMA((2, 6))
    scratch["out_sems"] = DMA((2, 2))
    scratch["grad_sems"] = DMA((2, 2))
    lanes_all, cols_wide = 2 * (768 + 1024), 768
    scratch["vecs"] = VMEM((8, lanes_all), F32)
    scratch["cols"] = VMEM((8, cols_wide), F32)
    scratch["vec_got"] = VMEM((3, 8, lanes_all // 4), F32)
    scratch["small"] = VMEM((8, lanes_all // 4 + cols_wide), F32)
    scratch["slots"] = VMEM((3, 4, 8, lanes_all // 4 + cols_wide), F32)
    scratch["vec_sum"] = VMEM((8, lanes_all), F32)
    scratch["total_sems"] = DMA((2, 13))
    outs["vecs_out"] = jax.ShapeDtypeStruct((8, lanes_all), F32)
    outs["cols_out"] = jax.ShapeDtypeStruct((8, cols_wide), F32)
    for b in range(2):
        for i in range(2):
            sh = SHAPES[b][i]
            slab = (sh.part, sh.width)
            for name, shape, kind in (
                    ("offset", (1, 3 * sh.inner), F32), ("xf", (4,) + slab, BF16), ("nf", (4,) + slab, BF16),
                    ("qkv", (3 * sh.length, 3 * sh.inner), BF16), ("mixed", (sh.tokens, sh.inner), BF16),
                    ("slope", (sh.tokens, sh.hidden), BF16), ("active", (sh.tokens, sh.hidden), BF16),
                    ("first", slab, F32), ("second", slab, F32)):
                scratch[f"{name}{b}{i}"] = VMEM(shape, kind)
    return call(whole_kernel, inputs, outs, scratch, 0)


def finish_kernel(g):
    for i, count in enumerate((32, 36)):
        for name in ("out", "grad"):
            src, dst = getattr(g, f"{name}{i}"), getattr(g, f"{name}{i}_end")
            if i == 0:
                dst[...] = src[...].reshape(dst.shape)
            else:
                value = src[...].astype(F32)
                for b in range(3):
                    dst[b] = value[b * count:(b + 1) * count].astype(dst.dtype)
    lane = 0
    for k, n in enumerate(f"{b}{i}" for b in range(2) for i in range(2)):
        sum_p, sum_r = getattr(g, "sum_p" + n), getattr(g, "sum_r" + n)
        proj, out, up, down = [getattr(g, p + n) for p in ("proj", "out", "up", "down")]
        a, f = proj.shape[2], up.shape[1]
        for c in range(3):
            proj[c] = sum_p[:, c * a:(c + 1) * a]
        up[...] = sum_r[:, :f]
        down[...] = sum_r[:, f:2 * f]
        out[...] = sum_r[:, 2 * f:2 * f + a]
        head_bias, up_bias, bias, gain = [getattr(g, p + n) for p in ("head_bias", "up_bias", "bias", "gain")]
        head_bias[0:1] = g.cols[2 * k:2 * k + 1, :a]
        head_bias[1:2] = g.cols[2 * k:2 * k + 1, 2 * a:3 * a]
        up_bias[...] = g.cols[2 * k + 1:2 * k + 2, :f]
        width = bias.shape[1]
        bias[...] = g.vecs[0:4, lane:lane + width]
        gain[...] = g.vecs[4:6, lane:lane + width]
        lane += width


def on_device(*args):
    text_in, image_in, text_lengths, image_lengths, text_cot, image_cot = args[:6]
    matrix_names = ("proj", "out", "up", "down")
    small_names = ("head_bias", "up_bias", "bias", "gain")

    def tokens_of(value):
        value = value.reshape(-1, value.shape[-1])
        return jnp.pad(value, ((0, -value.shape[0] % 16), (0, 0)))
    inputs = {"x0": tokens_of(text_in), "x1": tokens_of(image_in), "cot0": tokens_of(text_cot),
              "cot1": tokens_of(image_cot), "lengths0": text_lengths, "lengths1": image_lengths}
    shapes = {}
    names = [f"{b}{i}" for b in range(2) for i in range(2)]
    for k, n in enumerate(names):
        for name, value in zip(matrix_names + small_names, args[6 + 8 * k:14 + 8 * k]):
            inputs[name + n] = value.transpose(1, 0, 2) if name == "proj" else value
            shapes[name + n] = jax.ShapeDtypeStruct(inputs[name + n].shape, F32)
    done = whole(inputs)
    ends, outs = {"vecs": done["vecs_out"], "cols": done["cols_out"]}, {}
    for name, like in (("out0", text_in), ("out1", image_in), ("grad0", text_in), ("grad1", image_in)):
        ends[name] = done[name + "_end"]
        outs[name + "_end"] = jax.ShapeDtypeStruct(like.shape, like.dtype)
    for n in names:
        ends["sum_p" + n] = done["sum_p" + n]
        ends["sum_r" + n] = done["sum_r" + n]
        for p in matrix_names + small_names:
            outs[p + n] = shapes[p + n]
    return tuple(value.transpose(1, 0, 2) if name.startswith("proj") else value
                 for name, value in call(finish_kernel, ends, outs, {}).items())


def solution(mesh):
    kinds = [P("rows", None, "seq"), P("rows", "seq"), P("rows", "seq"), P("rows", "seq"), P(None, "seq"),
             P(None, "seq"), P(), P()] * 4
    position = P("rows", "seq", None)
    return jax.shard_map(
        on_device, mesh=mesh,
        in_specs=tuple([position, position, P("rows", None), P("rows", None), position, position] + kinds),
        out_specs=tuple([position] * 4 + kinds), check_vma=False)
```

```python
import jax
import jax.numpy as jnp
from jax import lax
from jax.experimental import pallas as pl
from jax.experimental.pallas import tpu as pltpu
from jax.sharding import PartitionSpec as P

MESH = pl.DeviceIdType.MESH
VMEM = pltpu.VMEM
DMA = pltpu.SemaphoreType.DMA
F32, BF16 = jnp.float32, jnp.bfloat16
NN, NT, TN = ((1,), (0,)), ((1,), (1,)), ((0,), (0,))
EPS = 1e-05
MASKED = -1000000000.0
LIMIT = 63 * 1024 * 1024


class Bag:
    pass


RATE = {"x+": 48e3, "x-": 48e3, "y+": 48e3, "y-": 48e3, "z": 48e3, "over": 48e3, "beside": 600e3}
DELAY = {"beside": 1.1}


class Plan:
    def __init__(self):
        self.now = 0.0
        self.free = {}
        self.done = set()

    def post(self, *event):
        self.done.add(event)

    def arrival(self, link, size):
        self.now += 0.06
        begin = max(self.now, self.free.get(link, 0.0))
        self.free[link] = begin + size / RATE[link]
        return self.free[link] + DELAY.get(link, 3.6)

    def run(self, tasks):
        waiting = [[rank, n, task, ("at", 0.0)] for n, (rank, task) in enumerate(tasks)]
        while waiting:
            best = None
            for entry in waiting:
                kind, what = entry[3]
                if kind == "event":
                    if what not in self.done:
                        continue
                    due = self.now
                else:
                    due = max(what, self.now)
                key = (due, entry[0], entry[1])
                if best is None or key < best[0]:
                    best = (key, entry)
            assert best is not None, "stuck"
            entry = best[1]
            self.now = best[0][0]
            try:
                need = next(entry[2])
            except StopIteration:
                waiting.remove(entry)
                continue
            if need[0] == "for":
                self.now += need[1]
                need = ("at", self.now)
            entry[3] = need


class Place:
    def __init__(self, plan):
        r = lax.axis_index("rows")
        s = lax.axis_index("seq")
        self.plan = plan
        self.r, self.s = r, s
        self.x, self.z, self.y = r // 8, (r // 4) % 2, r % 4
        self.zh, self.c = s // 2, s % 2
        self.own = s
        self.sib_slab = self.zh * 2 + 1 - self.c
        self.mate_slab = (1 - self.zh) * 2 + self.c
        self.far_slab = (1 - self.zh) * 2 + 1 - self.c
        self.sib = (r, self.sib_slab)
        across = (self.x * 2 + 1 - self.z) * 4 + self.y
        self.mate = (across, self.mate_slab)
        self.far = (across, self.far_slab)

    def along(self, axis, step):
        x, z, y = self.x, self.z, self.y
        if axis == "x":
            x = (x + step) % 4
        elif axis == "y":
            y = (y + step) % 4
        else:
            z = 1 - z
        return ((x * 2 + z) * 4 + y, self.s)

    def push(self, src, dst, sems, k, device, link):
        copy = pltpu.make_async_remote_copy(
            src_ref=src, dst_ref=dst, send_sem=sems.at[0, k], recv_sem=sems.at[1, k],
            device_id=device, device_id_type=MESH)
        copy.start()
        size = src.dtype.itemsize
        for n in src.shape:
            size *= n
        copy.due = self.plan.arrival(link, size)
        return copy


def greet(devices):
    barrier = pltpu.get_barrier_semaphore()
    for device in devices:
        pl.semaphore_signal(barrier, inc=1, device_id=device, device_id_type=MESH)
    pl.semaphore_wait(barrier, len(devices))


def at(copy, *more):
    return ("at", max(c.due for c in (copy,) + more))


def need(*event):
    return ("event", event)


def spent(cost):
    return ("for", 0.72 * cost)


class Trade:
    def __init__(self, me, pairs, sems):
        self.me, self.pairs, self.sems = me, pairs, sems

    def copies(self):
        return [pltpu.make_async_remote_copy(
            src_ref=src, dst_ref=dst, send_sem=self.sems.at[0, k], recv_sem=self.sems.at[1, k],
            device_id=self.me.along("z", 1), device_id_type=MESH) for k, (src, dst) in enumerate(self.pairs)]

    def start(self):
        @pl.when(self.me.zh == 1)
        def _():
            for copy in self.copies():
                copy.start()

        @pl.when(self.me.zh == 0)
        def _():
            for src, dst in self.pairs:
                dst[...] = src[...]

    def finish(self):
        @pl.when(self.me.zh == 1)
        def _():
            for copy in self.copies():
                copy.wait()


def dot(a, b, dims):
    return lax.dot_general(a, b, (dims, ((), ())), preferred_element_type=F32)


def loop(count, body):
    for i in range(count):
        body(i)


def lanes(i, size=256, base=0):
    return slice(base + i * size, base + (i + 1) * size)


def span(start, size):
    return pl.ds(pl.multiple_of(start, 16), size)


def add_rows(dst, start, src, first, count):
    def one(i):
        to, come = span(start + 16 * i, 16), span(first + 16 * i, 16)
        total = dst[to].astype(F32)
        for ref in src:
            total = total + ref[come].astype(F32)
        dst[to] = total.astype(dst.dtype)
    loop(count // 16, one)


def add_slabs(dst, src, count):
    def one(i):
        to = dst(i)
        total = to[...].astype(F32)
        for ref in src(i):
            total = total + ref[...].astype(F32)
        to[...] = total.astype(to.dtype)
    loop(count, one)


def middle_of(columns):
    return columns // 256 * 128


def gather_text(me, pieces, w, sems, started, ready, z_first):
    columns = w.shape[1]
    cut = middle_of(columns)
    x, z, y = me.x, me.z, me.y
    copies = [me.push(pieces.at[y], pieces.at[y], sems, n, me.along("y", n + 1), link)
              for n, link in enumerate(("y+", "y+", "y-"))]
    yield at(*copies)
    for copy in copies:
        copy.wait_recv()
    base = (x * 2 + z) * 96
    w[span(base, 96)] = pieces[...].astype(F32).reshape(96, columns).astype(BF16)
    yield spent(0.2)
    right, left = me.along("x", 1), me.along("x", 3)
    block = w.at[span(base, 96)]
    if z_first:
        e = me.push(block, block, sems, 4, me.along("z", 1), "z")
        yield at(e)
        e.wait_recv()
        block = w.at[span(192 * x, 192)]
    f = me.push(block, block, sems, 5, right, "x+")
    g = me.push(block, block, sems, 6, left, "x-")
    if z_first:
        me.plan.post(*started)
    yield at(f)
    f.wait_recv()
    place = 192 * ((x + 3) % 4)
    block = w.at[span(place, 96)] if z_first else w.at[span(place + 96 * z, 96), :cut]
    h = me.push(block, block, sems, 7, right, "x+")
    yield at(g)
    g.wait_recv()
    place = 192 * ((x + 1) % 4)
    block = w.at[span(place + 96, 96)] if z_first else w.at[span(place + 96 * z, 96), cut:]
    i = me.push(block, block, sems, 8, left, "x-")
    copies += [f, g, h, i]
    if z_first:
        copies.append(e)
    else:
        me.plan.post(*started)
        over = []
        for n, step in enumerate((0, 3, 1)):
            block = w.at[span(192 * ((x + step) % 4) + 96 * z, 96)]
            over.append(me.push(block, block, sems, 9 + n, me.along("z", 1), "z"))
        yield at(h, i)
    if z_first:
        yield at(h, i)
    h.wait_recv()
    i.wait_recv()
    if not z_first:
        block = w.at[span(192 * ((x + 2) % 4) + 96 * z, 96)]
        over.append(me.push(block, block, sems, 12, me.along("z", 1), "z"))
        yield at(*over)
        for copy in over:
            copy.wait_recv()
        copies += over
    me.plan.post(*ready)
    for copy in copies:
        copy.wait_send()


def image_views(me, w, light):
    x, z, y = me.x, me.z, me.y
    if light == "x":
        return (lambda n: w.at[(x + n) % 4, :, y], lambda n, h: w.at[(x + n) % 4, h, y],
                lambda n: w.at[:, :, (y + n) % 4], lambda n, h: w.at[2 * h:2 * h + 2, :, (y + n) % 4])
    return (lambda n: w.at[x, :, (y + n) % 4], lambda n, h: w.at[x, h, (y + n) % 4],
            lambda n: w.at[(x + n) % 4], lambda n, h: w.at[(x + n) % 4, :, 2 * h:2 * h + 2])


def gather_image(me, w, sems, started, ready, light):
    x, z, y = me.x, me.z, me.y
    heavy = "y" if light == "x" else "x"
    few, few_half, many, many_half = image_views(me, w, light)
    copies = [me.push(w.at[x, z, y], w.at[x, z, y], sems, 0, me.along("z", 1), "z")]
    yield at(copies[0])
    copies[0].wait_recv()
    for k, axis, whole, part in ((1, light, few, few_half), (5, heavy, many, many_half)):
        right, left = me.along(axis, 1), me.along(axis, 3)
        a = me.push(whole(0), whole(0), sems, k, right, axis + "+")
        b = me.push(whole(0), whole(0), sems, k + 1, left, axis + "-")
        if axis == heavy:
            me.plan.post(*started)
        yield at(a)
        a.wait_recv()
        c = me.push(part(3, 0), part(3, 0), sems, k + 2, right, axis + "+")
        yield at(b)
        b.wait_recv()
        d = me.push(part(1, 1), part(1, 1), sems, k + 3, left, axis + "-")
        yield at(c, d)
        c.wait_recv()
        d.wait_recv()
        copies += [a, b, c, d]
    me.plan.post(*ready)
    for copy in copies:
        copy.wait_send()


def reduce_text(me, dw, out, t, sems, z_first):
    columns = dw.shape[1]
    cut = middle_of(columns)
    cost = columns / 2000.0
    x, z, y = me.x, me.z, me.y
    right, left = me.along("x", 1), me.along("x", 3)
    copies = []
    if z_first:
        def mine(step):
            return 192 * ((x + step) % 4) + 96 * z
        over = []
        for n, step in enumerate((2, 1, 3, 0)):
            place = (x + step) % 4
            over.append(me.push(dw.at[span(192 * place + 96 * (1 - z), 96)], t.across.at[place], sems, 9 + n,
                                me.along("z", 1), "z"))
        yield at(over[0])
        over[0].wait_recv()
        add_rows(dw, mine(2), [t.across.at[(x + 2) % 4]], 0, 96)
        a = me.push(dw.at[span(mine(2), 96), :cut], t.halves.at[0, :, :cut], sems, 0, right, "x+")
        b = me.push(dw.at[span(mine(2), 96), cut:], t.halves.at[1, :, cut:], sems, 1, left, "x-")
        yield spent(0.4 * cost)
        yield at(a, over[1])
        over[1].wait_recv()
        add_rows(dw, mine(1), [t.across.at[(x + 1) % 4]], 0, 96)
        a.wait_recv()
        add_rows(dw.at[:, :cut], mine(1), [t.halves.at[0, :, :cut]], 0, 96)
        c = me.push(dw.at[span(mine(1), 96)], t.chunks.at[0], sems, 2, right, "x+")
        yield spent(0.6 * cost)
        yield at(b, over[2])
        over[2].wait_recv()
        add_rows(dw, mine(3), [t.across.at[(x + 3) % 4]], 0, 96)
        b.wait_recv()
        add_rows(dw.at[:, cut:], mine(3), [t.halves.at[1, :, cut:]], 0, 96)
        d = me.push(dw.at[span(mine(3), 96)], t.chunks.at[1], sems, 3, left, "x-")
        yield spent(0.6 * cost)
        yield at(c, d, over[3])
        over[3].wait_recv()
        c.wait_recv()
        d.wait_recv()
        total = (dw[span(mine(0), 96)].astype(F32) + t.across[x].astype(F32) + t.chunks[0].astype(F32)
                 + t.chunks[1].astype(F32))
        copies += over
    else:
        far = 192 * ((x + 2) % 4)
        a = me.push(dw.at[span(far, 96)], t.halves.at[0], sems, 0, right, "x+")
        b = me.push(dw.at[span(far + 96, 96)], t.halves.at[1], sems, 1, left, "x-")
        yield at(a)
        a.wait_recv()
        first = 192 * ((x + 1) % 4)
        add_rows(dw, first, [t.halves.at[0]], 0, 96)
        c = me.push(dw.at[span(first, 192)], t.chunks.at[0], sems, 2, right, "x+")
        yield spent(0.4 * cost)
        yield at(b)
        b.wait_recv()
        first = 192 * ((x + 3) % 4)
        add_rows(dw, first + 96, [t.halves.at[1]], 0, 96)
        d = me.push(dw.at[span(first, 192)], t.chunks.at[1], sems, 3, left, "x-")
        yield spent(0.4 * cost)
        yield at(c, d)
        c.wait_recv()
        d.wait_recv()
        add_rows(dw, 192 * x + 96 * (1 - z), [t.chunks.at[0], t.chunks.at[1]], 96 * (1 - z), 96)
        e = me.push(dw.at[span(192 * x + 96 * (1 - z), 96)], t.across, sems, 4, me.along("z", 1), "z")
        add_rows(dw, 192 * x + 96 * z, [t.chunks.at[0], t.chunks.at[1]], 96 * z, 96)
        yield spent(1.0 * cost)
        yield at(e)
        e.wait_recv()
        total = dw[span(192 * x + 96 * z, 96)].astype(F32) + t.across[...].astype(F32)
        copies.append(e)
    t.pieces[...] = total.reshape(4, 24, columns).astype(BF16)
    yield spent(0.4 * cost)
    pieces = t.pieces
    last = [me.push(pieces.at[(y + n + 1) % 4], t.small_chunks.at[n], sems, 5 + n, me.along("y", n + 1), link)
            for n, link in enumerate(("y+", "y+", "y-"))]
    yield at(*last)
    for copy in last:
        copy.wait_recv()
    total = pieces[y].astype(F32) + t.small_chunks[0].astype(F32)
    out[...] = total + t.small_chunks[1].astype(F32) + t.small_chunks[2].astype(F32)
    copies += [a, b, c, d] + last
    for copy in copies:
        copy.wait_send()
    yield spent(0.2 * cost)


def add_block(dst, src):
    lead = [()]
    for n in dst.shape[:-2]:
        lead = [at_ + (k,) for at_ in lead for k in range(n)]
    for place in lead:
        total = dst[place].astype(F32)
        for ref in src:
            total = total + ref[place].astype(F32)
        dst[place] = total.astype(dst.dtype)


def reduce_image(me, dw, out, t, sems, light):
    cost = dw.shape[4] / 1500.0
    x, z, y = me.x, me.z, me.y
    heavy = "y" if light == "x" else "x"
    few, few_half, many, many_half = image_views(me, dw, light)
    copies = []
    for k, axis, whole, part, halves, chunks, scale in (
            (0, heavy, many, many_half, t.halves, t.chunks, 1.0), (4, light, few, few_half, t.small_halves, t.small_chunks, 0.3)):
        right, left = me.along(axis, 1), me.along(axis, 3)
        a = me.push(part(2, 0), halves.at[0], sems, k, right, axis + "+")
        b = me.push(part(2, 1), halves.at[1], sems, k + 1, left, axis + "-")
        yield at(a)
        a.wait_recv()
        add_block(part(1, 0), [halves.at[0]])
        c = me.push(whole(1), chunks.at[0], sems, k + 2, right, axis + "+")
        yield spent(0.4 * cost * scale)
        yield at(b)
        b.wait_recv()
        add_block(part(3, 1), [halves.at[1]])
        d = me.push(whole(3), chunks.at[1], sems, k + 3, left, axis + "-")
        yield spent(0.4 * cost * scale)
        yield at(c, d)
        c.wait_recv()
        d.wait_recv()
        add_block(whole(0), [chunks.at[0], chunks.at[1]])
        copies += [a, b, c, d]
        yield spent(1.2 * cost * scale)
    i = me.push(dw.at[x, 1 - z, y], t.across, sems, 8, me.along("z", 1), "z")
    yield at(i)
    i.wait_recv()
    out[...] = dw[x, z, y].astype(F32) + t.across[...].astype(F32)
    for copy in copies + [i]:
        copy.wait_send()
    yield spent(0.2 * cost)


def total_steps(me, vecs, cols, got, slots, small, vec_out, col_out, sems):
    wide = vecs.shape[1] // 4

    def quarter(k):
        return pl.ds(pl.multiple_of(k * wide, 128), wide)
    mates = ((me.sib, me.sib_slab, "beside"), (me.mate, me.mate_slab, "over"), (me.far, me.far_slab, "over"))
    sent = [me.push(vecs.at[:, quarter(slab)], got.at[k], sems, k, device, link)
            for k, (device, slab, link) in enumerate(mates)]
    yield at(*sent)
    for copy in sent:
        copy.wait_recv()
    small[:, :wide] = vecs[:, quarter(me.own)] + got[0] + got[1] + got[2]
    small[:, wide:] = cols[...]
    k = 3
    for stage, (axis, place, count) in enumerate((("x", me.x, 4), ("y", me.y, 4), ("z", me.z, 2))):
        slots[stage, place] = small[...]
        copies = [me.push(slots.at[stage, place], slots.at[stage, place], sems, k + n, me.along(axis, n + 1),
                          axis + "++-"[n] if count == 4 else "z") for n in range(count - 1)]
        k += count - 1
        yield at(*copies)
        for copy in copies:
            copy.wait_recv()
        total = slots[stage, 0] + slots[stage, 1]
        if count == 4:
            total = total + slots[stage, 2] + slots[stage, 3]
        small[...] = total
        sent += copies
    col_out[...] = small[:, wide:]
    vec_out[:, quarter(me.own)] = small[:, :wide]
    mine = vec_out.at[:, quarter(me.own)]
    last = [me.push(mine, mine, sems, k + n, device, link) for n, (device, slab, link) in enumerate(mates)]
    yield at(*last)
    for copy in last:
        copy.wait_recv()
    for copy in sent + last:
        copy.wait_send()


class Wire:
    def __init__(self, me, part, from_sib, from_mate, sems, start, size):
        self.me, self.part, self.from_sib, self.from_mate, self.sems = me, part, from_sib, from_mate, sems
        self.start, self.size = start, size
        self.rows = pl.ds(start, size)
        self.steps = [pl.ds(start + 16 * i, 16) for i in range(size // 16)]

    def gather(self, buf):
        me, rows = self.me, self.rows
        mine, theirs = buf.at[me.own, rows], buf.at[me.mate_slab, rows]
        over = me.push(mine, mine, self.sems, 0, me.mate, "over")
        beside = me.push(mine, mine, self.sems, 1, me.sib, "beside")
        yield at(over)
        over.wait_recv()
        on = me.push(theirs, theirs, self.sems, 2, me.sib, "beside")
        yield at(beside, on)
        beside.wait_recv()
        on.wait_recv()
        for copy in (over, beside, on):
            copy.wait_send()

    def reduce(self):
        me, part, from_sib, rows = self.me, self.part, self.from_sib, self.rows
        a = me.push(part.at[me.far_slab, rows], from_sib.at[0, rows], self.sems, 3, me.sib, "beside")
        b = me.push(part.at[me.sib_slab, rows], from_sib.at[1, rows], self.sems, 4, me.sib, "beside")
        yield at(a)
        a.wait_recv()
        for step in self.steps:
            part[me.mate_slab, step] = (
                part[me.mate_slab, step].astype(F32) + from_sib[0, step].astype(F32)).astype(BF16)
        d = me.push(part.at[me.mate_slab, rows], self.from_mate.at[rows], self.sems, 5, me.mate, "over")
        yield spent(0.2)
        yield at(b, d)
        b.wait_recv()
        d.wait_recv()
        for copy in (a, b, d):
            copy.wait_send()

    def total(self, rows):
        return (self.part[self.me.own, rows].astype(F32) + self.from_sib[1, rows].astype(F32)
                + self.from_mate[rows].astype(F32))


class Shape:
    def __init__(self, stream, part, length, width, inner, hidden, head):
        self.stream, self.part, self.length, self.width = stream, part, length, width
        self.inner, self.hidden, self.head = inner, hidden, head
        self.tokens = 4 * part
        self.out_at = 3 * inner
        self.columns = {"p": 4 * inner, "u": 2 * hidden}
        self.halves = ((0, 48), (48, 48)) if stream == 0 else ((0, 64), (64, 48))


SHAPES = ((Shape(0, 96, 128, 768, 256, 768, 128), Shape(1, 112, 144, 1024, 256, 256, 128)),
          (Shape(0, 96, 128, 768, 192, 768, 64), Shape(1, 112, 144, 1024, 256, 256, 128)))

GATHERS = {
        (0, 0): (("p", 0, 384, True, "q", 0), ("p", 384, 768, False, "q", 0), ("p", 768, 1024, False, "o", 5), ("u",
        0, 768, True, "u", 14), ("u", 768, 1536, False, "u", 14)),
        (0, 1): (("p", 0, 384, True, "q", 0), ("p", 384, 768, False, "q", 0), ("p", 768, 1024, True, "o", 8), ("u",
        0, 512, True, "u", 14)),
        (1, 0): (("p", 0, 384, True, "q", 20), ("p", 384, 768, False, "q", 32), ("u", 0, 768, False, "u", 34), ("u",
        768, 1536, True, "u", 37)),
        (1, 1): (("p", 0, 1024, True, "q", 20), ("u", 0, 512, True, "u", 28)),
}
SUMS = ({"ua": ("u", False, ((0, 768), (0, 768))),
         "ub": ("u", True, ((768, 1536), (768, 1536))),
         "pa": ("p", True, ((0, 384), (0, 384))),
         "pb": ("p", False, ((384, 768), (384, 768))),
         "o": ("p", False, ((768, 1024), None)),
         },
        {"u": ("u", True, ((0, 512), (0, 512))),
         "qa": ("p", True, ((0, 384), (0, 384))),
         "qb": ("p", False, ((384, 768), (384, 768))),
         "o": ("p", True, ((768, 1024), (768, 1024))),
         })
RANKS = {"gather": 0, "stream": 1, "attention": 2.5, "close": 0, "vectors": 0.5, "sums": 0.5,
         "feed1": 3, "feed0": 1.5, "head1": 2.5, "head0": 0.9, "cols": 0}


def columns_of(sh, w, cols):
    if sh.stream == 0:
        return w[:, cols]
    return w[:, :, :, :, cols].reshape(sh.width, -1)


def rows_of(sh, w, i, cols):
    if sh.stream == 0:
        return w[lanes(i), cols]
    value = w[i, :, :, :, cols]
    return value.reshape(256, value.shape[-1])


def set_rows(sh, w, i, cols, value):
    if sh.stream == 0:
        w[lanes(i), cols] = value
    else:
        w[i, :, :, :, cols] = value.reshape(2, 4, 32, value.shape[-1])


def normal(value):
    centre = jnp.mean(value, axis=-1, keepdims=True)
    moved = value - centre
    scale = lax.rsqrt(jnp.mean(moved * moved, axis=-1, keepdims=True) + EPS)
    return moved * scale, scale


def flat(ref):
    value = ref[...]
    return value.reshape(value.shape[0] * value.shape[1], value.shape[2])


def part_of(ref, rows):
    value = ref[:, rows]
    return value.reshape(value.shape[0] * value.shape[1], value.shape[2])


def put_by_row(ref, half, cols, value):
    runs = ((0, 0, 32, 0), (1, 0, 16, 32)) if half == 0 else ((1, 16, 16, 0), (2, 0, 32, 16))
    for p in range(4):
        for b, q, count, offset in runs:
            to = 128 * b + 32 * p + q
            ref[to:to + count, cols] = value[48 * p + offset:48 * p + offset + count]


def put_by_part(ref, b, cols, value):
    for p in range(4):
        ref[p, 32 * b:32 * b + 32, cols] = value[32 * p:32 * p + 32]


def project(sh, v, half):
    whole = part_of(v.xf, v.wires[half].rows)

    def put(cols, value):
        if sh.stream == 0:
            put_by_row(v.qkv, half, cols, value)
        else:
            v.gp[:, v.wires[half].rows, cols] = value.reshape(4, v.wires[half].size, -1)
    if sh.inner % 256:
        cols = slice(0, 3 * sh.inner)
        put(cols, (dot(whole, columns_of(sh, v.wp, cols), NN) + v.offset[...]).astype(BF16))
    else:
        def one(i):
            cols = lanes(i)
            put(cols, (dot(whole, columns_of(sh, v.wp, cols), NN) + v.offset[:, cols]).astype(BF16))
        loop(3 * sh.inner // 256, one)


def probabilities(query, key, col_ids, row_ids, scale):
    raw = dot(query, key, NT)
    scores = jnp.where(col_ids == row_ids, raw * scale, MASKED)
    grown = jnp.exp(scores - jnp.max(scores, axis=-1, keepdims=True))
    return grown * (1.0 / jnp.sum(grown, axis=-1, keepdims=True))


def attend(sh, v, kv, key_length):
    h, a = sh.head, sh.inner
    for b in range(3):
        mine = pl.ds(b * sh.length, sh.length)
        theirs = pl.ds(b * key_length, key_length)
        for n in range(a // h):
            q_at, k_at, v_at = [slice(c * a + n * h, c * a + (n + 1) * h) for c in range(3)]
            p = probabilities(v.qkv[mine, q_at], kv.qkv[theirs, k_at], v.ids_col[b], kv.ids_row[b], h ** -0.5)
            result = dot(p.astype(BF16), kv.qkv[theirs, v_at], NN).astype(BF16)
            if sh.stream == 0:
                put_by_part(v.mixed, b, q_at, result)
            else:
                v.mixed_rows[mine, q_at] = result
        yield spent(0.6)
    if sh.stream == 1:
        v.mixed[...] = dot(v.to_parts[...], v.mixed_rows[...], NN).astype(BF16).reshape(4, sh.part, a)
        yield spent(0.3)


def spread_out(sh, v, half, left, w, cols):
    wire = v.wires[half]
    value = part_of(left, wire.rows)

    def one(i):
        result = dot(value, rows_of(sh, w, i, cols), NT)
        wire.part[:, wire.rows, lanes(i)] = result.reshape(4, wire.size, 256).astype(BF16)
    loop(sh.width // 256, one)


def norm_forward(sh, v, half, base, sums, which, result, low):
    bias = v.bias[which:which + 1].astype(F32)
    shift = v.bias[2 + which:3 + which].astype(F32)
    gain = v.gain[which:which + 1].astype(F32)
    for rows in v.wires[half].steps:
        value = base[rows] + v.wires[half].total(rows) + bias
        sums[rows] = value
        value = normal(value)[0] * gain + shift
        result[rows] = value
        low[rows] = value.astype(BF16)


def feed(sh, v, half):
    wire = v.wires[half]
    whole = part_of(v.nf, wire.rows)
    k = (2.0 / jnp.pi) ** 0.5

    def one(i):
        cols = lanes(i)
        u = dot(whole, columns_of(sh, v.wu, cols), NN) + v.up_bias[:, cols].astype(F32)
        square = u * u
        t = jnp.tanh(k * u * (1.0 + 0.044715 * square))
        half_sum = 0.5 * (1.0 + t)
        slope = half_sum + 0.5 * u * (1.0 - t * t) * (k * (1.0 + 3 * 0.044715 * square))
        v.active[:, wire.rows, cols] = (u * half_sum).astype(BF16).reshape(4, wire.size, 256)
        v.slope[:, wire.rows, cols] = slope.astype(BF16).reshape(4, wire.size, 256)
    loop(sh.hidden // 256, one)


def norm_backward(sh, v, half, grad, sums, which, result, low, bias_row):
    gain = v.gain[which:which + 1].astype(F32)

    def fold(value):
        return value[:8] + value[8:]
    totals = None
    for rows in v.wires[half].steps:
        g = grad(rows)
        n, scale = normal(sums[rows])
        gn = g * gain
        out = scale * (gn - jnp.mean(gn, axis=-1, keepdims=True) - n * jnp.mean(gn * n, axis=-1, keepdims=True))
        rounded = out.astype(BF16)
        result[rows] = out
        low[rows] = rounded
        terms = (fold(rounded.astype(F32)), fold(g), fold(g * n))
        totals = terms if totals is None else tuple(x + y for x, y in zip(totals, terms))
    for at_row, total in zip((bias_row, 2 + which, 4 + which), totals):
        v.vec[at_row:at_row + 1] += jnp.sum(total, axis=0, keepdims=True)


def weight_grad(sh, left, right, dw, start):
    cols = slice(start, start + right.shape[2])

    def one(i):
        piece = left[:, :, lanes(i)].reshape(sh.tokens, 256)
        set_rows(sh, dw, i, cols, dot(piece, flat(right), TN).astype(BF16))
    loop(sh.width // 256, one)


def feed_back(sh, v, half):
    wire = v.wires[half]
    whole = part_of(v.gs, wire.rows)

    def one(i):
        cols = lanes(i)
        grad = dot(whole, columns_of(sh, v.wu, lanes(i, 256, sh.hidden)), NN)
        gu = (grad * v.slope[:, wire.rows, cols].reshape(4 * wire.size, 256).astype(F32)).astype(BF16)
        v.gu[:, wire.rows, cols] = gu.reshape(4, wire.size, 256)
        v.col_up[:, cols] += jnp.sum(gu.astype(F32), axis=0, keepdims=True)
    loop(sh.hidden // 256, one)


def mix_back(sh, v, half):
    wire = v.wires[half]
    cols = slice(sh.out_at, sh.out_at + sh.inner)
    value = dot(part_of(v.gb, wire.rows), columns_of(sh, v.wp, cols), NN).astype(BF16)
    if sh.stream == 0:
        put_by_row(v.gm, half, slice(0, sh.inner), value)
    else:
        v.gm_parts[:, wire.rows] = value.reshape(4, wire.size, sh.inner)


def attend_back(sh, v, key_sh, kv):
    h, a = sh.head, sh.inner
    scale = h ** -0.5

    def put(to_sh, to, b, cols, value):
        value = value.astype(BF16)
        if to_sh.stream == 0:
            put_by_part(to.gp, b, cols, value)
        else:
            to.gp_rows[pl.ds(b * to_sh.length, to_sh.length), cols] = value
    if sh.stream == 1:
        v.gm[...] = dot(v.to_rows[...], flat(v.gm_parts), NN).astype(BF16)
    for b in range(3):
        mine = pl.ds(b * sh.length, sh.length)
        theirs = pl.ds(b * key_sh.length, key_sh.length)
        for n in range(a // h):
            q_at, k_at, v_at = [slice(c * a + n * h, c * a + (n + 1) * h) for c in range(3)]
            query, key, value = v.qkv[mine, q_at], kv.qkv[theirs, k_at], kv.qkv[theirs, v_at]
            grad = v.gm[mine, q_at]
            p = probabilities(query, key, v.ids_col[b], kv.ids_row[b], scale)
            gp = dot(grad, value, NT)
            gs = (p * (gp - jnp.sum(gp * p, axis=-1, keepdims=True)) * scale).astype(BF16)
            put(sh, v, b, q_at, dot(gs, key, NN))
            put(key_sh, kv, b, k_at, dot(gs, query, TN))
            put(key_sh, kv, b, v_at, dot(p.astype(BF16), grad, TN))
        yield spent(1.3)


def set_ids(ref, lengths, axis):
    shape = ref.shape[1:]
    position = lax.broadcasted_iota(jnp.int32, shape, axis)
    for b in range(3):
        bound = jnp.zeros((1, 1), jnp.int32)
        seg = jnp.zeros(shape, jnp.int32)
        for j in range(4):
            bound = bound + lengths[b:b + 1, j:j + 1]
            seg = seg + (position >= bound).astype(jnp.int32)
        ref[b] = seg.astype(F32)


def row_of_part(token):
    def over(value, size, most):
        return sum((value >= k * size).astype(jnp.int32) for k in range(1, most))
    p = over(token, 112, 4)
    within = token - 112 * p
    row = over(within, 36, 4)
    return jnp.where(row < 3, 144 * row + 36 * p + within - 36 * row, -1)


def stream(plan, i, half, views, base, cot, outs, grads):
    big = i == 0
    for b in range(2):
        sh, v = SHAPES[b][i], views[b][i]
        wire = v.wires[half]
        own = wire.me.own
        yield from wire.gather(v.xf)
        yield need("wq", b, i)
        project(sh, v, half)
        yield spent(0.6)
        plan.post("qkv", b, i, half)
        yield need("mixed", b, i)
        yield need("wo", b, i)
        spread_out(sh, v, half, v.mixed, v.wp, slice(sh.out_at, sh.out_at + sh.inner))
        yield spent(0.4)
        yield from wire.reduce()
        norm_forward(sh, v, half, base, v.first, 0, v.normed, v.nf.at[own])
        yield spent(0.4)
        yield from wire.gather(v.nf)
        yield need("wu", b, i)
        feed(sh, v, half)
        yield spent(1.1 if big else 0.6)
        spread_out(sh, v, half, v.active, v.wu, slice(sh.hidden, 2 * sh.hidden))
        yield spent(0.7 if big else 0.4)
        yield from wire.reduce()
        norm_forward(sh, v, half, v.normed, v.second, 1, base, views[1][i].xf.at[own] if b == 0 else outs)
        yield spent(0.4)
    plan.post("out", i, half)
    for b in (1, 0):
        sh, v = SHAPES[b][i], views[b][i]
        wire = v.wires[half]
        own = wire.me.own
        norm_backward(sh, v, half, (lambda rows: cot[rows].astype(F32)) if b == 1 else (lambda rows: base[rows]),
                      v.second, 1, v.normed, v.gs.at[own], 1)
        yield spent(0.6)
        yield from wire.gather(v.gs)
        plan.post("gs", b, i, half)
        if b == 0:
            yield need("dwu", 1, i)
        feed_back(sh, v, half)
        yield spent(0.9 if big else 0.5)
        plan.post("gu", b, i, half)
        if b == 0:
            yield need("dwo", 1, i)
        spread_out(sh, v, half, v.gu, v.wu, slice(0, sh.hidden))
        yield spent(0.7 if big else 0.4)
        yield from wire.reduce()
        norm_backward(sh, v, half, lambda rows, v=v: v.normed[rows] + v.wires[half].total(rows), v.first, 0, v.normed,
                      v.gb.at[own], 0)
        yield spent(0.6)
        yield from wire.gather(v.gb)
        plan.post("gb", b, i, half)
        mix_back(sh, v, half)
        yield spent(0.4)
        plan.post("gm", b, i, half)
        yield need("gp", b, i)
        if b == 1:
            yield need("dwd", 1, i)
        spread_out(sh, v, half, v.gp, v.wp, slice(0, 3 * sh.inner))
        yield spent(0.7)
        yield from wire.reduce()
        for rows in wire.steps:
            value = v.normed[rows] + wire.total(rows)
            if b == 1:
                base[rows] = value
            else:
                grads[rows] = value.astype(BF16)
        yield spent(0.2)
    plan.post("grad", i, half)


def attention(plan, b, i, views):
    key_stream = 1 - i if b == 0 else i
    sh, v = SHAPES[b][i], views[b][i]
    kv = views[b][key_stream]
    for half in range(2):
        yield need("qkv", b, i, half)
    if i == 1:
        v.qkv[...] = dot(v.to_rows[...], flat(v.gp), NN).astype(BF16)
        yield spent(0.6)
    plan.post("rows", b, i)
    yield need("rows", b, key_stream)
    for half in range(2):
        yield need("qkv", b, key_stream, half)
    yield from attend(sh, v, kv, SHAPES[b][key_stream].length)
    plan.post("mixed", b, i)


def attention_back(plan, b, i, views):
    key_stream = 1 - i if b == 0 else i
    sh, v = SHAPES[b][i], views[b][i]
    for half in range(2):
        yield need("gm", b, i, half)
    if b == 0:
        yield need("gp", 1, 0)
        yield need("gp", 1, 1)
        yield need("dwp", 1, 1)
    yield from attend_back(sh, v, SHAPES[b][key_stream], views[b][key_stream])
    plan.post("attended", b, i)
    yield need("attended", b, key_stream)
    if i == 1:
        v.gp[...] = dot(v.to_parts[...], v.gp_rows[...], NN).astype(BF16).reshape(4, sh.part, 3 * sh.inner)
        yield spent(0.6)
    plan.post("gp", b, i)


def feed_grads(plan, b, i, v):
    sh = SHAPES[b][i]
    for half in range(2):
        yield need("gs", b, i, half)
    weight_grad(sh, v.gs, v.active, v.dwu, sh.hidden)
    yield spent(1.6 if i == 0 else 0.9)
    plan.post("dwd", b, i)
    for half in range(2):
        yield need("gu", b, i, half)
    weight_grad(sh, v.nf, v.gu, v.dwu, 0)
    yield spent(1.6 if i == 0 else 0.9)
    plan.post("dwu", b, i)


def head_grads(plan, b, i, v):
    sh = SHAPES[b][i]
    for half in range(2):
        yield need("gb", b, i, half)
    weight_grad(sh, v.gb, v.mixed, v.dwp, sh.out_at)
    yield spent(0.8)
    plan.post("dwo", b, i)
    yield need("gp", b, i)
    weight_grad(sh, v.xf, v.gp, v.dwp, 0)
    yield spent(1.8)
    plan.post("dwp", b, i)


def head_sums(plan, b, i, v):
    yield need("gp", b, i)
    if b == 1:
        yield need("dwp", b, i)
    v.col_proj[:, :3 * SHAPES[b][i].inner] = jnp.sum(flat(v.gp).astype(F32), axis=0, keepdims=True)
    yield spent(0.4)
    plan.post("cols", b, i)


def lane_cut(ref, lane, stop):
    return ref.at[(slice(None),) * (len(ref.shape) - 1) + (slice(lane, stop),)]


def sums_of(plan, me, name, i, views, outs, t, sems, credit):
    pack, first, ranges = SUMS[i][name]
    neighbours = [me.along("z", 1), me.along("x", 1), me.along("x", 3), me.along("y", 1), me.along("y", 3)]
    for b in (1, 0):
        if ranges[b] is None:
            continue
        yield need("dwu" if pack == "u" else "dwo" if name == "o" else "dwp", b, i)
        if name in ("pa", "pb") and b == 1 and i == 0:
            yield need("dwo", b, i)
        if b == 0 and ranges[1] is not None:
            pl.semaphore_wait(credit, 5)
        dw = lane_cut(getattr(views[b][i], "dw" + pack), *ranges[b])
        out = lane_cut(outs[b][pack], *ranges[b])
        if i == 0:
            yield from reduce_text(me, dw, out, t, sems, first)
        else:
            yield from reduce_image(me, dw, out, t, sems, "x" if first else "y")
        if b == 1:
            for device in neighbours:
                pl.semaphore_signal(credit, inc=1, device_id=device, device_id_type=MESH)
    plan.post("summed", name, i)


def gathers(plan, me, b, i, n, v, g):
    pack, lane, stop, first, label, begin = GATHERS[b, i][n]
    yield need("packed", b, i)
    yield ("at", begin)
    sems = getattr(g, f"gather_sems{b}{i}{n}")
    started, ready = ("started", b, i, n), ("got", b, i, n)
    w = lane_cut(getattr(v, "w" + pack), lane, stop)
    if i == 0:
        yield from gather_text(me, lane_cut(getattr(g, f"pieces_{pack}{b}"), lane, stop), w, sems, started, ready, first)
    else:
        yield from gather_image(me, w, sems, started, ready, "x" if first else "y")
    rest = [k for k, other in enumerate(GATHERS[b, i]) if other[4] == label]
    if all(("got", b, i, k) in plan.done for k in rest):
        plan.post("w" + label, b, i)
        if label == "q" and not any(other[4] == "o" for other in GATHERS[b, i]):
            plan.post("wo", b, i)


def whole_kernel(g):
    plan = Plan()
    me = Place(plan)
    wires = [[Wire(me, getattr(g, f"part{i}"), getattr(g, f"from_sib{i}"), getattr(g, f"from_mate{i}"),
                   getattr(g, f"wire_sems{i}{h}"), *SHAPES[0][i].halves[h]) for h in range(2)] for i in range(2)]
    views = []
    lane = 0
    for b in range(2):
        pair = []
        for i in range(2):
            sh = SHAPES[b][i]
            v = Bag()
            v.wires = wires[i]
            for name in ("head_bias", "up_bias", "bias", "gain", "offset", "xf", "qkv", "mixed", "nf", "slope",
                         "active", "first", "second"):
                setattr(v, name, getattr(g, f"{name}{b}{i}"))
            for name in ("ids_col", "ids_row", "normed", "gs", "gb", "gu"):
                setattr(v, name, getattr(g, f"{name}{i}"))
            v.gm, v.gp = (getattr(g, f"gm0{b}"), getattr(g, f"gp0{b}")) if i == 0 else (g.gm1, g.gp1)
            for pack in "pu":
                wide = sh.columns[pack]
                w, dw = getattr(g, f"w{pack}{b}{i}"), getattr(g, f"w{pack}1{i}" if b == 0 else f"dw{pack}{i}")
                setattr(v, "w" + pack, lane_cut(w, 0, wide))
                setattr(v, "dw" + pack, lane_cut(dw, 0, wide))
            if i == 1:
                for name in ("mixed_rows", "gp_rows", "gm_parts", "to_rows", "to_parts"):
                    setattr(v, name, getattr(g, name))
            v.vec = g.vecs.at[:, lane:lane + sh.width]
            lane += sh.width
            k = 2 * (2 * b + i)
            v.col_proj = g.cols.at[k:k + 1]
            v.col_up = g.cols.at[k + 1:k + 2]
            pair.append(v)
        views.append(pair)

    def packed(b, i):
        sh, v = SHAPES[b][i], views[b][i]
        a, f = sh.inner, sh.hidden
        proj, out, up, down = [getattr(g, f"{p}{b}{i}") for p in ("proj", "out", "up", "down")]
        if i == 0:
            to_p, to_u = getattr(g, f"pieces_p{b}").at[me.y], getattr(g, f"pieces_u{b}").at[me.y]
        else:
            to_p, to_u = v.wp.at[me.x, me.z, me.y], v.wu.at[me.x, me.z, me.y]
        for c in range(3):
            to_p[:, c * a:(c + 1) * a] = proj[c]
        to_p[:, 3 * a:4 * a] = out[...]
        to_u[:, :f] = up[...]
        to_u[:, f:2 * f] = down[...]
        plan.post("packed", b, i)
    for i in range(2):
        packed(0, i)
    near = [me.along("z", 1), me.along("x", 1), me.along("x", 3), me.along("y", 1), me.along("y", 3)]
    greet(near + [me.along("x", 2), me.along("y", 2), me.sib, me.mate, me.far])
    entry = Trade(me, [(g.x0, g.x_got0), (g.x1, g.x_got1), (g.lengths0, g.lengths_got0), (g.lengths1, g.lengths_got1),
                       (g.cot0, g.cot_got0), (g.cot1, g.cot_got1)], g.entry_sems)
    out_trade = Trade(me, [(g.out0, g.out0_done), (g.out1, g.out1_done)], g.out_sems)
    grad_trades = [Trade(me, [(g.grad0, g.grad0_done)], g.grad_sems0), Trade(me, [(g.grad1, g.grad1_done)], g.grad_sems1)]
    base = (g.base0, g.base1)

    def opening():
        entry.start()
        yield spent(0.3)
        for i in range(2):
            packed(1, i)
        for b in range(2):
            for i in range(2):
                v, a = views[b][i], SHAPES[b][i].inner
                v.offset[:, :a] = v.head_bias[0:1].astype(F32)
                v.offset[:, a:2 * a] = jnp.zeros((1, a), F32)
                v.offset[:, 2 * a:] = v.head_bias[1:2].astype(F32)
        g.vecs[...] = jnp.zeros_like(g.vecs)
        g.cols[...] = jnp.zeros_like(g.cols)
        place = lax.broadcasted_iota(jnp.int32, (432, 448), 0)
        token = row_of_part(lax.broadcasted_iota(jnp.int32, (1, 448), 1))
        g.to_rows[...] = (place == token).astype(F32).astype(BF16)
        place = lax.broadcasted_iota(jnp.int32, (448, 432), 1)
        token = row_of_part(lax.broadcasted_iota(jnp.int32, (448, 1), 0))
        g.to_parts[...] = (place == token).astype(F32).astype(BF16)
        yield spent(2.0)
        yield ("at", 8.0)
        entry.finish()
        for i in range(2):
            set_ids(getattr(g, f"ids_col{i}"), getattr(g, f"lengths_got{i}"), 0)
            set_ids(getattr(g, f"ids_row{i}"), getattr(g, f"lengths_got{i}"), 1)
        for i, got in enumerate((g.x_got0, g.x_got1)):
            views[0][i].xf[me.own] = got[...]
            base[i][...] = got[...].astype(F32)
        yield spent(1.0)
        for i in range(2):
            plan.post("x", i)

    def begun(i, half):
        yield need("x", i)
        yield from stream(plan, i, half, views, base[i], (g.cot_got0, g.cot_got1)[i], (g.out0, g.out1)[i],
                          (g.grad0, g.grad1)[i])

    def closing():
        for i in range(2):
            for half in range(2):
                yield need("out", i, half)
        out_trade.start()

    def closing_grad(i):
        for half in range(2):
            yield need("grad", i, half)
        grad_trades[i].start()

    def vectors():
        for b in range(2):
            for i in range(2):
                yield need("cols", b, i)
        for i in range(2):
            for half in range(2):
                yield need("gb", 0, i, half)
        yield from total_steps(me, g.vecs, g.cols, g.vec_got, g.slots, g.small, g.vec_sum, g.cols_out, g.total_sems)

    tasks = []
    order = sorted((b, "qou".index(label), n, i) for (b, i), cuts in GATHERS.items()
                   for n, (_, _, _, _, label, _) in enumerate(cuts))
    for b, stage, n, i in order:
        tasks.append((RANKS["gather"], gathers(plan, me, b, i, n, views[b][i], g)))
    tasks.append((RANKS["gather"], opening()))
    for i in (1, 0):
        for half in range(2):
            tasks.append((RANKS["stream"], begun(i, half)))
    for b in range(2):
        for i in (1, 0):
            tasks.append((RANKS["attention"], attention(plan, b, i, views)))
            tasks.append((RANKS["attention"], attention_back(plan, b, i, views)))
    tasks.append((RANKS["close"], closing()))
    for i in range(2):
        tasks.append((RANKS["close"], closing_grad(i)))
    tasks.append((RANKS["vectors"], vectors()))
    for i in range(2):
        for name in SUMS[i]:
            t = Bag()
            for part in ("halves", "chunks", "across", "small_chunks", "pieces" if i == 0 else "small_halves"):
                setattr(t, part, getattr(g, f"{part}_{name}{i}"))
            outs = [{pack: getattr(g, f"sum_{pack}{b}{i}") for pack in "pu"} for b in range(2)]
            tasks.append((RANKS["sums"], sums_of(plan, me, name, i, views, outs, t, getattr(g, f"reduce_sems_{name}{i}"),
                                     getattr(g, f"credit_{name}{i}"))))
    for b in (1, 0):
        for i in (1, 0):
            tasks.append((RANKS[f"feed{b}"], feed_grads(plan, b, i, views[b][i])))
            tasks.append((RANKS[f"head{b}"], head_grads(plan, b, i, views[b][i])))
            tasks.append((RANKS["cols"], head_sums(plan, b, i, views[b][i])))
    plan.run(tasks)
    out_trade.finish()
    for trade in grad_trades:
        trade.finish()
    g.vecs_out[...] = g.vec_sum[...]
    for name in ("out0", "out1", "grad0", "grad1"):
        getattr(g, name + "_end")[...] = getattr(g, name + "_done")[...]


def call(kernel, inputs, outs, scratch, collective_id=None):
    names = list(inputs) + list(outs) + list(scratch)

    def body(*refs):
        bag = Bag()
        for name, ref in zip(names, refs):
            setattr(bag, name, ref)
        kernel(bag)
    vm = pl.BlockSpec(memory_space=pltpu.VMEM)
    results = pl.pallas_call(
        body, out_shape=list(outs.values()), in_specs=[vm] * len(inputs), out_specs=[vm] * len(outs),
        scratch_shapes=list(scratch.values()),
        compiler_params=pltpu.CompilerParams(collective_id=collective_id, has_side_effects=collective_id is not None,
                                             vmem_limit_bytes=LIMIT),
    )(*inputs.values())
    return dict(zip(outs, results))


def whole(inputs):
    outs, scratch = {}, {}
    for i in range(2):
        sh = SHAPES[0][i]
        slab = (sh.part, sh.width)
        for name in ("x_got", "cot_got"):
            scratch[f"{name}{i}"] = VMEM(slab, BF16)
        scratch[f"lengths_got{i}"] = VMEM((3, 4), jnp.int32)
        for name in ("out", "grad"):
            scratch[f"{name}{i}"] = VMEM(slab, BF16)
            scratch[f"{name}{i}_done"] = VMEM(slab, BF16)
            outs[f"{name}{i}_end"] = jax.ShapeDtypeStruct(slab, BF16)
        scratch[f"base{i}"] = VMEM(slab, F32)
        scratch[f"normed{i}"] = VMEM(slab, F32)
        for name in ("gs", "gb", "part"):
            scratch[f"{name}{i}"] = VMEM((4,) + slab, BF16)
        scratch[f"gu{i}"] = VMEM((4, sh.part, sh.hidden), BF16)
        scratch[f"from_sib{i}"] = VMEM((2,) + slab, BF16)
        scratch[f"from_mate{i}"] = VMEM(slab, BF16)
        for half in range(2):
            scratch[f"wire_sems{i}{half}"] = DMA((2, 6))
        scratch[f"grad_sems{i}"] = DMA((2, 1))
        scratch[f"ids_col{i}"] = VMEM((3, sh.length, 1), F32)
        scratch[f"ids_row{i}"] = VMEM((3, 1, sh.length), F32)
        for pack in "pu":
            wide = sh.columns[pack]
            matrix = (768, wide) if i == 0 else (4, 2, 4, 32, wide)
            self_wide = SHAPES[1][i].columns[pack]
            scratch[f"dw{pack}{i}"] = VMEM(matrix[:-1] + (self_wide,), BF16)
            for b in range(2):
                scratch[f"w{pack}{b}{i}"] = VMEM(matrix, BF16)
                cols = SHAPES[b][i].columns[pack]
                if i == 0:
                    scratch[f"pieces_{pack}{b}"] = VMEM((4, 24, cols), BF16)
                outs[f"sum_{pack}{b}{i}"] = jax.ShapeDtypeStruct((24 if i == 0 else 32, cols), F32)
        for b in range(2):
            for n in range(len(GATHERS[b, i])):
                scratch[f"gather_sems{b}{i}{n}"] = DMA((2, 13))
        for name, (pack, first, ranges) in SUMS[i].items():
            wide = max(r[1] - r[0] for r in ranges if r is not None)
            scratch[f"reduce_sems_{name}{i}"] = DMA((2, 13))
            scratch[f"credit_{name}{i}"] = pltpu.SemaphoreType.REGULAR
            if i == 1:
                sizes = {"halves": (2, 2, 2, 32, wide), "chunks": (2,) + ((4, 2) if first else (2, 4)) + (32, wide), "across": (32, wide),
                         "small_halves": (2, 32, wide), "small_chunks": (2, 2, 32, wide)}
            else:
                sizes = {"halves": (2, 96, wide), "chunks": (2, 96 if first else 192, wide),
                         "across": (4, 96, wide) if first else (96, wide),
                         "pieces": (4, 24, wide), "small_chunks": (3, 24, wide)}
            for part, size in sizes.items():
                scratch[f"{part}_{name}{i}"] = VMEM(size, BF16)
    scratch["mixed_rows"] = VMEM((432, 256), BF16)
    scratch["gp_rows"] = VMEM((432, 768), BF16)
    scratch["gm1"] = VMEM((432, 256), BF16)
    scratch["gm_parts"] = VMEM((4, 112, 256), BF16)
    scratch["gp1"] = VMEM((4, 112, 768), BF16)
    for b in range(2):
        scratch[f"gm0{b}"] = VMEM((384, SHAPES[b][0].inner), BF16)
        scratch[f"gp0{b}"] = VMEM((4, 96, 3 * SHAPES[b][0].inner), BF16)
    scratch["to_rows"] = VMEM((432, 448), BF16)
    scratch["to_parts"] = VMEM((448, 432), BF16)
    scratch["entry_sems"] = DMA((2, 6))
    scratch["out_sems"] = DMA((2, 2))
    lanes_all, cols_wide = 2 * (768 + 1024), 768
    scratch["vecs"] = VMEM((8, lanes_all), F32)
    scratch["cols"] = VMEM((8, cols_wide), F32)
    scratch["vec_got"] = VMEM((3, 8, lanes_all // 4), F32)
    scratch["small"] = VMEM((8, lanes_all // 4 + cols_wide), F32)
    scratch["slots"] = VMEM((3, 4, 8, lanes_all // 4 + cols_wide), F32)
    scratch["vec_sum"] = VMEM((8, lanes_all), F32)
    scratch["total_sems"] = DMA((2, 13))
    outs["vecs_out"] = jax.ShapeDtypeStruct((8, lanes_all), F32)
    outs["cols_out"] = jax.ShapeDtypeStruct((8, cols_wide), F32)
    for b in range(2):
        for i in range(2):
            sh = SHAPES[b][i]
            slab = (sh.part, sh.width)
            for name, shape, kind in (
                    ("offset", (1, 3 * sh.inner), F32), ("xf", (4,) + slab, BF16), ("nf", (4,) + slab, BF16),
                    ("qkv", (3 * sh.length, 3 * sh.inner), BF16), ("mixed", (4, sh.part, sh.inner), BF16),
                    ("slope", (4, sh.part, sh.hidden), BF16), ("active", (4, sh.part, sh.hidden), BF16),
                    ("first", slab, F32), ("second", slab, F32)):
                scratch[f"{name}{b}{i}"] = VMEM(shape, kind)
    return call(whole_kernel, inputs, outs, scratch, 0)


def finish_kernel(g):
    for i, count in enumerate((32, 36)):
        for name in ("out", "grad"):
            src, dst = getattr(g, f"{name}{i}"), getattr(g, f"{name}{i}_end")
            if i == 0:
                dst[...] = src[...].reshape(dst.shape)
            else:
                value = src[...].astype(F32)
                for b in range(3):
                    dst[b] = value[b * count:(b + 1) * count].astype(dst.dtype)
    lane = 0
    for k, n in enumerate(f"{b}{i}" for b in range(2) for i in range(2)):
        sum_p, sum_u = getattr(g, "sum_p" + n), getattr(g, "sum_u" + n)
        proj, out, up, down = [getattr(g, p + n) for p in ("proj", "out", "up", "down")]
        a, f = proj.shape[2], up.shape[1]
        for c in range(3):
            proj[c] = sum_p[:, c * a:(c + 1) * a]
        out[...] = sum_p[:, 3 * a:4 * a]
        up[...] = sum_u[:, :f]
        down[...] = sum_u[:, f:2 * f]
        head_bias, up_bias, bias, gain = [getattr(g, p + n) for p in ("head_bias", "up_bias", "bias", "gain")]
        head_bias[0:1] = g.cols[2 * k:2 * k + 1, :a]
        head_bias[1:2] = g.cols[2 * k:2 * k + 1, 2 * a:3 * a]
        up_bias[...] = g.cols[2 * k + 1:2 * k + 2, :f]
        width = bias.shape[1]
        bias[...] = g.vecs[0:4, lane:lane + width]
        gain[...] = g.vecs[4:6, lane:lane + width]
        lane += width


def on_device(*args):
    text_in, image_in, text_lengths, image_lengths, text_cot, image_cot = args[:6]
    matrix_names = ("proj", "out", "up", "down")
    small_names = ("head_bias", "up_bias", "bias", "gain")

    def tokens_of(value):
        value = value.reshape(-1, value.shape[-1])
        return jnp.pad(value, ((0, -value.shape[0] % 16), (0, 0)))
    inputs = {"x0": tokens_of(text_in), "x1": tokens_of(image_in), "cot0": tokens_of(text_cot),
              "cot1": tokens_of(image_cot), "lengths0": text_lengths, "lengths1": image_lengths}
    shapes = {}
    names = [f"{b}{i}" for b in range(2) for i in range(2)]
    for k, n in enumerate(names):
        for name, value in zip(matrix_names + small_names, args[6 + 8 * k:14 + 8 * k]):
            inputs[name + n] = value.transpose(1, 0, 2) if name == "proj" else value
            shapes[name + n] = jax.ShapeDtypeStruct(inputs[name + n].shape, F32)
    done = whole(inputs)
    ends, outs = {"vecs": done["vecs_out"], "cols": done["cols_out"]}, {}
    for name, like in (("out0", text_in), ("out1", image_in), ("grad0", text_in), ("grad1", image_in)):
        ends[name] = done[name + "_end"]
        outs[name + "_end"] = jax.ShapeDtypeStruct(like.shape, like.dtype)
    for n in names:
        ends["sum_p" + n] = done["sum_p" + n]
        ends["sum_u" + n] = done["sum_u" + n]
        for p in matrix_names + small_names:
            outs[p + n] = shapes[p + n]
    return tuple(value.transpose(1, 0, 2) if name.startswith("proj") else value
                 for name, value in call(finish_kernel, ends, outs, {}).items())


def solution(mesh):
    kinds = [P("rows", None, "seq"), P("rows", "seq"), P("rows", "seq"), P("rows", "seq"), P(None, "seq"),
             P(None, "seq"), P(), P()] * 4
    position = P("rows", "seq", None)
    return jax.shard_map(
        on_device, mesh=mesh,
        in_specs=tuple([position, position, P("rows", None), P("rows", None), position, position] + kinds),
        out_specs=tuple([position] * 4 + kinds), check_vma=False)
```

```python
import jax
import jax.numpy as jnp
from jax import lax
from jax.experimental import pallas as pl
from jax.experimental.pallas import tpu as pltpu
from jax.sharding import PartitionSpec as P

MESH = pl.DeviceIdType.MESH
VMEM = pltpu.VMEM
DMA = pltpu.SemaphoreType.DMA
F32, BF16 = jnp.float32, jnp.bfloat16
NN, NT, TN = ((1,), (0,)), ((1,), (1,)), ((0,), (0,))
EPS = 1e-05
MASKED = -1000000000.0
LIMIT = 63 * 1024 * 1024


class Bag:
    pass


RATE = {"x+": 48e3, "x-": 48e3, "y+": 48e3, "y-": 48e3, "z": 48e3, "over": 48e3, "beside": 600e3}
DELAY = {"beside": 1.1}


class Plan:
    def __init__(self):
        self.now = 0.0
        self.free = {}
        self.done = set()

    def post(self, *event):
        self.done.add(event)

    def arrival(self, link, size):
        self.now += 0.06
        begin = max(self.now, self.free.get(link, 0.0))
        self.free[link] = begin + size / RATE[link]
        return self.free[link] + DELAY.get(link, 3.6)

    def run(self, tasks):
        waiting = [[rank, n, task, ("at", 0.0)] for n, (rank, task) in enumerate(tasks)]
        while waiting:
            best = None
            for entry in waiting:
                kind, what = entry[3][:2]
                rank = entry[3][2] if len(entry[3]) > 2 else entry[0]
                if kind == "event":
                    if what not in self.done:
                        continue
                    due = self.now
                else:
                    due = max(what, self.now)
                key = (due, rank, entry[1])
                if best is None or key < best[0]:
                    best = (key, entry)
            assert best is not None, "stuck"
            entry = best[1]
            self.now = best[0][0]
            try:
                need = next(entry[2])
            except StopIteration:
                waiting.remove(entry)
                continue
            if need[0] == "for":
                self.now += need[1]
                need = ("at", self.now)
            entry[3] = need


class Place:
    def __init__(self, plan):
        r = lax.axis_index("rows")
        s = lax.axis_index("seq")
        self.plan = plan
        self.r, self.s = r, s
        self.x, self.z, self.y = r // 8, (r // 4) % 2, r % 4
        self.zh, self.c = s // 2, s % 2
        self.own = s
        self.sib_slab = self.zh * 2 + 1 - self.c
        self.mate_slab = (1 - self.zh) * 2 + self.c
        self.far_slab = (1 - self.zh) * 2 + 1 - self.c
        self.sib = (r, self.sib_slab)
        across = (self.x * 2 + 1 - self.z) * 4 + self.y
        self.mate = (across, self.mate_slab)
        self.far = (across, self.far_slab)

    def along(self, axis, step):
        x, z, y = self.x, self.z, self.y
        if axis == "x":
            x = (x + step) % 4
        elif axis == "y":
            y = (y + step) % 4
        else:
            z = 1 - z
        return ((x * 2 + z) * 4 + y, self.s)

    def push(self, src, dst, sems, k, device, link):
        copy = pltpu.make_async_remote_copy(
            src_ref=src, dst_ref=dst, send_sem=sems.at[0, k], recv_sem=sems.at[1, k],
            device_id=device, device_id_type=MESH)
        copy.start()
        size = src.dtype.itemsize
        for n in src.shape:
            size *= n
        copy.due = self.plan.arrival(link, size)
        return copy


def greet(devices):
    barrier = pltpu.get_barrier_semaphore()
    for device in devices:
        pl.semaphore_signal(barrier, inc=1, device_id=device, device_id_type=MESH)
    pl.semaphore_wait(barrier, len(devices))


def at(copy, *more):
    return ("at", max(c.due for c in (copy,) + more))


def need(*event):
    return ("event", event)


def spent(cost):
    return ("for", 0.72 * cost)


class Trade:
    def __init__(self, me, pairs, sems):
        self.me, self.pairs, self.sems = me, pairs, sems

    def copies(self):
        return [pltpu.make_async_remote_copy(
            src_ref=src, dst_ref=dst, send_sem=self.sems.at[0, k], recv_sem=self.sems.at[1, k],
            device_id=self.me.along("z", 1), device_id_type=MESH) for k, (src, dst) in enumerate(self.pairs)]

    def start(self):
        @pl.when(self.me.zh == 1)
        def _():
            for copy in self.copies():
                copy.start()

        @pl.when(self.me.zh == 0)
        def _():
            for src, dst in self.pairs:
                dst[...] = src[...]

    def finish(self):
        @pl.when(self.me.zh == 1)
        def _():
            for copy in self.copies():
                copy.wait()


def dot(a, b, dims):
    return lax.dot_general(a, b, (dims, ((), ())), preferred_element_type=F32)


def loop(count, body):
    for i in range(count):
        body(i)


def lanes(i, size=256, base=0):
    return slice(base + i * size, base + (i + 1) * size)


def span(start, size):
    return pl.ds(pl.multiple_of(start, 16), size)


def add_rows(dst, start, src, first, count):
    def one(i):
        to, come = span(start + 16 * i, 16), span(first + 16 * i, 16)
        total = dst[to].astype(F32)
        for ref in src:
            total = total + ref[come].astype(F32)
        dst[to] = total.astype(dst.dtype)
    loop(count // 16, one)


def add_slabs(dst, src, count):
    def one(i):
        to = dst(i)
        total = to[...].astype(F32)
        for ref in src(i):
            total = total + ref[...].astype(F32)
        to[...] = total.astype(to.dtype)
    loop(count, one)


def middle_of(columns):
    return columns // 256 * 128


def gather_text(me, pieces, w, sems, started, ready, z_first):
    columns = w.shape[1]
    cut = middle_of(columns)
    x, z, y = me.x, me.z, me.y
    copies = [me.push(pieces.at[y], pieces.at[y], sems, n, me.along("y", n + 1), link)
              for n, link in enumerate(("y+", "y+", "y-"))]
    yield at(*copies)
    for copy in copies:
        copy.wait_recv()
    base = (x * 2 + z) * 96
    w[span(base, 96)] = pieces[...].astype(F32).reshape(96, columns).astype(BF16)
    yield spent(0.2)
    right, left = me.along("x", 1), me.along("x", 3)
    block = w.at[span(base, 96)]
    if z_first:
        e = me.push(block, block, sems, 4, me.along("z", 1), "z")
        yield at(e)
        e.wait_recv()
        block = w.at[span(192 * x, 192)]
    f = me.push(block, block, sems, 5, right, "x+")
    g = me.push(block, block, sems, 6, left, "x-")
    if z_first:
        me.plan.post(*started)
    yield at(f)
    f.wait_recv()
    place = 192 * ((x + 3) % 4)
    block = w.at[span(place, 96)] if z_first else w.at[span(place + 96 * z, 96), :cut]
    h = me.push(block, block, sems, 7, right, "x+")
    yield at(g)
    g.wait_recv()
    place = 192 * ((x + 1) % 4)
    block = w.at[span(place + 96, 96)] if z_first else w.at[span(place + 96 * z, 96), cut:]
    i = me.push(block, block, sems, 8, left, "x-")
    copies += [f, g, h, i]
    if z_first:
        copies.append(e)
    else:
        me.plan.post(*started)
        over = []
        for n, step in enumerate((0, 3, 1)):
            block = w.at[span(192 * ((x + step) % 4) + 96 * z, 96)]
            over.append(me.push(block, block, sems, 9 + n, me.along("z", 1), "z"))
        yield at(h, i)
    if z_first:
        yield at(h, i)
    h.wait_recv()
    i.wait_recv()
    if not z_first:
        block = w.at[span(192 * ((x + 2) % 4) + 96 * z, 96)]
        over.append(me.push(block, block, sems, 12, me.along("z", 1), "z"))
        yield at(*over)
        for copy in over:
            copy.wait_recv()
        copies += over
    me.plan.post(*ready)
    for copy in copies:
        copy.wait_send()


def image_views(me, w, light):
    x, z, y = me.x, me.z, me.y
    if light == "x":
        return (lambda n: w.at[(x + n) % 4, :, y], lambda n, h: w.at[(x + n) % 4, h, y],
                lambda n: w.at[:, :, (y + n) % 4], lambda n, h: w.at[2 * h:2 * h + 2, :, (y + n) % 4])
    return (lambda n: w.at[x, :, (y + n) % 4], lambda n, h: w.at[x, h, (y + n) % 4],
            lambda n: w.at[(x + n) % 4], lambda n, h: w.at[(x + n) % 4, :, 2 * h:2 * h + 2])


def gather_image(me, w, sems, started, ready, light):
    x, z, y = me.x, me.z, me.y
    heavy = "y" if light == "x" else "x"
    few, few_half, many, many_half = image_views(me, w, light)
    copies = [me.push(w.at[x, z, y], w.at[x, z, y], sems, 0, me.along("z", 1), "z")]
    yield at(copies[0])
    copies[0].wait_recv()
    lights = [me.push(few(0), few(0), sems, n, me.along(light, n), light + "++-"[n - 1]) for n in (1, 2, 3)]
    yield at(*lights)
    for copy in lights:
        copy.wait_recv()
    copies += lights
    right, left = me.along(heavy, 1), me.along(heavy, 3)
    a = me.push(many(0), many(0), sems, 5, right, heavy + "+")
    b = me.push(many(0), many(0), sems, 6, left, heavy + "-")
    me.plan.post(*started)
    yield at(a)
    a.wait_recv()
    c = me.push(many_half(3, 0), many_half(3, 0), sems, 7, right, heavy + "+")
    yield at(b)
    b.wait_recv()
    d = me.push(many_half(1, 1), many_half(1, 1), sems, 8, left, heavy + "-")
    yield at(c, d)
    c.wait_recv()
    d.wait_recv()
    copies += [a, b, c, d]
    me.plan.post(*ready)
    for copy in copies:
        copy.wait_send()


def reduce_text(me, dw, out, t, sems, z_first):
    columns = dw.shape[1]
    cut = middle_of(columns)
    cost = columns / 2000.0
    x, z, y = me.x, me.z, me.y
    right, left = me.along("x", 1), me.along("x", 3)
    copies = []
    if z_first:
        def mine(step):
            return 192 * ((x + step) % 4) + 96 * z
        over = []
        for n, step in enumerate((2, 1, 3, 0)):
            place = (x + step) % 4
            over.append(me.push(dw.at[span(192 * place + 96 * (1 - z), 96)], t.across.at[place], sems, 9 + n,
                                me.along("z", 1), "z"))
        yield at(over[0])
        over[0].wait_recv()
        add_rows(dw, mine(2), [t.across.at[(x + 2) % 4]], 0, 96)
        a = me.push(dw.at[span(mine(2), 96), :cut], t.halves.at[0, :, :cut], sems, 0, right, "x+")
        b = me.push(dw.at[span(mine(2), 96), cut:], t.halves.at[1, :, cut:], sems, 1, left, "x-")
        yield spent(0.4 * cost)
        yield at(a, over[1])
        over[1].wait_recv()
        add_rows(dw, mine(1), [t.across.at[(x + 1) % 4]], 0, 96)
        a.wait_recv()
        add_rows(dw.at[:, :cut], mine(1), [t.halves.at[0, :, :cut]], 0, 96)
        c = me.push(dw.at[span(mine(1), 96)], t.chunks.at[0], sems, 2, right, "x+")
        yield spent(0.6 * cost)
        yield at(b, over[2])
        over[2].wait_recv()
        add_rows(dw, mine(3), [t.across.at[(x + 3) % 4]], 0, 96)
        b.wait_recv()
        add_rows(dw.at[:, cut:], mine(3), [t.halves.at[1, :, cut:]], 0, 96)
        d = me.push(dw.at[span(mine(3), 96)], t.chunks.at[1], sems, 3, left, "x-")
        yield spent(0.6 * cost)
        yield at(c, d, over[3])
        over[3].wait_recv()
        c.wait_recv()
        d.wait_recv()
        total = (dw[span(mine(0), 96)].astype(F32) + t.across[x].astype(F32) + t.chunks[0].astype(F32)
                 + t.chunks[1].astype(F32))
        copies += over
    else:
        far = 192 * ((x + 2) % 4)
        a = me.push(dw.at[span(far, 96)], t.halves.at[0], sems, 0, right, "x+")
        b = me.push(dw.at[span(far + 96, 96)], t.halves.at[1], sems, 1, left, "x-")
        yield at(a)
        a.wait_recv()
        first = 192 * ((x + 1) % 4)
        add_rows(dw, first, [t.halves.at[0]], 0, 96)
        c = me.push(dw.at[span(first, 192)], t.chunks.at[0], sems, 2, right, "x+")
        yield spent(0.4 * cost)
        yield at(b)
        b.wait_recv()
        first = 192 * ((x + 3) % 4)
        add_rows(dw, first + 96, [t.halves.at[1]], 0, 96)
        d = me.push(dw.at[span(first, 192)], t.chunks.at[1], sems, 3, left, "x-")
        yield spent(0.4 * cost)
        yield at(c, d)
        c.wait_recv()
        d.wait_recv()
        add_rows(dw, 192 * x + 96 * (1 - z), [t.chunks.at[0], t.chunks.at[1]], 96 * (1 - z), 96)
        e = me.push(dw.at[span(192 * x + 96 * (1 - z), 96)], t.across, sems, 4, me.along("z", 1), "z")
        add_rows(dw, 192 * x + 96 * z, [t.chunks.at[0], t.chunks.at[1]], 96 * z, 96)
        yield spent(1.0 * cost)
        yield at(e)
        e.wait_recv()
        total = dw[span(192 * x + 96 * z, 96)].astype(F32) + t.across[...].astype(F32)
        copies.append(e)
    t.pieces[...] = total.reshape(4, 24, columns).astype(BF16)
    yield spent(0.4 * cost)
    pieces = t.pieces
    last = [me.push(pieces.at[(y + n + 1) % 4], t.small_chunks.at[n], sems, 5 + n, me.along("y", n + 1), link)
            for n, link in enumerate(("y+", "y+", "y-"))]
    yield at(*last)
    for copy in last:
        copy.wait_recv()
    total = pieces[y].astype(F32) + t.small_chunks[0].astype(F32)
    out[...] = total + t.small_chunks[1].astype(F32) + t.small_chunks[2].astype(F32)
    copies += [a, b, c, d] + last
    for copy in copies:
        copy.wait_send()
    yield spent(0.2 * cost)


def add_block(dst, src):
    lead = [()]
    for n in dst.shape[:-2]:
        lead = [at_ + (k,) for at_ in lead for k in range(n)]
    for place in lead:
        total = dst[place].astype(F32)
        for ref in src:
            total = total + ref[place].astype(F32)
        dst[place] = total.astype(dst.dtype)


def reduce_image(me, dw, out, t, sems, light):
    cost = dw.shape[4] / 1500.0
    x, z, y = me.x, me.z, me.y
    heavy = "y" if light == "x" else "x"
    few, few_half, many, many_half = image_views(me, dw, light)
    copies = []
    right, left = me.along(heavy, 1), me.along(heavy, 3)
    a = me.push(many_half(2, 0), t.halves.at[0], sems, 0, right, heavy + "+")
    b = me.push(many_half(2, 1), t.halves.at[1], sems, 1, left, heavy + "-")
    yield at(a)
    a.wait_recv()
    add_block(many_half(1, 0), [t.halves.at[0]])
    c = me.push(many(1), t.chunks.at[0], sems, 2, right, heavy + "+")
    yield spent(0.4 * cost)
    yield at(b)
    b.wait_recv()
    add_block(many_half(3, 1), [t.halves.at[1]])
    d = me.push(many(3), t.chunks.at[1], sems, 3, left, heavy + "-")
    yield spent(0.4 * cost)
    yield at(c, d)
    c.wait_recv()
    d.wait_recv()
    add_block(many(0), [t.chunks.at[0], t.chunks.at[1]])
    lights = [me.push(few(n), t.small_chunks.at[n - 1], sems, 3 + n, me.along(light, n), light + "++-"[n - 1])
              for n in (2, 1, 3)]
    yield spent(1.2 * cost)
    yield at(*lights)
    for copy in lights:
        copy.wait_recv()
    add_block(few(0), [t.small_chunks.at[n] for n in range(3)])
    copies += [a, b, c, d] + lights
    yield spent(0.4 * cost)
    i = me.push(dw.at[x, 1 - z, y], t.across, sems, 8, me.along("z", 1), "z")
    yield at(i)
    i.wait_recv()
    out[...] = dw[x, z, y].astype(F32) + t.across[...].astype(F32)
    for copy in copies + [i]:
        copy.wait_send()
    yield spent(0.2 * cost)


def total_steps(me, vecs, cols, got, slots, small, vec_out, col_out, sems):
    wide = vecs.shape[1] // 4

    def quarter(k):
        return pl.ds(pl.multiple_of(k * wide, 128), wide)
    mates = ((me.sib, me.sib_slab, "beside"), (me.mate, me.mate_slab, "over"), (me.far, me.far_slab, "over"))
    sent = [me.push(vecs.at[:, quarter(slab)], got.at[k], sems, k, device, link)
            for k, (device, slab, link) in enumerate(mates)]
    yield at(*sent)
    for copy in sent:
        copy.wait_recv()
    small[:, :wide] = vecs[:, quarter(me.own)] + got[0] + got[1] + got[2]
    small[:, wide:] = cols[...]
    k = 3
    for stage, (axis, place, count) in enumerate((("x", me.x, 4), ("y", me.y, 4), ("z", me.z, 2))):
        slots[stage, place] = small[...]
        copies = [me.push(slots.at[stage, place], slots.at[stage, place], sems, k + n, me.along(axis, n + 1),
                          axis + "++-"[n] if count == 4 else "z") for n in range(count - 1)]
        k += count - 1
        yield at(*copies)
        for copy in copies:
            copy.wait_recv()
        total = slots[stage, 0] + slots[stage, 1]
        if count == 4:
            total = total + slots[stage, 2] + slots[stage, 3]
        small[...] = total
        sent += copies
    col_out[...] = small[:, wide:]
    vec_out[:, quarter(me.own)] = small[:, :wide]
    mine = vec_out.at[:, quarter(me.own)]
    last = [me.push(mine, mine, sems, k + n, device, link) for n, (device, slab, link) in enumerate(mates)]
    yield at(*last)
    for copy in last:
        copy.wait_recv()
    for copy in sent + last:
        copy.wait_send()


class Wire:
    def __init__(self, me, part, from_sib, from_mate, sems, start, size):
        self.me, self.part, self.from_sib, self.from_mate, self.sems = me, part, from_sib, from_mate, sems
        self.start, self.size = start, size
        self.rows = pl.ds(start, size)
        self.steps = [pl.ds(start + 16 * i, 16) for i in range(size // 16)]

    def gather(self, buf):
        me, rows = self.me, self.rows
        mine, theirs = buf.at[me.own, rows], buf.at[me.mate_slab, rows]
        over = me.push(mine, mine, self.sems, 0, me.mate, "over")
        beside = me.push(mine, mine, self.sems, 1, me.sib, "beside")
        yield at(over) + (-1,)
        over.wait_recv()
        on = me.push(theirs, theirs, self.sems, 2, me.sib, "beside")
        yield at(beside, on)
        beside.wait_recv()
        on.wait_recv()
        for copy in (over, beside, on):
            copy.wait_send()

    def reduce(self):
        me, part, from_sib, rows = self.me, self.part, self.from_sib, self.rows
        a = me.push(part.at[me.far_slab, rows], from_sib.at[0, rows], self.sems, 3, me.sib, "beside")
        b = me.push(part.at[me.sib_slab, rows], from_sib.at[1, rows], self.sems, 4, me.sib, "beside")
        yield at(a) + (-1,)
        a.wait_recv()
        for step in self.steps:
            part[me.mate_slab, step] = (
                part[me.mate_slab, step].astype(F32) + from_sib[0, step].astype(F32)).astype(BF16)
        d = me.push(part.at[me.mate_slab, rows], self.from_mate.at[rows], self.sems, 5, me.mate, "over")
        yield spent(0.2)
        yield at(b, d)
        b.wait_recv()
        d.wait_recv()
        for copy in (a, b, d):
            copy.wait_send()

    def total(self, rows):
        return (self.part[self.me.own, rows].astype(F32) + self.from_sib[1, rows].astype(F32)
                + self.from_mate[rows].astype(F32))


class Shape:
    def __init__(self, stream, part, length, width, inner, hidden, head):
        self.stream, self.part, self.length, self.width = stream, part, length, width
        self.inner, self.hidden, self.head = inner, hidden, head
        self.tokens = 4 * part
        self.out_at = 3 * inner
        self.columns = {"p": 4 * inner, "u": 2 * hidden}
        self.halves = ((0, 48), (48, 48)) if stream == 0 else ((0, 64), (64, 48))


SHAPES = ((Shape(0, 96, 128, 768, 256, 768, 128), Shape(1, 112, 144, 1024, 256, 256, 128)),
          (Shape(0, 96, 128, 768, 192, 768, 64), Shape(1, 112, 144, 1024, 256, 256, 128)))

GATHERS = {
    (0, 0): (
        ("p", 0, 384, False, "q", 6),
        ("p", 384, 768, True, "q", 0),
        ("p", 768, 1024, False, "o", 1),
        ("u", 0, 768, False, "u", 22),
        ("u", 768, 1536, True, "u", 19),
    ),
    (0, 1): (
        ("p", 0, 384, True, "q", 3),
        ("p", 384, 768, True, "q", 0),
        ("p", 768, 1024, False, "o", 3),
        ("u", 0, 512, True, "u", 14),
    ),
    (1, 0): (
        ("p", 0, 384, True, "q", 38),
        ("p", 384, 768, False, "q", 39),
        ("u", 0, 768, True, "u", 44),
        ("u", 768, 1536, False, "u", 57),
    ),
    (1, 1): (
        ("p", 0, 1024, True, "q", 18),
        ("u", 0, 512, True, "u", 45),
    ),
}
SUMS = (
    {
        "ua": ("u", False, ((0, 768), (0, 768))),
        "ub": ("u", True, ((768, 1536), (768, 1536))),
        "pa": ("p", True, ((0, 384), (0, 384))),
        "pb": ("p", False, ((384, 768), (384, 768))),
        "o": ("p", True, ((768, 1024), None)),
    },
    {
        "u": ("u", True, ((0, 512), (0, 512))),
        "qa": ("p", True, ((0, 384), (0, 384))),
        "qb": ("p", True, ((384, 768), (384, 768))),
        "o": ("p", False, ((768, 1024), (768, 1024))),
    },
)
RANKS = {
    "gather000": 3, "gather001": 2, "gather002": 2, "gather003": 0.7, "gather004": 1.5, "gather010": 0.7,
    "gather011": 0, "gather012": 0.9, "gather013": 0.9, "gather100": 0.7, "gather101": 1.5, "gather102": 0,
    "gather103": 2, "gather110": 4, "gather111": 1.5, "stream00": 1.1, "stream01": 1.5, "stream10": 2,
    "stream11": 1.1, "attention00": 2, "back00": 1.1, "feed00": 3, "head00": 0.9, "cols00": 0.3, "attention01":
    0.3, "back01": 1, "feed01": 3, "head01": 1, "cols01": 0.5, "attention10": 0.7, "back10": 0.5, "feed10": 0.3,
    "head10": 3, "cols10": 4, "attention11": 3, "back11": 0.9, "feed11": 2.5, "head11": 1.1, "cols11": 0.9,
    "sums0ua": 3, "sums0ub": 4, "sums0pa": 2.5, "sums0pb": 1, "sums0o": 1.1, "sums1u": 0, "sums1qa": 1,
    "sums1qb": 0, "sums1o": 0.5, "close": 0.3, "vectors": 0.3}


def columns_of(sh, w, cols):
    if sh.stream == 0:
        return w[:, cols]
    return w[:, :, :, :, cols].reshape(sh.width, -1)


def rows_of(sh, w, i, cols):
    if sh.stream == 0:
        return w[lanes(i), cols]
    value = w[i, :, :, :, cols]
    return value.reshape(256, value.shape[-1])


def set_rows(sh, w, i, cols, value):
    if sh.stream == 0:
        w[lanes(i), cols] = value
    else:
        w[i, :, :, :, cols] = value.reshape(2, 4, 32, value.shape[-1])


def normal(value):
    centre = jnp.mean(value, axis=-1, keepdims=True)
    moved = value - centre
    scale = lax.rsqrt(jnp.mean(moved * moved, axis=-1, keepdims=True) + EPS)
    return moved * scale, scale


def flat(ref):
    value = ref[...]
    return value.reshape(value.shape[0] * value.shape[1], value.shape[2])


def part_of(ref, rows):
    value = ref[:, rows]
    return value.reshape(value.shape[0] * value.shape[1], value.shape[2])


def put_by_row(ref, half, cols, value):
    runs = ((0, 0, 32, 0), (1, 0, 16, 32)) if half == 0 else ((1, 16, 16, 0), (2, 0, 32, 16))
    for p in range(4):
        for b, q, count, offset in runs:
            to = 128 * b + 32 * p + q
            ref[to:to + count, cols] = value[48 * p + offset:48 * p + offset + count]


def put_by_part(ref, b, cols, value):
    for p in range(4):
        ref[p, 32 * b:32 * b + 32, cols] = value[32 * p:32 * p + 32]


def project(sh, v, half):
    whole = part_of(v.xf, v.wires[half].rows)

    def put(cols, value):
        if sh.stream == 0:
            put_by_row(v.qkv, half, cols, value)
        else:
            v.gp[:, v.wires[half].rows, cols] = value.reshape(4, v.wires[half].size, -1)
    if sh.inner % 256:
        cols = slice(0, 3 * sh.inner)
        put(cols, (dot(whole, columns_of(sh, v.wp, cols), NN) + v.offset[...]).astype(BF16))
    else:
        def one(i):
            cols = lanes(i)
            put(cols, (dot(whole, columns_of(sh, v.wp, cols), NN) + v.offset[:, cols]).astype(BF16))
        loop(3 * sh.inner // 256, one)


def probabilities(query, key, col_ids, row_ids, scale):
    raw = dot(query, key, NT)
    scores = jnp.where(col_ids == row_ids, raw * scale, MASKED)
    grown = jnp.exp(scores - jnp.max(scores, axis=-1, keepdims=True))
    return grown * (1.0 / jnp.sum(grown, axis=-1, keepdims=True))


def attend(sh, v, kv, key_length):
    h, a = sh.head, sh.inner
    for b in range(3):
        mine = pl.ds(b * sh.length, sh.length)
        theirs = pl.ds(b * key_length, key_length)
        for n in range(a // h):
            q_at, k_at, v_at = [slice(c * a + n * h, c * a + (n + 1) * h) for c in range(3)]
            p = probabilities(v.qkv[mine, q_at], kv.qkv[theirs, k_at], v.ids_col[b], kv.ids_row[b], h ** -0.5)
            result = dot(p.astype(BF16), kv.qkv[theirs, v_at], NN).astype(BF16)
            if sh.stream == 0:
                put_by_part(v.mixed, b, q_at, result)
            else:
                v.mixed_rows[mine, q_at] = result
        yield spent(0.6)
    if sh.stream == 1:
        v.mixed[...] = dot(v.to_parts[...], v.mixed_rows[...], NN).astype(BF16).reshape(4, sh.part, a)
        yield spent(0.3)


def spread_out(sh, v, half, left, w, cols):
    wire = v.wires[half]
    value = part_of(left, wire.rows)

    def one(i):
        result = dot(value, rows_of(sh, w, i, cols), NT)
        wire.part[:, wire.rows, lanes(i)] = result.reshape(4, wire.size, 256).astype(BF16)
    loop(sh.width // 256, one)


def norm_forward(sh, v, half, base, sums, which, result, low):
    bias = v.bias[which:which + 1].astype(F32)
    shift = v.bias[2 + which:3 + which].astype(F32)
    gain = v.gain[which:which + 1].astype(F32)
    for rows in v.wires[half].steps:
        value = base[rows] + v.wires[half].total(rows) + bias
        sums[rows] = value
        value = normal(value)[0] * gain + shift
        result[rows] = value
        low[rows] = value.astype(BF16)


def feed(sh, v, half):
    wire = v.wires[half]
    whole = part_of(v.nf, wire.rows)
    k = (2.0 / jnp.pi) ** 0.5

    def one(i):
        cols = lanes(i)
        u = dot(whole, columns_of(sh, v.wu, cols), NN) + v.up_bias[:, cols].astype(F32)
        square = u * u
        t = jnp.tanh(k * u * (1.0 + 0.044715 * square))
        half_sum = 0.5 * (1.0 + t)
        slope = half_sum + 0.5 * u * (1.0 - t * t) * (k * (1.0 + 3 * 0.044715 * square))
        v.active[:, wire.rows, cols] = (u * half_sum).astype(BF16).reshape(4, wire.size, 256)
        v.slope[:, wire.rows, cols] = slope.astype(BF16).reshape(4, wire.size, 256)
    loop(sh.hidden // 256, one)


def norm_backward(sh, v, half, grad, sums, which, result, low, bias_row):
    gain = v.gain[which:which + 1].astype(F32)

    def fold(value):
        return value[:8] + value[8:]
    totals = None
    for rows in v.wires[half].steps:
        g = grad(rows)
        n, scale = normal(sums[rows])
        gn = g * gain
        out = scale * (gn - jnp.mean(gn, axis=-1, keepdims=True) - n * jnp.mean(gn * n, axis=-1, keepdims=True))
        rounded = out.astype(BF16)
        result[rows] = out
        low[rows] = rounded
        terms = (fold(rounded.astype(F32)), fold(g), fold(g * n))
        totals = terms if totals is None else tuple(x + y for x, y in zip(totals, terms))
    for at_row, total in zip((bias_row, 2 + which, 4 + which), totals):
        v.vec[at_row:at_row + 1] += jnp.sum(total, axis=0, keepdims=True)


def weight_grad(sh, left, right, dw, start):
    cols = slice(start, start + right.shape[2])

    def one(i):
        piece = left[:, :, lanes(i)].reshape(sh.tokens, 256)
        set_rows(sh, dw, i, cols, dot(piece, flat(right), TN).astype(BF16))
    loop(sh.width // 256, one)


def feed_back(sh, v, half):
    wire = v.wires[half]
    whole = part_of(v.gs, wire.rows)

    def one(i):
        cols = lanes(i)
        grad = dot(whole, columns_of(sh, v.wu, lanes(i, 256, sh.hidden)), NN)
        gu = (grad * v.slope[:, wire.rows, cols].reshape(4 * wire.size, 256).astype(F32)).astype(BF16)
        v.gu[:, wire.rows, cols] = gu.reshape(4, wire.size, 256)
        v.col_up[:, cols] += jnp.sum(gu.astype(F32), axis=0, keepdims=True)
    loop(sh.hidden // 256, one)


def mix_back(sh, v, half):
    wire = v.wires[half]
    cols = slice(sh.out_at, sh.out_at + sh.inner)
    value = dot(part_of(v.gb, wire.rows), columns_of(sh, v.wp, cols), NN).astype(BF16)
    if sh.stream == 0:
        put_by_row(v.gm, half, slice(0, sh.inner), value)
    else:
        v.gm_parts[:, wire.rows] = value.reshape(4, wire.size, sh.inner)


def attend_back(sh, v, key_sh, kv):
    h, a = sh.head, sh.inner
    scale = h ** -0.5

    def put(to_sh, to, b, cols, value):
        value = value.astype(BF16)
        if to_sh.stream == 0:
            put_by_part(to.gp, b, cols, value)
        else:
            to.gp_rows[pl.ds(b * to_sh.length, to_sh.length), cols] = value
    if sh.stream == 1:
        v.gm[...] = dot(v.to_rows[...], flat(v.gm_parts), NN).astype(BF16)
    for b in range(3):
        mine = pl.ds(b * sh.length, sh.length)
        theirs = pl.ds(b * key_sh.length, key_sh.length)
        for n in range(a // h):
            q_at, k_at, v_at = [slice(c * a + n * h, c * a + (n + 1) * h) for c in range(3)]
            query, key, value = v.qkv[mine, q_at], kv.qkv[theirs, k_at], kv.qkv[theirs, v_at]
            grad = v.gm[mine, q_at]
            p = probabilities(query, key, v.ids_col[b], kv.ids_row[b], scale)
            gp = dot(grad, value, NT)
            gs = (p * (gp - jnp.sum(gp * p, axis=-1, keepdims=True)) * scale).astype(BF16)
            put(sh, v, b, q_at, dot(gs, key, NN))
            put(key_sh, kv, b, k_at, dot(gs, query, TN))
            put(key_sh, kv, b, v_at, dot(p.astype(BF16), grad, TN))
        yield spent(1.3)


def set_ids(ref, lengths, axis):
    shape = ref.shape[1:]
    position = lax.broadcasted_iota(jnp.int32, shape, axis)
    for b in range(3):
        bound = jnp.zeros((1, 1), jnp.int32)
        seg = jnp.zeros(shape, jnp.int32)
        for j in range(4):
            bound = bound + lengths[b:b + 1, j:j + 1]
            seg = seg + (position >= bound).astype(jnp.int32)
        ref[b] = seg.astype(F32)


def row_of_part(token):
    def over(value, size, most):
        return sum((value >= k * size).astype(jnp.int32) for k in range(1, most))
    p = over(token, 112, 4)
    within = token - 112 * p
    row = over(within, 36, 4)
    return jnp.where(row < 3, 144 * row + 36 * p + within - 36 * row, -1)


def stream(plan, i, half, views, base, cot, outs, grads):
    big = i == 0
    for b in range(2):
        sh, v = SHAPES[b][i], views[b][i]
        wire = v.wires[half]
        own = wire.me.own
        yield from wire.gather(v.xf)
        yield need("wq", b, i)
        project(sh, v, half)
        yield spent(0.6)
        plan.post("qkv", b, i, half)
        yield need("mixed", b, i)
        yield need("wo", b, i)
        spread_out(sh, v, half, v.mixed, v.wp, slice(sh.out_at, sh.out_at + sh.inner))
        yield spent(0.4)
        yield from wire.reduce()
        norm_forward(sh, v, half, base, v.first, 0, v.normed, v.nf.at[own])
        yield spent(0.4)
        yield from wire.gather(v.nf)
        yield need("wu", b, i)
        feed(sh, v, half)
        yield spent(1.1 if big else 0.6)
        spread_out(sh, v, half, v.active, v.wu, slice(sh.hidden, 2 * sh.hidden))
        yield spent(0.7 if big else 0.4)
        yield from wire.reduce()
        norm_forward(sh, v, half, v.normed, v.second, 1, base, views[1][i].xf.at[own] if b == 0 else outs)
        yield spent(0.4)
    plan.post("out", i, half)
    for b in (1, 0):
        sh, v = SHAPES[b][i], views[b][i]
        wire = v.wires[half]
        own = wire.me.own
        norm_backward(sh, v, half, (lambda rows: cot[rows].astype(F32)) if b == 1 else (lambda rows: base[rows]),
                      v.second, 1, v.normed, v.gs.at[own], 1)
        yield spent(0.6)
        yield from wire.gather(v.gs)
        plan.post("gs", b, i, half)
        if b == 0:
            yield need("dwu", 1, i)
        feed_back(sh, v, half)
        yield spent(0.9 if big else 0.5)
        plan.post("gu", b, i, half)
        if b == 0:
            yield need("dwo", 1, i)
        spread_out(sh, v, half, v.gu, v.wu, slice(0, sh.hidden))
        yield spent(0.7 if big else 0.4)
        yield from wire.reduce()
        norm_backward(sh, v, half, lambda rows, v=v: v.normed[rows] + v.wires[half].total(rows), v.first, 0, v.normed,
                      v.gb.at[own], 0)
        yield spent(0.6)
        yield from wire.gather(v.gb)
        plan.post("gb", b, i, half)
        mix_back(sh, v, half)
        yield spent(0.4)
        plan.post("gm", b, i, half)
        yield need("gp", b, i)
        if b == 1:
            yield need("dwd", 1, i)
        spread_out(sh, v, half, v.gp, v.wp, slice(0, 3 * sh.inner))
        yield spent(0.7)
        yield from wire.reduce()
        for rows in wire.steps:
            value = v.normed[rows] + wire.total(rows)
            if b == 1:
                base[rows] = value
            else:
                grads[rows] = value.astype(BF16)
        yield spent(0.2)
    plan.post("grad", i, half)


def attention(plan, b, i, views):
    key_stream = 1 - i if b == 0 else i
    sh, v = SHAPES[b][i], views[b][i]
    kv = views[b][key_stream]
    for half in range(2):
        yield need("qkv", b, i, half)
    if i == 1:
        v.qkv[...] = dot(v.to_rows[...], flat(v.gp), NN).astype(BF16)
        yield spent(0.6)
    plan.post("rows", b, i)
    yield need("rows", b, key_stream)
    for half in range(2):
        yield need("qkv", b, key_stream, half)
    yield from attend(sh, v, kv, SHAPES[b][key_stream].length)
    plan.post("mixed", b, i)


def attention_back(plan, b, i, views):
    key_stream = 1 - i if b == 0 else i
    sh, v = SHAPES[b][i], views[b][i]
    for half in range(2):
        yield need("gm", b, i, half)
    if b == 0:
        yield need("gp", 1, 0)
        yield need("gp", 1, 1)
        yield need("dwp", 1, 1)
    yield from attend_back(sh, v, SHAPES[b][key_stream], views[b][key_stream])
    plan.post("attended", b, i)
    yield need("attended", b, key_stream)
    if i == 1:
        v.gp[...] = dot(v.to_parts[...], v.gp_rows[...], NN).astype(BF16).reshape(4, sh.part, 3 * sh.inner)
        yield spent(0.6)
    plan.post("gp", b, i)


def feed_grads(plan, b, i, v):
    sh = SHAPES[b][i]
    for half in range(2):
        yield need("gs", b, i, half)
    weight_grad(sh, v.gs, v.active, v.dwu, sh.hidden)
    yield spent(1.6 if i == 0 else 0.9)
    plan.post("dwd", b, i)
    for half in range(2):
        yield need("gu", b, i, half)
    weight_grad(sh, v.nf, v.gu, v.dwu, 0)
    yield spent(1.6 if i == 0 else 0.9)
    plan.post("dwu", b, i)


def head_grads(plan, b, i, v):
    sh = SHAPES[b][i]
    for half in range(2):
        yield need("gb", b, i, half)
    weight_grad(sh, v.gb, v.mixed, v.dwp, sh.out_at)
    yield spent(0.8)
    plan.post("dwo", b, i)
    yield need("gp", b, i)
    weight_grad(sh, v.xf, v.gp, v.dwp, 0)
    yield spent(1.8)
    plan.post("dwp", b, i)


def head_sums(plan, b, i, v):
    yield need("gp", b, i)
    if b == 1:
        yield need("dwp", b, i)
    v.col_proj[:, :3 * SHAPES[b][i].inner] = jnp.sum(flat(v.gp).astype(F32), axis=0, keepdims=True)
    yield spent(0.4)
    plan.post("cols", b, i)


def lane_cut(ref, lane, stop):
    return ref.at[(slice(None),) * (len(ref.shape) - 1) + (slice(lane, stop),)]


def sums_of(plan, me, name, i, views, outs, t, sems, credit):
    pack, first, ranges = SUMS[i][name]
    neighbours = [me.along("z", 1), me.along("x", 1), me.along("x", 3), me.along("y", 1), me.along("y", 3)]
    for b in (1, 0):
        if ranges[b] is None:
            continue
        yield need("dwu" if pack == "u" else "dwo" if name == "o" else "dwp", b, i)
        if name in ("pa", "pb") and b == 1 and i == 0:
            yield need("dwo", b, i)
        if b == 0 and ranges[1] is not None:
            pl.semaphore_wait(credit, 5)
        dw = lane_cut(getattr(views[b][i], "dw" + pack), *ranges[b])
        out = lane_cut(outs[b][pack], *ranges[b])
        if i == 0:
            yield from reduce_text(me, dw, out, t, sems, first)
        else:
            yield from reduce_image(me, dw, out, t, sems, "x" if first else "y")
        if b == 1:
            for device in neighbours:
                pl.semaphore_signal(credit, inc=1, device_id=device, device_id_type=MESH)
    plan.post("summed", name, i)


def gathers(plan, me, b, i, n, v, g):
    pack, lane, stop, first, label, begin = GATHERS[b, i][n]
    yield need("packed", b, i)
    yield ("at", begin)
    sems = getattr(g, f"gather_sems{b}{i}{n}")
    started, ready = ("started", b, i, n), ("got", b, i, n)
    w = lane_cut(getattr(v, "w" + pack), lane, stop)
    if i == 0:
        yield from gather_text(me, lane_cut(getattr(g, f"pieces_{pack}{b}"), lane, stop), w, sems, started, ready, first)
    else:
        yield from gather_image(me, w, sems, started, ready, "x" if first else "y")
    rest = [k for k, other in enumerate(GATHERS[b, i]) if other[4] == label]
    if all(("got", b, i, k) in plan.done for k in rest):
        plan.post("w" + label, b, i)
        if label == "q" and not any(other[4] == "o" for other in GATHERS[b, i]):
            plan.post("wo", b, i)


def whole_kernel(g):
    plan = Plan()
    me = Place(plan)
    wires = [[Wire(me, getattr(g, f"part{i}"), getattr(g, f"from_sib{i}"), getattr(g, f"from_mate{i}"),
                   getattr(g, f"wire_sems{i}{h}"), *SHAPES[0][i].halves[h]) for h in range(2)] for i in range(2)]
    views = []
    lane = 0
    for b in range(2):
        pair = []
        for i in range(2):
            sh = SHAPES[b][i]
            v = Bag()
            v.wires = wires[i]
            for name in ("head_bias", "up_bias", "bias", "gain", "offset", "xf", "qkv", "mixed", "nf", "slope",
                         "active", "first", "second"):
                setattr(v, name, getattr(g, f"{name}{b}{i}"))
            for name in ("ids_col", "ids_row", "normed", "gs", "gb", "gu"):
                setattr(v, name, getattr(g, f"{name}{i}"))
            v.gm, v.gp = (getattr(g, f"gm0{b}"), getattr(g, f"gp0{b}")) if i == 0 else (g.gm1, g.gp1)
            for pack in "pu":
                wide = sh.columns[pack]
                w, dw = getattr(g, f"w{pack}{b}{i}"), getattr(g, f"w{pack}1{i}" if b == 0 else f"dw{pack}{i}")
                setattr(v, "w" + pack, lane_cut(w, 0, wide))
                setattr(v, "dw" + pack, lane_cut(dw, 0, wide))
            if i == 1:
                for name in ("gp_rows", "gm_parts", "to_rows", "to_parts"):
                    setattr(v, name, getattr(g, name))
                v.mixed_rows = g.gm1
            v.vec = g.vecs.at[:, lane:lane + sh.width]
            lane += sh.width
            k = 2 * (2 * b + i)
            v.col_proj = g.cols.at[k:k + 1]
            v.col_up = g.cols.at[k + 1:k + 2]
            pair.append(v)
        views.append(pair)

    def packed(b, i):
        sh, v = SHAPES[b][i], views[b][i]
        a, f = sh.inner, sh.hidden
        proj, out, up, down = [getattr(g, f"{p}{b}{i}") for p in ("proj", "out", "up", "down")]
        if i == 0:
            to_p, to_u = getattr(g, f"pieces_p{b}").at[me.y], getattr(g, f"pieces_u{b}").at[me.y]
        else:
            to_p, to_u = v.wp.at[me.x, me.z, me.y], v.wu.at[me.x, me.z, me.y]
        for c in range(3):
            to_p[:, c * a:(c + 1) * a] = proj[c]
        to_p[:, 3 * a:4 * a] = out[...]
        to_u[:, :f] = up[...]
        to_u[:, f:2 * f] = down[...]
        plan.post("packed", b, i)
    for i in range(2):
        packed(0, i)
    near = [me.along("z", 1), me.along("x", 1), me.along("x", 3), me.along("y", 1), me.along("y", 3)]
    greet(near + [me.along("x", 2), me.along("y", 2), me.sib, me.mate, me.far])
    entry = Trade(me, [(g.out0, g.xf00.at[me.own]), (g.out1, g.xf01.at[me.own]), (g.lengths0, g.lengths_got0),
                       (g.lengths1, g.lengths_got1), (g.grad0, g.cot_got0), (g.grad1, g.cot_got1)], g.entry_sems)
    out_trade = Trade(me, [(g.out0, g.out0_done), (g.out1, g.out1_done)], g.out_sems)
    grad_trades = [Trade(me, [(g.grad0, g.grad0_done)], g.grad_sems0), Trade(me, [(g.grad1, g.grad1_done)], g.grad_sems1)]
    base = (g.base0, g.base1)

    def opening():
        for name, held in (("x", "out"), ("cot", "grad")):
            getattr(g, held + "0")[...] = getattr(g, f"raw_{name}0")[...].reshape(96, 768)
            raw, padded = getattr(g, f"raw_{name}1"), g.base1
            for b in range(3):
                padded[36 * b:36 * b + 36] = raw[b].astype(F32)
            padded[108:] = jnp.zeros((4, 1024), F32)
            getattr(g, held + "1")[...] = padded[...].astype(BF16)
        entry.start()
        yield spent(0.3)
        for i in range(2):
            packed(1, i)
        for b in range(2):
            for i in range(2):
                v, a = views[b][i], SHAPES[b][i].inner
                v.offset[:, :a] = v.head_bias[0:1].astype(F32)
                v.offset[:, a:2 * a] = jnp.zeros((1, a), F32)
                v.offset[:, 2 * a:] = v.head_bias[1:2].astype(F32)
        g.vecs[...] = jnp.zeros_like(g.vecs)
        g.cols[...] = jnp.zeros_like(g.cols)
        place = lax.broadcasted_iota(jnp.int32, (432, 448), 0)
        token = row_of_part(lax.broadcasted_iota(jnp.int32, (1, 448), 1))
        g.to_rows[...] = (place == token).astype(F32).astype(BF16)
        place = lax.broadcasted_iota(jnp.int32, (448, 432), 1)
        token = row_of_part(lax.broadcasted_iota(jnp.int32, (448, 1), 0))
        g.to_parts[...] = (place == token).astype(F32).astype(BF16)
        yield spent(2.0)
        yield ("at", 8.0)
        entry.finish()
        for i in range(2):
            set_ids(getattr(g, f"ids_col{i}"), getattr(g, f"lengths_got{i}"), 0)
            set_ids(getattr(g, f"ids_row{i}"), getattr(g, f"lengths_got{i}"), 1)
        for i in range(2):
            base[i][...] = views[0][i].xf[me.own].astype(F32)
        yield spent(1.0)
        for i in range(2):
            plan.post("x", i)

    def begun(i, half):
        yield need("x", i)
        yield from stream(plan, i, half, views, base[i], (g.cot_got0, g.cot_got1)[i], (g.out0, g.out1)[i],
                          (g.grad0, g.grad1)[i])

    def closing():
        for i in range(2):
            for half in range(2):
                yield need("out", i, half)
        out_trade.start()

    def closing_grad(i):
        for half in range(2):
            yield need("grad", i, half)
        grad_trades[i].start()

    def vectors():
        for b in range(2):
            for i in range(2):
                yield need("cols", b, i)
        for i in range(2):
            for half in range(2):
                yield need("gb", 0, i, half)
        yield from total_steps(me, g.vecs, g.cols, g.vec_got, g.slots, g.small, g.vec_sum, g.cols_out, g.total_sems)

    tasks = []
    order = sorted((b, "qou".index(label), n, i) for (b, i), cuts in GATHERS.items()
                   for n, (_, _, _, _, label, _) in enumerate(cuts))
    for b, stage, n, i in order:
        tasks.append((RANKS[f"gather{b}{i}{n}"], gathers(plan, me, b, i, n, views[b][i], g)))
    tasks.append((0, opening()))
    for i in (1, 0):
        for half in range(2):
            tasks.append((RANKS[f"stream{i}{half}"], begun(i, half)))
    for b in range(2):
        for i in (1, 0):
            tasks.append((RANKS[f"attention{b}{i}"], attention(plan, b, i, views)))
            tasks.append((RANKS[f"back{b}{i}"], attention_back(plan, b, i, views)))
    tasks.append((RANKS["close"], closing()))
    for i in range(2):
        tasks.append((RANKS["close"], closing_grad(i)))
    tasks.append((RANKS["vectors"], vectors()))
    for i in range(2):
        for name in SUMS[i]:
            t = Bag()
            for part in ("halves", "chunks", "across", "small_chunks") + (("pieces",) if i == 0 else ()):
                setattr(t, part, getattr(g, f"{part}_{name}{i}"))
            outs = [{pack: getattr(g, f"sum_{pack}{b}{i}") for pack in "pu"} for b in range(2)]
            tasks.append((RANKS[f"sums{i}{name}"], sums_of(plan, me, name, i, views, outs, t, getattr(g, f"reduce_sems_{name}{i}"),
                                     getattr(g, f"credit_{name}{i}"))))
    for b in (1, 0):
        for i in (1, 0):
            tasks.append((RANKS[f"feed{b}{i}"], feed_grads(plan, b, i, views[b][i])))
            tasks.append((RANKS[f"head{b}{i}"], head_grads(plan, b, i, views[b][i])))
            tasks.append((RANKS[f"cols{b}{i}"], head_sums(plan, b, i, views[b][i])))
    plan.run(tasks)
    out_trade.finish()
    for trade in grad_trades:
        trade.finish()
    g.vecs_out[...] = g.vec_sum[...]
    for name in ("out0", "out1", "grad0", "grad1"):
        getattr(g, name + "_end")[...] = getattr(g, name + "_done")[...]


def call(kernel, inputs, outs, scratch, collective_id=None):
    names = list(inputs) + list(outs) + list(scratch)

    def body(*refs):
        bag = Bag()
        for name, ref in zip(names, refs):
            setattr(bag, name, ref)
        kernel(bag)
    vm = pl.BlockSpec(memory_space=pltpu.VMEM)
    results = pl.pallas_call(
        body, out_shape=list(outs.values()), in_specs=[vm] * len(inputs), out_specs=[vm] * len(outs),
        scratch_shapes=list(scratch.values()),
        compiler_params=pltpu.CompilerParams(collective_id=collective_id, has_side_effects=collective_id is not None,
                                             vmem_limit_bytes=LIMIT),
    )(*inputs.values())
    return dict(zip(outs, results))


def whole(inputs):
    outs, scratch = {}, {}
    for i in range(2):
        sh = SHAPES[0][i]
        slab = (sh.part, sh.width)
        scratch[f"cot_got{i}"] = VMEM(slab, BF16)
        scratch[f"lengths_got{i}"] = VMEM((3, 4), jnp.int32)
        for name in ("out", "grad"):
            scratch[f"{name}{i}"] = VMEM(slab, BF16)
            scratch[f"{name}{i}_done"] = VMEM(slab, BF16)
            outs[f"{name}{i}_end"] = jax.ShapeDtypeStruct(slab, BF16)
        scratch[f"base{i}"] = VMEM(slab, F32)
        scratch[f"normed{i}"] = VMEM(slab, F32)
        for name in ("gs", "gb", "part"):
            scratch[f"{name}{i}"] = VMEM((4,) + slab, BF16)
        scratch[f"gu{i}"] = VMEM((4, sh.part, sh.hidden), BF16)
        scratch[f"from_sib{i}"] = VMEM((2,) + slab, BF16)
        scratch[f"from_mate{i}"] = VMEM(slab, BF16)
        for half in range(2):
            scratch[f"wire_sems{i}{half}"] = DMA((2, 6))
        scratch[f"grad_sems{i}"] = DMA((2, 1))
        scratch[f"ids_col{i}"] = VMEM((3, sh.length, 1), F32)
        scratch[f"ids_row{i}"] = VMEM((3, 1, sh.length), F32)
        for pack in "pu":
            wide = sh.columns[pack]
            matrix = (768, wide) if i == 0 else (4, 2, 4, 32, wide)
            self_wide = SHAPES[1][i].columns[pack]
            scratch[f"dw{pack}{i}"] = VMEM(matrix[:-1] + (self_wide,), BF16)
            for b in range(2):
                scratch[f"w{pack}{b}{i}"] = VMEM(matrix, BF16)
                cols = SHAPES[b][i].columns[pack]
                if i == 0:
                    scratch[f"pieces_{pack}{b}"] = VMEM((4, 24, cols), BF16)
                outs[f"sum_{pack}{b}{i}"] = jax.ShapeDtypeStruct((24 if i == 0 else 32, cols), F32)
        for b in range(2):
            for n in range(len(GATHERS[b, i])):
                scratch[f"gather_sems{b}{i}{n}"] = DMA((2, 13))
        for name, (pack, first, ranges) in SUMS[i].items():
            wide = max(r[1] - r[0] for r in ranges if r is not None)
            scratch[f"reduce_sems_{name}{i}"] = DMA((2, 13))
            scratch[f"credit_{name}{i}"] = pltpu.SemaphoreType.REGULAR
            if i == 1:
                sizes = {"halves": (2, 2, 2, 32, wide), "chunks": (2,) + ((4, 2) if first else (2, 4)) + (32, wide), "across": (32, wide),
                         "small_chunks": (3, 2, 32, wide)}
            else:
                sizes = {"halves": (2, 96, wide), "chunks": (2, 96 if first else 192, wide),
                         "across": (4, 96, wide) if first else (96, wide),
                         "pieces": (4, 24, wide), "small_chunks": (3, 24, wide)}
            for part, size in sizes.items():
                scratch[f"{part}_{name}{i}"] = VMEM(size, BF16)
    scratch["gp_rows"] = VMEM((432, 768), BF16)
    scratch["gm1"] = VMEM((432, 256), BF16)
    scratch["gm_parts"] = VMEM((4, 112, 256), BF16)
    scratch["gp1"] = VMEM((4, 112, 768), BF16)
    for b in range(2):
        scratch[f"gm0{b}"] = VMEM((384, SHAPES[b][0].inner), BF16)
        scratch[f"gp0{b}"] = VMEM((4, 96, 3 * SHAPES[b][0].inner), BF16)
    scratch["to_rows"] = VMEM((432, 448), BF16)
    scratch["to_parts"] = VMEM((448, 432), BF16)
    scratch["entry_sems"] = DMA((2, 6))
    scratch["out_sems"] = DMA((2, 2))
    lanes_all, cols_wide = 2 * (768 + 1024), 768
    scratch["vecs"] = VMEM((8, lanes_all), F32)
    scratch["cols"] = VMEM((8, cols_wide), F32)
    scratch["vec_got"] = VMEM((3, 8, lanes_all // 4), F32)
    scratch["small"] = VMEM((8, lanes_all // 4 + cols_wide), F32)
    scratch["slots"] = VMEM((3, 4, 8, lanes_all // 4 + cols_wide), F32)
    scratch["vec_sum"] = VMEM((8, lanes_all), F32)
    scratch["total_sems"] = DMA((2, 13))
    outs["vecs_out"] = jax.ShapeDtypeStruct((8, lanes_all), F32)
    outs["cols_out"] = jax.ShapeDtypeStruct((8, cols_wide), F32)
    for b in range(2):
        for i in range(2):
            sh = SHAPES[b][i]
            slab = (sh.part, sh.width)
            for name, shape, kind in (
                    ("offset", (1, 3 * sh.inner), F32), ("xf", (4,) + slab, BF16), ("nf", (4,) + slab, BF16),
                    ("qkv", (3 * sh.length, 3 * sh.inner), BF16), ("mixed", (4, sh.part, sh.inner), BF16),
                    ("slope", (4, sh.part, sh.hidden), BF16), ("active", (4, sh.part, sh.hidden), BF16),
                    ("first", slab, F32), ("second", slab, F32)):
                scratch[f"{name}{b}{i}"] = VMEM(shape, kind)
    return call(whole_kernel, inputs, outs, scratch, 0)


def finish_kernel(g):
    for i, count in enumerate((32, 36)):
        for name in ("out", "grad"):
            src, dst = getattr(g, f"{name}{i}"), getattr(g, f"{name}{i}_end")
            if i == 0:
                dst[...] = src[...].reshape(dst.shape)
            else:
                value = src[...].astype(F32)
                for b in range(3):
                    dst[b] = value[b * count:(b + 1) * count].astype(dst.dtype)
    lane = 0
    for k, n in enumerate(f"{b}{i}" for b in range(2) for i in range(2)):
        sum_p, sum_u = getattr(g, "sum_p" + n), getattr(g, "sum_u" + n)
        proj, out, up, down = [getattr(g, p + n) for p in ("proj", "out", "up", "down")]
        a, f = proj.shape[2], up.shape[1]
        for c in range(3):
            proj[c] = sum_p[:, c * a:(c + 1) * a]
        out[...] = sum_p[:, 3 * a:4 * a]
        up[...] = sum_u[:, :f]
        down[...] = sum_u[:, f:2 * f]
        head_bias, up_bias, bias, gain = [getattr(g, p + n) for p in ("head_bias", "up_bias", "bias", "gain")]
        head_bias[0:1] = g.cols[2 * k:2 * k + 1, :a]
        head_bias[1:2] = g.cols[2 * k:2 * k + 1, 2 * a:3 * a]
        up_bias[...] = g.cols[2 * k + 1:2 * k + 2, :f]
        width = bias.shape[1]
        bias[...] = g.vecs[0:4, lane:lane + width]
        gain[...] = g.vecs[4:6, lane:lane + width]
        lane += width


def on_device(*args):
    text_in, image_in, text_lengths, image_lengths, text_cot, image_cot = args[:6]
    matrix_names = ("proj", "out", "up", "down")
    small_names = ("head_bias", "up_bias", "bias", "gain")

    inputs = {"raw_x0": text_in, "raw_x1": image_in, "raw_cot0": text_cot, "raw_cot1": image_cot,
              "lengths0": text_lengths, "lengths1": image_lengths}
    shapes = {}
    names = [f"{b}{i}" for b in range(2) for i in range(2)]
    for k, n in enumerate(names):
        for name, value in zip(matrix_names + small_names, args[6 + 8 * k:14 + 8 * k]):
            inputs[name + n] = value.transpose(1, 0, 2) if name == "proj" else value
            shapes[name + n] = jax.ShapeDtypeStruct(inputs[name + n].shape, F32)
    done = whole(inputs)
    ends, outs = {"vecs": done["vecs_out"], "cols": done["cols_out"]}, {}
    for name, like in (("out0", text_in), ("out1", image_in), ("grad0", text_in), ("grad1", image_in)):
        ends[name] = done[name + "_end"]
        outs[name + "_end"] = jax.ShapeDtypeStruct(like.shape, like.dtype)
    for n in names:
        ends["sum_p" + n] = done["sum_p" + n]
        ends["sum_u" + n] = done["sum_u" + n]
        for p in matrix_names + small_names:
            outs[p + n] = shapes[p + n]
    return tuple(value.transpose(1, 0, 2) if name.startswith("proj") else value
                 for name, value in call(finish_kernel, ends, outs, {}).items())


def solution(mesh):
    kinds = [P("rows", None, "seq"), P("rows", "seq"), P("rows", "seq"), P("rows", "seq"), P(None, "seq"),
             P(None, "seq"), P(), P()] * 4
    position = P("rows", "seq", None)
    return jax.shard_map(
        on_device, mesh=mesh,
        in_specs=tuple([position, position, P("rows", None), P("rows", None), position, position] + kinds),
        out_specs=tuple([position] * 4 + kinds), check_vma=False)
```

```python
import jax
import jax.numpy as jnp
from jax import lax
from jax.experimental import pallas as pl
from jax.experimental.pallas import tpu as pltpu
from jax.sharding import PartitionSpec as P

MESH = pl.DeviceIdType.MESH
VMEM = pltpu.VMEM
DMA = pltpu.SemaphoreType.DMA
F32, BF16 = jnp.float32, jnp.bfloat16
NN, NT, TN = ((1,), (0,)), ((1,), (1,)), ((0,), (0,))
EPS = 1e-05
MASKED = -1000000000.0
LIMIT = 63 * 1024 * 1024


class Bag:
    pass


RATE = {"x+": 48e3, "x-": 48e3, "y+": 48e3, "y-": 48e3, "z": 48e3, "over": 48e3, "beside": 600e3}
DELAY = {"beside": 1.1}


class Plan:
    def __init__(self):
        self.now = 0.0
        self.free = {}
        self.done = set()

    def post(self, *event):
        self.done.add(event)

    def arrival(self, link, size):
        self.now += 0.06
        begin = max(self.now, self.free.get(link, 0.0))
        self.free[link] = begin + size / RATE[link]
        return self.free[link] + DELAY.get(link, 3.6)

    def run(self, tasks):
        waiting = [[rank, n, task, ("at", 0.0)] for n, (rank, task) in enumerate(tasks)]
        while waiting:
            best = None
            for entry in waiting:
                kind, what = entry[3][:2]
                rank = entry[3][2] if len(entry[3]) > 2 else entry[0]
                if kind == "event":
                    if what not in self.done:
                        continue
                    due = self.now
                else:
                    due = max(what, self.now)
                key = (due, rank, entry[1])
                if best is None or key < best[0]:
                    best = (key, entry)
            assert best is not None, "stuck"
            entry = best[1]
            self.now = best[0][0]
            try:
                need = next(entry[2])
            except StopIteration:
                waiting.remove(entry)
                continue
            if need[0] == "for":
                self.now += need[1]
                need = ("at", self.now)
            entry[3] = need


class Place:
    def __init__(self, plan):
        r = lax.axis_index("rows")
        s = lax.axis_index("seq")
        self.plan = plan
        self.r, self.s = r, s
        self.x, self.z, self.y = r // 8, (r // 4) % 2, r % 4
        self.zh, self.c = s // 2, s % 2
        self.own = s
        self.sib_slab = self.zh * 2 + 1 - self.c
        self.mate_slab = (1 - self.zh) * 2 + self.c
        self.far_slab = (1 - self.zh) * 2 + 1 - self.c
        self.sib = (r, self.sib_slab)
        across = (self.x * 2 + 1 - self.z) * 4 + self.y
        self.mate = (across, self.mate_slab)
        self.far = (across, self.far_slab)

    def along(self, axis, step):
        x, z, y = self.x, self.z, self.y
        if axis == "x":
            x = (x + step) % 4
        elif axis == "y":
            y = (y + step) % 4
        else:
            z = 1 - z
        return ((x * 2 + z) * 4 + y, self.s)

    def push(self, src, dst, sems, k, device, link):
        copy = pltpu.make_async_remote_copy(
            src_ref=src, dst_ref=dst, send_sem=sems.at[0, k], recv_sem=sems.at[1, k],
            device_id=device, device_id_type=MESH)
        copy.start()
        size = src.dtype.itemsize
        for n in src.shape:
            size *= n
        copy.due = self.plan.arrival(link, size)
        return copy


def at(copy, *more):
    return ("at", max(c.due for c in (copy,) + more))


def need(*event):
    return ("event", event)


def part_spent(cost):
    return spent(cost * 0.67 + 0.08)


def spent(cost):
    return ("for", 0.72 * cost)


class Trade:
    def __init__(self, me, pairs, sems):
        self.me, self.pairs, self.sems = me, pairs, sems

    def copies(self):
        return [pltpu.make_async_remote_copy(
            src_ref=src, dst_ref=dst, send_sem=self.sems.at[0, k], recv_sem=self.sems.at[1, k],
            device_id=self.me.along("z", 1), device_id_type=MESH) for k, (src, dst) in enumerate(self.pairs)]

    def start(self):
        @pl.when(self.me.zh == 1)
        def _():
            for copy in self.copies():
                copy.start()

        @pl.when(self.me.zh == 0)
        def _():
            for src, dst in self.pairs:
                dst[...] = src[...]

    def finish(self):
        @pl.when(self.me.zh == 1)
        def _():
            for copy in self.copies():
                copy.wait()


def dot(a, b, dims):
    return lax.dot_general(a, b, (dims, ((), ())), preferred_element_type=F32)


def loop(count, body):
    for i in range(count):
        body(i)


def lanes(i, size=256, base=0):
    return slice(base + i * size, base + (i + 1) * size)


def span(start, size):
    return pl.ds(pl.multiple_of(start, 16), size)


def add_rows(dst, start, src, first, count):
    def one(i):
        to, come = span(start + 16 * i, 16), span(first + 16 * i, 16)
        total = dst[to].astype(F32)
        for ref in src:
            total = total + ref[come].astype(F32)
        dst[to] = total.astype(dst.dtype)
    loop(count // 16, one)


def add_slabs(dst, src, count):
    def one(i):
        to = dst(i)
        total = to[...].astype(F32)
        for ref in src(i):
            total = total + ref[...].astype(F32)
        to[...] = total.astype(to.dtype)
    loop(count, one)


def middle_of(columns):
    return columns // 256 * 128


def gather_text(me, pieces, w, sems, started, ready, z_first):
    columns = w.shape[1]
    cut = middle_of(columns)
    x, z, y = me.x, me.z, me.y
    copies = [me.push(pieces.at[y], pieces.at[y], sems, n, me.along("y", n + 1), link)
              for n, link in enumerate(("y+", "y+", "y-"))]
    yield at(*copies)
    for copy in copies:
        copy.wait_recv()
    base = (x * 2 + z) * 96
    w[span(base, 96)] = pieces[...].astype(F32).reshape(96, columns).astype(BF16)
    yield spent(0.2)
    right, left = me.along("x", 1), me.along("x", 3)
    block = w.at[span(base, 96)]
    if z_first:
        e = me.push(block, block, sems, 4, me.along("z", 1), "z")
        yield at(e)
        e.wait_recv()
        block = w.at[span(192 * x, 192)]
    f = me.push(block, block, sems, 5, right, "x+")
    g = me.push(block, block, sems, 6, left, "x-")
    if z_first:
        me.plan.post(*started)
    yield at(f)
    f.wait_recv()
    place = 192 * ((x + 3) % 4)
    block = w.at[span(place, 96)] if z_first else w.at[span(place + 96 * z, 96), :cut]
    h = me.push(block, block, sems, 7, right, "x+")
    yield at(g)
    g.wait_recv()
    place = 192 * ((x + 1) % 4)
    block = w.at[span(place + 96, 96)] if z_first else w.at[span(place + 96 * z, 96), cut:]
    i = me.push(block, block, sems, 8, left, "x-")
    copies += [f, g, h, i]
    if z_first:
        copies.append(e)
    else:
        me.plan.post(*started)
        over = []
        for n, step in enumerate((0, 3, 1)):
            block = w.at[span(192 * ((x + step) % 4) + 96 * z, 96)]
            over.append(me.push(block, block, sems, 9 + n, me.along("z", 1), "z"))
        yield at(h, i)
    if z_first:
        yield at(h, i)
    h.wait_recv()
    i.wait_recv()
    if not z_first:
        block = w.at[span(192 * ((x + 2) % 4) + 96 * z, 96)]
        over.append(me.push(block, block, sems, 12, me.along("z", 1), "z"))
        yield at(*over)
        for copy in over:
            copy.wait_recv()
        copies += over
    me.plan.post(*ready)
    for copy in copies:
        copy.wait_send()


def image_views(me, w, light):
    x, z, y = me.x, me.z, me.y
    if light == "x":
        return (lambda n: w.at[(x + n) % 4, :, y], lambda n, h: w.at[(x + n) % 4, h, y],
                lambda n: w.at[:, :, (y + n) % 4], lambda n, h: w.at[2 * h:2 * h + 2, :, (y + n) % 4])
    return (lambda n: w.at[x, :, (y + n) % 4], lambda n, h: w.at[x, h, (y + n) % 4],
            lambda n: w.at[(x + n) % 4], lambda n, h: w.at[(x + n) % 4, :, 2 * h:2 * h + 2])


def gather_image(me, w, sems, started, ready, light):
    x, z, y = me.x, me.z, me.y
    heavy = "y" if light == "x" else "x"
    few, few_half, many, many_half = image_views(me, w, light)
    copies = [me.push(w.at[x, z, y], w.at[x, z, y], sems, 0, me.along("z", 1), "z")]
    yield at(copies[0])
    copies[0].wait_recv()
    lights = [me.push(few(0), few(0), sems, n, me.along(light, n), light + "++-"[n - 1]) for n in (1, 2, 3)]
    yield at(*lights)
    for copy in lights:
        copy.wait_recv()
    copies += lights
    right, left = me.along(heavy, 1), me.along(heavy, 3)
    a = me.push(many(0), many(0), sems, 5, right, heavy + "+")
    b = me.push(many(0), many(0), sems, 6, left, heavy + "-")
    me.plan.post(*started)
    yield at(a)
    a.wait_recv()
    c = me.push(many_half(3, 0), many_half(3, 0), sems, 7, right, heavy + "+")
    yield at(b)
    b.wait_recv()
    d = me.push(many_half(1, 1), many_half(1, 1), sems, 8, left, heavy + "-")
    yield at(c, d)
    c.wait_recv()
    d.wait_recv()
    copies += [a, b, c, d]
    me.plan.post(*ready)
    for copy in copies:
        copy.wait_send()


def reduce_text(me, dw, out, t, sems, z_first):
    columns = dw.shape[1]
    cut = middle_of(columns)
    cost = columns / 2000.0
    x, z, y = me.x, me.z, me.y
    right, left = me.along("x", 1), me.along("x", 3)
    copies = []
    if z_first:
        def mine(step):
            return 192 * ((x + step) % 4) + 96 * z
        over = []
        for n, step in enumerate((2, 1, 3, 0)):
            place = (x + step) % 4
            over.append(me.push(dw.at[span(192 * place + 96 * (1 - z), 96)], t.across.at[place], sems, 9 + n,
                                me.along("z", 1), "z"))
        yield at(over[0])
        over[0].wait_recv()
        add_rows(dw, mine(2), [t.across.at[(x + 2) % 4]], 0, 96)
        a = me.push(dw.at[span(mine(2), 96), :cut], t.halves.at[0, :, :cut], sems, 0, right, "x+")
        b = me.push(dw.at[span(mine(2), 96), cut:], t.halves.at[1, :, cut:], sems, 1, left, "x-")
        yield spent(0.4 * cost)
        yield at(a, over[1])
        over[1].wait_recv()
        add_rows(dw, mine(1), [t.across.at[(x + 1) % 4]], 0, 96)
        a.wait_recv()
        add_rows(dw.at[:, :cut], mine(1), [t.halves.at[0, :, :cut]], 0, 96)
        c = me.push(dw.at[span(mine(1), 96)], t.chunks.at[0], sems, 2, right, "x+")
        yield spent(0.6 * cost)
        yield at(b, over[2])
        over[2].wait_recv()
        add_rows(dw, mine(3), [t.across.at[(x + 3) % 4]], 0, 96)
        b.wait_recv()
        add_rows(dw.at[:, cut:], mine(3), [t.halves.at[1, :, cut:]], 0, 96)
        d = me.push(dw.at[span(mine(3), 96)], t.chunks.at[1], sems, 3, left, "x-")
        yield spent(0.6 * cost)
        yield at(c, d, over[3])
        over[3].wait_recv()
        c.wait_recv()
        d.wait_recv()
        total = (dw[span(mine(0), 96)].astype(F32) + t.across[x].astype(F32) + t.chunks[0].astype(F32)
                 + t.chunks[1].astype(F32))
        copies += over
    else:
        far = 192 * ((x + 2) % 4)
        a = me.push(dw.at[span(far, 96)], t.halves.at[0], sems, 0, right, "x+")
        b = me.push(dw.at[span(far + 96, 96)], t.halves.at[1], sems, 1, left, "x-")
        yield at(a)
        a.wait_recv()
        first = 192 * ((x + 1) % 4)
        add_rows(dw, first, [t.halves.at[0]], 0, 96)
        c = me.push(dw.at[span(first, 192)], t.chunks.at[0], sems, 2, right, "x+")
        yield spent(0.4 * cost)
        yield at(b)
        b.wait_recv()
        first = 192 * ((x + 3) % 4)
        add_rows(dw, first + 96, [t.halves.at[1]], 0, 96)
        d = me.push(dw.at[span(first, 192)], t.chunks.at[1], sems, 3, left, "x-")
        yield spent(0.4 * cost)
        yield at(c, d)
        c.wait_recv()
        d.wait_recv()
        add_rows(dw, 192 * x + 96 * (1 - z), [t.chunks.at[0], t.chunks.at[1]], 96 * (1 - z), 96)
        e = me.push(dw.at[span(192 * x + 96 * (1 - z), 96)], t.across, sems, 4, me.along("z", 1), "z")
        add_rows(dw, 192 * x + 96 * z, [t.chunks.at[0], t.chunks.at[1]], 96 * z, 96)
        yield spent(1.0 * cost)
        yield at(e)
        e.wait_recv()
        total = dw[span(192 * x + 96 * z, 96)].astype(F32) + t.across[...].astype(F32)
        copies.append(e)
    t.pieces[...] = total.reshape(4, 24, columns).astype(BF16)
    yield spent(0.4 * cost)
    pieces = t.pieces
    last = [me.push(pieces.at[(y + n + 1) % 4], t.small_chunks.at[n], sems, 5 + n, me.along("y", n + 1), link)
            for n, link in enumerate(("y+", "y+", "y-"))]
    yield at(*last)
    for copy in last:
        copy.wait_recv()
    total = pieces[y].astype(F32) + t.small_chunks[0].astype(F32)
    out[...] = total + t.small_chunks[1].astype(F32) + t.small_chunks[2].astype(F32)
    copies += [a, b, c, d] + last
    for copy in copies:
        copy.wait_send()
    yield spent(0.2 * cost)


def add_block(dst, src):
    lead = [()]
    for n in dst.shape[:-2]:
        lead = [at_ + (k,) for at_ in lead for k in range(n)]
    for place in lead:
        total = dst[place].astype(F32)
        for ref in src:
            total = total + ref[place].astype(F32)
        dst[place] = total.astype(dst.dtype)


def reduce_image(me, dw, out, t, sems, light):
    cost = dw.shape[4] / 1500.0
    x, z, y = me.x, me.z, me.y
    heavy = "y" if light == "x" else "x"
    few, few_half, many, many_half = image_views(me, dw, light)
    copies = []
    right, left = me.along(heavy, 1), me.along(heavy, 3)
    a = me.push(many_half(2, 0), t.halves.at[0], sems, 0, right, heavy + "+")
    b = me.push(many_half(2, 1), t.halves.at[1], sems, 1, left, heavy + "-")
    yield at(a)
    a.wait_recv()
    add_block(many_half(1, 0), [t.halves.at[0]])
    c = me.push(many(1), t.chunks.at[0], sems, 2, right, heavy + "+")
    yield spent(0.4 * cost)
    yield at(b)
    b.wait_recv()
    add_block(many_half(3, 1), [t.halves.at[1]])
    d = me.push(many(3), t.chunks.at[1], sems, 3, left, heavy + "-")
    yield spent(0.4 * cost)
    yield at(c, d)
    c.wait_recv()
    d.wait_recv()
    add_block(many(0), [t.chunks.at[0], t.chunks.at[1]])
    lights = [me.push(few(n), t.small_chunks.at[n - 1], sems, 3 + n, me.along(light, n), light + "++-"[n - 1])
              for n in (2, 1, 3)]
    yield spent(1.2 * cost)
    yield at(*lights)
    for copy in lights:
        copy.wait_recv()
    add_block(few(0), [t.small_chunks.at[n] for n in range(3)])
    copies += [a, b, c, d] + lights
    yield spent(0.4 * cost)
    i = me.push(dw.at[x, 1 - z, y], t.across, sems, 8, me.along("z", 1), "z")
    yield at(i)
    i.wait_recv()
    out[...] = dw[x, z, y].astype(F32) + t.across[...].astype(F32)
    for copy in copies + [i]:
        copy.wait_send()
    yield spent(0.2 * cost)


def total_steps(me, vecs, cols, got, slots, small, vec_out, col_out, sems):
    wide = vecs.shape[1] // 4

    def quarter(k):
        return pl.ds(pl.multiple_of(k * wide, 128), wide)
    mates = ((me.sib, me.sib_slab, "beside"), (me.mate, me.mate_slab, "over"), (me.far, me.far_slab, "over"))
    sent = [me.push(vecs.at[:, quarter(slab)], got.at[k], sems, k, device, link)
            for k, (device, slab, link) in enumerate(mates)]
    yield at(*sent)
    for copy in sent:
        copy.wait_recv()
    small[:, :wide] = vecs[:, quarter(me.own)] + got[0] + got[1] + got[2]
    small[:, wide:] = cols[...]
    k = 3
    for stage, (axis, place, count) in enumerate((("x", me.x, 4), ("y", me.y, 4), ("z", me.z, 2))):
        slots[stage, place] = small[...]
        copies = [me.push(slots.at[stage, place], slots.at[stage, place], sems, k + n, me.along(axis, n + 1),
                          axis + "++-"[n] if count == 4 else "z") for n in range(count - 1)]
        k += count - 1
        yield at(*copies)
        for copy in copies:
            copy.wait_recv()
        total = slots[stage, 0] + slots[stage, 1]
        if count == 4:
            total = total + slots[stage, 2] + slots[stage, 3]
        small[...] = total
        sent += copies
    col_out[...] = small[:, wide:]
    vec_out[:, quarter(me.own)] = small[:, :wide]
    mine = vec_out.at[:, quarter(me.own)]
    last = [me.push(mine, mine, sems, k + n, device, link) for n, (device, slab, link) in enumerate(mates)]
    yield at(*last)
    for copy in last:
        copy.wait_recv()
    for copy in sent + last:
        copy.wait_send()


class Wire:
    def __init__(self, me, part, from_sib, from_mate, sems, start, size):
        self.me, self.part, self.from_sib, self.from_mate, self.sems = me, part, from_sib, from_mate, sems
        self.start, self.size = start, size
        self.rows = pl.ds(start, size)
        self.steps = [pl.ds(start + 16 * i, 16) for i in range(size // 16)]

    def gather(self, buf):
        me, rows = self.me, self.rows
        mine, theirs = buf.at[me.own, rows], buf.at[me.mate_slab, rows]
        over = me.push(mine, mine, self.sems, 0, me.mate, "over")
        beside = me.push(mine, mine, self.sems, 1, me.sib, "beside")
        yield at(over) + (-1,)
        over.wait_recv()
        on = me.push(theirs, theirs, self.sems, 2, me.sib, "beside")
        yield at(beside, on)
        beside.wait_recv()
        on.wait_recv()
        for copy in (over, beside, on):
            copy.wait_send()

    def reduce(self):
        me, part, from_sib, rows = self.me, self.part, self.from_sib, self.rows
        a = me.push(part.at[me.far_slab, rows], from_sib.at[0, rows], self.sems, 3, me.sib, "beside")
        b = me.push(part.at[me.sib_slab, rows], from_sib.at[1, rows], self.sems, 4, me.sib, "beside")
        yield at(a) + (-1,)
        a.wait_recv()
        for step in self.steps:
            part[me.mate_slab, step] = (
                part[me.mate_slab, step].astype(F32) + from_sib[0, step].astype(F32)).astype(BF16)
        d = me.push(part.at[me.mate_slab, rows], self.from_mate.at[rows], self.sems, 5, me.mate, "over")
        yield spent(0.2)
        yield at(b, d)
        b.wait_recv()
        d.wait_recv()
        for copy in (a, b, d):
            copy.wait_send()

    def total(self, rows):
        return (self.part[self.me.own, rows].astype(F32) + self.from_sib[1, rows].astype(F32)
                + self.from_mate[rows].astype(F32))


class Shape:
    def __init__(self, stream, part, length, width, inner, hidden, head):
        self.stream, self.part, self.length, self.width = stream, part, length, width
        self.inner, self.hidden, self.head = inner, hidden, head
        self.tokens = 4 * part
        self.out_at = 3 * inner
        self.columns = {"p": 4 * inner, "u": 2 * hidden}
        self.thirds = ((0, 32), (32, 32), (64, 32)) if stream == 0 else ((0, 48), (48, 32), (80, 32))


SHAPES = ((Shape(0, 96, 128, 768, 256, 768, 128), Shape(1, 112, 144, 1024, 256, 256, 128)),
          (Shape(0, 96, 128, 768, 192, 768, 64), Shape(1, 112, 144, 1024, 256, 256, 128)))

GATHERS = {
    (0, 0): (
        ("p", 0, 384, False, "q", 3),
        ("p", 384, 768, False, "q", 0),
        ("p", 768, 1024, True, "o", 12),
        ("u", 0, 768, False, "u", 13),
        ("u", 768, 1536, True, "u", 23),
    ),
    (0, 1): (
        ("p", 0, 384, True, "q", 0),
        ("p", 384, 768, False, "q", 0),
        ("p", 768, 1024, True, "o", 6),
        ("u", 0, 512, True, "u", 12),
    ),
    (1, 0): (
        ("p", 0, 384, True, "q", 33),
        ("p", 384, 768, False, "q", 20),
        ("u", 0, 768, False, "u", 55),
        ("u", 768, 1536, True, "u", 60),
    ),
    (1, 1): (
        ("p", 0, 1024, True, "q", 23),
        ("u", 0, 512, True, "u", 46),
    ),
}
SUMS = (
    {
        "ua": ("u", True, ((0, 768), (0, 768))),
        "ub": ("u", False, ((768, 1536), (768, 1536))),
        "pa": ("p", True, ((0, 384), (0, 384))),
        "pb": ("p", True, ((384, 768), (384, 768))),
        "o": ("p", True, ((768, 1024), None)),
    },
    {
        "u": ("u", False, ((0, 512), (0, 512))),
        "qa": ("p", False, ((0, 384), (0, 384))),
        "qb": ("p", True, ((384, 768), (384, 768))),
        "o": ("p", True, ((768, 1024), (768, 1024))),
    },
)
RANKS = {
    "gather000": 0.3, "gather001": 0, "gather002": 1.5, "gather003": 1.3, "gather004": 2.5, "gather010": 0.7,
    "gather011": 0.7, "gather012": 0.7, "gather013": 3, "gather100": 0, "gather101": 0, "gather102": 0,
    "gather103": 4, "gather110": 1.1, "gather111": 3, "stream02": 0.5, "stream12": 0.7, "stream00": 0.9,
    "stream01": 2.5, "stream10": 3, "stream11": 1.3, "attention00": 2.5, "back00": 1, "feed00": 4, "head00": 2,
    "cols00": 1.3, "attention01": 1.1, "back01": 0.5, "feed01": 4, "head01": 1.1, "cols01": 1.1, "attention10":
    1, "back10": 4, "feed10": 1, "head10": 2.5, "cols10": 3, "attention11": 3, "back11": 1.3, "feed11": 4,
    "head11": 1.3, "cols11": 4, "sums0ua": 0.7, "sums0ub": 0.9, "sums0pa": 0, "sums0pb": 1.5, "sums0o": 0.9,
    "sums1u": 2, "sums1qa": 3, "sums1qb": 0.7, "sums1o": 4, "close": 1.1, "vectors": 0.5}


def columns_of(sh, w, cols):
    if sh.stream == 0:
        return w[:, cols]
    return w[:, :, :, :, cols].reshape(sh.width, -1)


def rows_of(sh, w, i, cols):
    if sh.stream == 0:
        return w[lanes(i), cols]
    value = w[i, :, :, :, cols]
    return value.reshape(256, value.shape[-1])


def set_rows(sh, w, i, cols, value):
    if sh.stream == 0:
        w[lanes(i), cols] = value
    else:
        w[i, :, :, :, cols] = value.reshape(2, 4, 32, value.shape[-1])


def normal(value):
    centre = jnp.mean(value, axis=-1, keepdims=True)
    moved = value - centre
    scale = lax.rsqrt(jnp.mean(moved * moved, axis=-1, keepdims=True) + EPS)
    return moved * scale, scale


def flat(ref):
    value = ref[...]
    return value.reshape(value.shape[0] * value.shape[1], value.shape[2])


def part_of(ref, rows):
    value = ref[:, rows]
    return value.reshape(value.shape[0] * value.shape[1], value.shape[2])


def put_by_row(ref, third, cols, value):
    ref[128 * third:128 * third + 128, cols] = value


def put_by_part(ref, b, cols, value):
    for p in range(4):
        ref[p, 32 * b:32 * b + 32, cols] = value[32 * p:32 * p + 32]


def project(sh, v, third):
    whole = part_of(v.xf, v.wires[third].rows)

    def put(cols, value):
        if sh.stream == 0:
            put_by_row(v.qkv, third, cols, value)
        else:
            v.gp[:, v.wires[third].rows, cols] = value.reshape(4, v.wires[third].size, -1)
    if sh.inner % 256:
        cols = slice(0, 3 * sh.inner)
        put(cols, (dot(whole, columns_of(sh, v.wp, cols), NN) + v.offset[...]).astype(BF16))
    else:
        def one(i):
            cols = lanes(i)
            put(cols, (dot(whole, columns_of(sh, v.wp, cols), NN) + v.offset[:, cols]).astype(BF16))
        loop(3 * sh.inner // 256, one)


def probabilities(query, key, col_ids, row_ids, scale):
    raw = dot(query, key, NT)
    scores = jnp.where(col_ids == row_ids, raw * scale, MASKED)
    grown = jnp.exp(scores - jnp.max(scores, axis=-1, keepdims=True))
    return grown * (1.0 / jnp.sum(grown, axis=-1, keepdims=True))


def attend(sh, v, kv, key_length):
    h, a = sh.head, sh.inner
    for b in range(3):
        mine = pl.ds(b * sh.length, sh.length)
        theirs = pl.ds(b * key_length, key_length)
        for n in range(a // h):
            q_at, k_at, v_at = [slice(c * a + n * h, c * a + (n + 1) * h) for c in range(3)]
            p = probabilities(v.qkv[mine, q_at], kv.qkv[theirs, k_at], v.ids_col[b], kv.ids_row[b], h ** -0.5)
            result = dot(p.astype(BF16), kv.qkv[theirs, v_at], NN).astype(BF16)
            if sh.stream == 0:
                put_by_part(v.mixed, b, q_at, result)
            else:
                v.mixed_rows[mine, q_at] = result
        yield spent(0.6)
    if sh.stream == 1:
        v.mixed[...] = dot(v.to_parts[...], v.mixed_rows[...], NN).astype(BF16).reshape(4, sh.part, a)
        yield spent(0.3)


def spread_out(sh, v, third, left, w, cols):
    wire = v.wires[third]
    value = part_of(left, wire.rows)

    def one(i):
        result = dot(value, rows_of(sh, w, i, cols), NT)
        wire.part[:, wire.rows, lanes(i)] = result.reshape(4, wire.size, 256).astype(BF16)
    loop(sh.width // 256, one)


def norm_forward(sh, v, third, base, sums, which, result, low):
    bias = v.bias[which:which + 1].astype(F32)
    shift = v.bias[2 + which:3 + which].astype(F32)
    gain = v.gain[which:which + 1].astype(F32)
    for rows in v.wires[third].steps:
        value = base[rows] + v.wires[third].total(rows) + bias
        sums[rows] = value
        value = normal(value)[0] * gain + shift
        result[rows] = value
        low[rows] = value.astype(BF16)


def feed(sh, v, third):
    wire = v.wires[third]
    whole = part_of(v.nf, wire.rows)
    k = (2.0 / jnp.pi) ** 0.5

    def one(i):
        cols = lanes(i)
        u = dot(whole, columns_of(sh, v.wu, cols), NN) + v.up_bias[:, cols].astype(F32)
        square = u * u
        t = jnp.tanh(k * u * (1.0 + 0.044715 * square))
        half_sum = 0.5 * (1.0 + t)
        slope = half_sum + 0.5 * u * (1.0 - t * t) * (k * (1.0 + 3 * 0.044715 * square))
        v.active[:, wire.rows, cols] = (u * half_sum).astype(BF16).reshape(4, wire.size, 256)
        v.slope[:, wire.rows, cols] = slope.astype(BF16).reshape(4, wire.size, 256)
    loop(sh.hidden // 256, one)


def norm_backward(sh, v, third, grad, sums, which, result, low, bias_row):
    gain = v.gain[which:which + 1].astype(F32)

    def fold(value):
        return value[:8] + value[8:]
    totals = None
    for rows in v.wires[third].steps:
        g = grad(rows)
        n, scale = normal(sums[rows])
        gn = g * gain
        out = scale * (gn - jnp.mean(gn, axis=-1, keepdims=True) - n * jnp.mean(gn * n, axis=-1, keepdims=True))
        rounded = out.astype(BF16)
        result[rows] = out
        low[rows] = rounded
        terms = (fold(rounded.astype(F32)), fold(g), fold(g * n))
        totals = terms if totals is None else tuple(x + y for x, y in zip(totals, terms))
    for at_row, total in zip((bias_row, 2 + which, 4 + which), totals):
        v.vec[at_row:at_row + 1] += jnp.sum(total, axis=0, keepdims=True)


def weight_grad(sh, left, right, dw, start):
    cols = slice(start, start + right.shape[2])

    def one(i):
        piece = left[:, :, lanes(i)].reshape(sh.tokens, 256)
        set_rows(sh, dw, i, cols, dot(piece, flat(right), TN).astype(BF16))
    loop(sh.width // 256, one)


def feed_back(sh, v, third):
    wire = v.wires[third]
    whole = part_of(v.gs, wire.rows)

    def one(i):
        cols = lanes(i)
        grad = dot(whole, columns_of(sh, v.wu, lanes(i, 256, sh.hidden)), NN)
        gu = (grad * v.slope[:, wire.rows, cols].reshape(4 * wire.size, 256).astype(F32)).astype(BF16)
        v.gu[:, wire.rows, cols] = gu.reshape(4, wire.size, 256)
        v.col_up[:, cols] += jnp.sum(gu.astype(F32), axis=0, keepdims=True)
    loop(sh.hidden // 256, one)


def mix_back(sh, v, third):
    wire = v.wires[third]
    cols = slice(sh.out_at, sh.out_at + sh.inner)
    value = dot(part_of(v.gb, wire.rows), columns_of(sh, v.wp, cols), NN).astype(BF16)
    if sh.stream == 0:
        put_by_row(v.gm, third, slice(0, sh.inner), value)
    else:
        v.gm_parts[:, wire.rows] = value.reshape(4, wire.size, sh.inner)


def attend_back(sh, v, key_sh, kv):
    h, a = sh.head, sh.inner
    scale = h ** -0.5

    def put(to_sh, to, b, cols, value):
        value = value.astype(BF16)
        if to_sh.stream == 0:
            put_by_part(to.gp, b, cols, value)
        else:
            to.gp_rows[pl.ds(b * to_sh.length, to_sh.length), cols] = value
    if sh.stream == 1:
        v.gm[...] = dot(v.to_rows[...], flat(v.gm_parts), NN).astype(BF16)
    for b in range(3):
        mine = pl.ds(b * sh.length, sh.length)
        theirs = pl.ds(b * key_sh.length, key_sh.length)
        for n in range(a // h):
            q_at, k_at, v_at = [slice(c * a + n * h, c * a + (n + 1) * h) for c in range(3)]
            query, key, value = v.qkv[mine, q_at], kv.qkv[theirs, k_at], kv.qkv[theirs, v_at]
            grad = v.gm[mine, q_at]
            p = probabilities(query, key, v.ids_col[b], kv.ids_row[b], scale)
            gp = dot(grad, value, NT)
            gs = (p * (gp - jnp.sum(gp * p, axis=-1, keepdims=True)) * scale).astype(BF16)
            put(sh, v, b, q_at, dot(gs, key, NN))
            put(key_sh, kv, b, k_at, dot(gs, query, TN))
            put(key_sh, kv, b, v_at, dot(p.astype(BF16), grad, TN))
        yield spent(1.3)


def set_ids(ref, lengths, axis):
    shape = ref.shape[1:]
    position = lax.broadcasted_iota(jnp.int32, shape, axis)
    for b in range(3):
        bound = jnp.zeros((1, 1), jnp.int32)
        seg = jnp.zeros(shape, jnp.int32)
        for j in range(4):
            bound = bound + lengths[b:b + 1, j:j + 1]
            seg = seg + (position >= bound).astype(jnp.int32)
        ref[b] = seg.astype(F32)


def row_of_part(token):
    def over(value, size, most):
        return sum((value >= k * size).astype(jnp.int32) for k in range(1, most))
    p = over(token, 112, 4)
    within = token - 112 * p
    row = over(within, 36, 4)
    return jnp.where(row < 3, 144 * row + 36 * p + within - 36 * row, -1)


def stream(plan, i, third, views, base, cot, outs, grads):
    big = i == 0
    for b in range(2):
        sh, v = SHAPES[b][i], views[b][i]
        wire = v.wires[third]
        own = wire.me.own
        yield from wire.gather(v.xf)
        yield need("wq", b, i)
        project(sh, v, third)
        yield part_spent(0.6)
        plan.post("qkv", b, i, third)
        yield need("mixed", b, i)
        yield need("wo", b, i)
        spread_out(sh, v, third, v.mixed, v.wp, slice(sh.out_at, sh.out_at + sh.inner))
        yield part_spent(0.4)
        yield from wire.reduce()
        norm_forward(sh, v, third, base, v.first, 0, v.normed, v.nf.at[own])
        yield part_spent(0.4)
        yield from wire.gather(v.nf)
        yield need("wu", b, i)
        feed(sh, v, third)
        yield part_spent(1.1 if big else 0.6)
        spread_out(sh, v, third, v.active, v.wu, slice(sh.hidden, 2 * sh.hidden))
        yield part_spent(0.7 if big else 0.4)
        yield from wire.reduce()
        norm_forward(sh, v, third, v.normed, v.second, 1, base, views[1][i].xf.at[own] if b == 0 else outs)
        yield part_spent(0.4)
    plan.post("out", i, third)
    for b in (1, 0):
        sh, v = SHAPES[b][i], views[b][i]
        wire = v.wires[third]
        own = wire.me.own
        norm_backward(sh, v, third, (lambda rows: cot[rows].astype(F32)) if b == 1 else (lambda rows: base[rows]),
                      v.second, 1, v.normed, v.gs.at[own], 1)
        yield part_spent(0.6)
        yield from wire.gather(v.gs)
        plan.post("gs", b, i, third)
        if b == 0:
            yield need("dwu", 1, i)
        feed_back(sh, v, third)
        yield part_spent(0.9 if big else 0.5)
        plan.post("gu", b, i, third)
        if b == 0:
            yield need("dwo", 1, i)
        spread_out(sh, v, third, v.gu, v.wu, slice(0, sh.hidden))
        yield part_spent(0.7 if big else 0.4)
        yield from wire.reduce()
        norm_backward(sh, v, third, lambda rows, v=v: v.normed[rows] + v.wires[third].total(rows), v.first, 0, v.normed,
                      v.gb.at[own], 0)
        yield part_spent(0.6)
        yield from wire.gather(v.gb)
        plan.post("gb", b, i, third)
        mix_back(sh, v, third)
        yield part_spent(0.4)
        plan.post("gm", b, i, third)
        yield need("gp", b, i)
        if b == 1:
            yield need("dwd", 1, i)
        spread_out(sh, v, third, v.gp, v.wp, slice(0, 3 * sh.inner))
        yield part_spent(0.7)
        yield from wire.reduce()
        for rows in wire.steps:
            value = v.normed[rows] + wire.total(rows)
            if b == 1:
                base[rows] = value
            else:
                grads[rows] = value.astype(BF16)
        yield part_spent(0.2)
    plan.post("grad", i, third)


def attention(plan, b, i, views):
    key_stream = 1 - i if b == 0 else i
    sh, v = SHAPES[b][i], views[b][i]
    kv = views[b][key_stream]
    for third in range(3):
        yield need("qkv", b, i, third)
    if i == 1:
        v.qkv[...] = dot(v.to_rows[...], flat(v.gp), NN).astype(BF16)
        yield spent(0.6)
    plan.post("rows", b, i)
    yield need("rows", b, key_stream)
    for third in range(3):
        yield need("qkv", b, key_stream, third)
    yield from attend(sh, v, kv, SHAPES[b][key_stream].length)
    plan.post("mixed", b, i)


def attention_back(plan, b, i, views):
    key_stream = 1 - i if b == 0 else i
    sh, v = SHAPES[b][i], views[b][i]
    for third in range(3):
        yield need("gm", b, i, third)
    if b == 0:
        yield need("gp", 1, 0)
        yield need("gp", 1, 1)
        yield need("dwp", 1, 1)
    yield from attend_back(sh, v, SHAPES[b][key_stream], views[b][key_stream])
    plan.post("attended", b, i)
    yield need("attended", b, key_stream)
    if i == 1:
        v.gp[...] = dot(v.to_parts[...], v.gp_rows[...], NN).astype(BF16).reshape(4, sh.part, 3 * sh.inner)
        yield spent(0.6)
    plan.post("gp", b, i)


def feed_grads(plan, b, i, v):
    sh = SHAPES[b][i]
    for third in range(3):
        yield need("gs", b, i, third)
    weight_grad(sh, v.gs, v.active, v.dwu, sh.hidden)
    yield spent(0.9 if i == 0 else 0.5)
    plan.post("dwd", b, i)
    for third in range(3):
        yield need("gu", b, i, third)
    weight_grad(sh, v.nf, v.gu, v.dwu, 0)
    yield spent(0.9 if i == 0 else 0.5)
    plan.post("dwu", b, i)


def head_grads(plan, b, i, v):
    sh = SHAPES[b][i]
    for third in range(3):
        yield need("gb", b, i, third)
    weight_grad(sh, v.gb, v.mixed, v.dwp, sh.out_at)
    yield spent(0.4)
    plan.post("dwo", b, i)
    yield need("gp", b, i)
    weight_grad(sh, v.xf, v.gp, v.dwp, 0)
    yield spent(1.1)
    plan.post("dwp", b, i)


def head_sums(plan, b, i, v):
    yield need("gp", b, i)
    if b == 1:
        yield need("dwp", b, i)
    v.col_proj[:, :3 * SHAPES[b][i].inner] = jnp.sum(flat(v.gp).astype(F32), axis=0, keepdims=True)
    yield spent(0.4)
    plan.post("cols", b, i)


def lane_cut(ref, lane, stop):
    return ref.at[(slice(None),) * (len(ref.shape) - 1) + (slice(lane, stop),)]


def sums_of(plan, me, name, i, views, outs, t, sems, credit):
    pack, first, ranges = SUMS[i][name]
    neighbours = [me.along("z", 1), me.along("x", 1), me.along("x", 3), me.along("y", 1), me.along("y", 3)]
    for b in (1, 0):
        if ranges[b] is None:
            continue
        yield need("dwu" if pack == "u" else "dwo" if name == "o" else "dwp", b, i)
        if name[0] == "p" and b == 1:
            yield need("dwo", b, i)
        if b == 0 and ranges[1] is not None:
            pl.semaphore_wait(credit, 5)
        dw = lane_cut(getattr(views[b][i], "dw" + pack), *ranges[b])
        out = lane_cut(outs[b][pack], *ranges[b])
        if i == 0:
            yield from reduce_text(me, dw, out, t, sems, first)
        else:
            yield from reduce_image(me, dw, out, t, sems, "x" if first else "y")
        if b == 1:
            for device in neighbours:
                pl.semaphore_signal(credit, inc=1, device_id=device, device_id_type=MESH)
    plan.post("summed", name, i)


def gathers(plan, me, b, i, n, v, g):
    pack, lane, stop, first, label, begin = GATHERS[b, i][n]
    yield need("packed", b, i)
    yield ("at", begin)
    sems = getattr(g, f"gather_sems{b}{i}{n}")
    started, ready = ("started", b, i, n), ("got", b, i, n)
    w = lane_cut(getattr(v, "w" + pack), lane, stop)
    if i == 0:
        yield from gather_text(me, lane_cut(getattr(g, f"pieces_{pack}{b}"), lane, stop), w, sems, started, ready, first)
    else:
        yield from gather_image(me, w, sems, started, ready, "x" if first else "y")
    rest = [k for k, other in enumerate(GATHERS[b, i]) if other[4] == label]
    if all(("got", b, i, k) in plan.done for k in rest):
        plan.post("w" + label, b, i)
        if label == "q" and not any(other[4] == "o" for other in GATHERS[b, i]):
            plan.post("wo", b, i)


def whole_kernel(g):
    plan = Plan()
    me = Place(plan)
    wires = [[Wire(me, getattr(g, f"part{i}"), getattr(g, f"from_sib{i}"), getattr(g, f"from_mate{i}"),
                   getattr(g, f"wire_sems{i}{h}"), *SHAPES[0][i].thirds[h]) for h in range(3)] for i in range(2)]
    views = []
    lane = 0
    for b in range(2):
        pair = []
        for i in range(2):
            sh = SHAPES[b][i]
            v = Bag()
            v.wires = wires[i]
            for name in ("head_bias", "up_bias", "bias", "gain", "offset", "xf", "qkv", "mixed", "nf", "slope",
                         "active", "first", "second"):
                setattr(v, name, getattr(g, f"{name}{b}{i}"))
            for name in ("ids_col", "ids_row", "normed", "gs", "gb", "gu"):
                setattr(v, name, getattr(g, f"{name}{i}"))
            v.gm, v.gp = (getattr(g, f"gm0{b}"), getattr(g, f"gp0{b}")) if i == 0 else (g.gm1, g.gp1)
            for pack in "pu":
                wide = sh.columns[pack]
                w, dw = getattr(g, f"w{pack}{b}{i}"), getattr(g, f"w{pack}1{i}" if b == 0 else f"dw{pack}{i}")
                setattr(v, "w" + pack, lane_cut(w, 0, wide))
                setattr(v, "dw" + pack, lane_cut(dw, 0, wide))
            if i == 1:
                for name in ("gp_rows", "gm_parts", "to_rows", "to_parts"):
                    setattr(v, name, getattr(g, name))
                v.mixed_rows = g.gm1
            v.vec = g.vecs.at[:, lane:lane + sh.width]
            lane += sh.width
            k = 2 * (2 * b + i)
            v.col_proj = g.cols.at[k:k + 1]
            v.col_up = g.cols.at[k + 1:k + 2]
            pair.append(v)
        views.append(pair)

    def packed(b, i):
        sh, v = SHAPES[b][i], views[b][i]
        a, f = sh.inner, sh.hidden
        proj, out, up, down = [getattr(g, f"{p}{b}{i}") for p in ("proj", "out", "up", "down")]
        if i == 0:
            to_p, to_u = getattr(g, f"pieces_p{b}").at[me.y], getattr(g, f"pieces_u{b}").at[me.y]
        else:
            to_p, to_u = v.wp.at[me.x, me.z, me.y], v.wu.at[me.x, me.z, me.y]
        for c in range(3):
            to_p[:, c * a:(c + 1) * a] = proj[c]
        to_p[:, 3 * a:4 * a] = out[...]
        to_u[:, :f] = up[...]
        to_u[:, f:2 * f] = down[...]
        plan.post("packed", b, i)
    near = [me.along("z", 1), me.along("x", 1), me.along("x", 3), me.along("y", 1), me.along("y", 3)]
    known = near + [me.along("x", 2), me.along("y", 2), me.sib, me.mate, me.far]
    barrier = pltpu.get_barrier_semaphore()
    for device in known:
        pl.semaphore_signal(barrier, inc=1, device_id=device, device_id_type=MESH)
    for i in range(2):
        packed(0, i)
    pl.semaphore_wait(barrier, len(known))
    entry = Trade(me, [(g.out0, g.xf00.at[me.own]), (g.out1, g.xf01.at[me.own]), (g.lengths0, g.lengths_got0),
                       (g.lengths1, g.lengths_got1), (g.grad0, g.cot_got0), (g.grad1, g.cot_got1)], g.entry_sems)
    out_trade = Trade(me, [(g.out0, g.out0_done), (g.out1, g.out1_done)], g.out_sems)
    grad_trades = [Trade(me, [(g.grad0, g.grad0_done)], g.grad_sems0), Trade(me, [(g.grad1, g.grad1_done)], g.grad_sems1)]
    base = (g.base0, g.base1)

    def opening():
        for name, held in (("x", "out"), ("cot", "grad")):
            getattr(g, held + "0")[...] = getattr(g, f"raw_{name}0")[...].reshape(96, 768)
            raw, padded = getattr(g, f"raw_{name}1"), g.base1
            for b in range(3):
                padded[36 * b:36 * b + 36] = raw[b].astype(F32)
            padded[108:] = jnp.zeros((4, 1024), F32)
            getattr(g, held + "1")[...] = padded[...].astype(BF16)
        entry.start()
        yield spent(0.3)
        for i in range(2):
            packed(1, i)
        for b in range(2):
            for i in range(2):
                v, a = views[b][i], SHAPES[b][i].inner
                v.offset[:, :a] = v.head_bias[0:1].astype(F32)
                v.offset[:, a:2 * a] = jnp.zeros((1, a), F32)
                v.offset[:, 2 * a:] = v.head_bias[1:2].astype(F32)
        g.vecs[...] = jnp.zeros_like(g.vecs)
        g.cols[...] = jnp.zeros_like(g.cols)
        place = lax.broadcasted_iota(jnp.int32, (432, 448), 0)
        token = row_of_part(lax.broadcasted_iota(jnp.int32, (1, 448), 1))
        g.to_rows[...] = (place == token).astype(F32).astype(BF16)
        place = lax.broadcasted_iota(jnp.int32, (448, 432), 1)
        token = row_of_part(lax.broadcasted_iota(jnp.int32, (448, 1), 0))
        g.to_parts[...] = (place == token).astype(F32).astype(BF16)
        yield spent(2.0)
        yield ("at", 8.0)
        entry.finish()
        for i in range(2):
            set_ids(getattr(g, f"ids_col{i}"), getattr(g, f"lengths_got{i}"), 0)
            set_ids(getattr(g, f"ids_row{i}"), getattr(g, f"lengths_got{i}"), 1)
        for i in range(2):
            base[i][...] = views[0][i].xf[me.own].astype(F32)
        yield spent(1.0)
        for i in range(2):
            plan.post("x", i)

    def begun(i, third):
        yield need("x", i)
        yield from stream(plan, i, third, views, base[i], (g.cot_got0, g.cot_got1)[i], (g.out0, g.out1)[i],
                          (g.grad0, g.grad1)[i])

    def closing():
        for i in range(2):
            for third in range(3):
                yield need("out", i, third)
        out_trade.start()

    def closing_grad(i):
        for third in range(3):
            yield need("grad", i, third)
        grad_trades[i].start()

    def vectors():
        for b in range(2):
            for i in range(2):
                yield need("cols", b, i)
        for i in range(2):
            for third in range(3):
                yield need("gb", 0, i, third)
        yield from total_steps(me, g.vecs, g.cols, g.vec_got, g.slots, g.small, g.vec_sum, g.cols_out, g.total_sems)

    tasks = []
    order = sorted((b, "qou".index(label), n, i) for (b, i), cuts in GATHERS.items()
                   for n, (_, _, _, _, label, _) in enumerate(cuts))
    for b, stage, n, i in order:
        tasks.append((RANKS[f"gather{b}{i}{n}"], gathers(plan, me, b, i, n, views[b][i], g)))
    tasks.append((0, opening()))
    for i in (1, 0):
        for third in range(3):
            tasks.append((RANKS[f"stream{i}{third}"], begun(i, third)))
    for b in range(2):
        for i in (1, 0):
            tasks.append((RANKS[f"attention{b}{i}"], attention(plan, b, i, views)))
            tasks.append((RANKS[f"back{b}{i}"], attention_back(plan, b, i, views)))
    tasks.append((RANKS["close"], closing()))
    for i in range(2):
        tasks.append((RANKS["close"], closing_grad(i)))
    tasks.append((RANKS["vectors"], vectors()))
    for i in range(2):
        for name in SUMS[i]:
            t = Bag()
            for part in ("halves", "chunks", "across", "small_chunks") + (("pieces",) if i == 0 else ()):
                setattr(t, part, getattr(g, f"{part}_{name}{i}"))
            outs = [{pack: getattr(g, f"sum_{pack}{b}{i}") for pack in "pu"} for b in range(2)]
            tasks.append((RANKS[f"sums{i}{name}"], sums_of(plan, me, name, i, views, outs, t, getattr(g, f"reduce_sems_{name}{i}"),
                                     getattr(g, f"credit_{name}{i}"))))
    for b in (1, 0):
        for i in (1, 0):
            tasks.append((RANKS[f"feed{b}{i}"], feed_grads(plan, b, i, views[b][i])))
            tasks.append((RANKS[f"head{b}{i}"], head_grads(plan, b, i, views[b][i])))
            tasks.append((RANKS[f"cols{b}{i}"], head_sums(plan, b, i, views[b][i])))
    plan.run(tasks)
    out_trade.finish()
    for trade in grad_trades:
        trade.finish()
    g.vecs_out[...] = g.vec_sum[...]
    for name in ("out0", "out1", "grad0", "grad1"):
        getattr(g, name + "_end")[...] = getattr(g, name + "_done")[...]


def call(kernel, inputs, outs, scratch, collective_id=None):
    names = list(inputs) + list(outs) + list(scratch)

    def body(*refs):
        bag = Bag()
        for name, ref in zip(names, refs):
            setattr(bag, name, ref)
        kernel(bag)
    vm = pl.BlockSpec(memory_space=pltpu.VMEM)
    results = pl.pallas_call(
        body, out_shape=list(outs.values()), in_specs=[vm] * len(inputs), out_specs=[vm] * len(outs),
        scratch_shapes=list(scratch.values()),
        compiler_params=pltpu.CompilerParams(collective_id=collective_id, has_side_effects=collective_id is not None,
                                             vmem_limit_bytes=LIMIT),
    )(*inputs.values())
    return dict(zip(outs, results))


def whole(inputs):
    outs, scratch = {}, {}
    for i in range(2):
        sh = SHAPES[0][i]
        slab = (sh.part, sh.width)
        scratch[f"cot_got{i}"] = VMEM(slab, BF16)
        scratch[f"lengths_got{i}"] = VMEM((3, 4), jnp.int32)
        for name in ("out", "grad"):
            scratch[f"{name}{i}"] = VMEM(slab, BF16)
            scratch[f"{name}{i}_done"] = VMEM(slab, BF16)
            outs[f"{name}{i}_end"] = jax.ShapeDtypeStruct(slab, BF16)
        scratch[f"base{i}"] = VMEM(slab, F32)
        scratch[f"normed{i}"] = VMEM(slab, F32)
        for name in ("gs", "gb", "part"):
            scratch[f"{name}{i}"] = VMEM((4,) + slab, BF16)
        scratch[f"gu{i}"] = VMEM((4, sh.part, sh.hidden), BF16)
        scratch[f"from_sib{i}"] = VMEM((2,) + slab, BF16)
        scratch[f"from_mate{i}"] = VMEM(slab, BF16)
        for third in range(3):
            scratch[f"wire_sems{i}{third}"] = DMA((2, 6))
        scratch[f"grad_sems{i}"] = DMA((2, 1))
        scratch[f"ids_col{i}"] = VMEM((3, sh.length, 1), F32)
        scratch[f"ids_row{i}"] = VMEM((3, 1, sh.length), F32)
        for pack in "pu":
            wide = sh.columns[pack]
            matrix = (768, wide) if i == 0 else (4, 2, 4, 32, wide)
            self_wide = SHAPES[1][i].columns[pack]
            scratch[f"dw{pack}{i}"] = VMEM(matrix[:-1] + (self_wide,), BF16)
            for b in range(2):
                scratch[f"w{pack}{b}{i}"] = VMEM(matrix, BF16)
                cols = SHAPES[b][i].columns[pack]
                if i == 0:
                    scratch[f"pieces_{pack}{b}"] = VMEM((4, 24, cols), BF16)
                outs[f"sum_{pack}{b}{i}"] = jax.ShapeDtypeStruct((24 if i == 0 else 32, cols), F32)
        for b in range(2):
            for n in range(len(GATHERS[b, i])):
                scratch[f"gather_sems{b}{i}{n}"] = DMA((2, 13))
        for name, (pack, first, ranges) in SUMS[i].items():
            wide = max(r[1] - r[0] for r in ranges if r is not None)
            scratch[f"reduce_sems_{name}{i}"] = DMA((2, 13))
            scratch[f"credit_{name}{i}"] = pltpu.SemaphoreType.REGULAR
            if i == 1:
                sizes = {"halves": (2, 2, 2, 32, wide), "chunks": (2,) + ((4, 2) if first else (2, 4)) + (32, wide), "across": (32, wide),
                         "small_chunks": (3, 2, 32, wide)}
            else:
                sizes = {"halves": (2, 96, wide), "chunks": (2, 96 if first else 192, wide),
                         "across": (4, 96, wide) if first else (96, wide),
                         "pieces": (4, 24, wide), "small_chunks": (3, 24, wide)}
            for part, size in sizes.items():
                scratch[f"{part}_{name}{i}"] = VMEM(size, BF16)
    scratch["gp_rows"] = VMEM((432, 768), BF16)
    scratch["gm1"] = VMEM((432, 256), BF16)
    scratch["gm_parts"] = VMEM((4, 112, 256), BF16)
    scratch["gp1"] = VMEM((4, 112, 768), BF16)
    for b in range(2):
        scratch[f"gm0{b}"] = VMEM((384, SHAPES[b][0].inner), BF16)
        scratch[f"gp0{b}"] = VMEM((4, 96, 3 * SHAPES[b][0].inner), BF16)
    scratch["to_rows"] = VMEM((432, 448), BF16)
    scratch["to_parts"] = VMEM((448, 432), BF16)
    scratch["entry_sems"] = DMA((2, 6))
    scratch["out_sems"] = DMA((2, 2))
    lanes_all, cols_wide = 2 * (768 + 1024), 768
    scratch["vecs"] = VMEM((8, lanes_all), F32)
    scratch["cols"] = VMEM((8, cols_wide), F32)
    scratch["vec_got"] = VMEM((3, 8, lanes_all // 4), F32)
    scratch["small"] = VMEM((8, lanes_all // 4 + cols_wide), F32)
    scratch["slots"] = VMEM((3, 4, 8, lanes_all // 4 + cols_wide), F32)
    scratch["vec_sum"] = VMEM((8, lanes_all), F32)
    scratch["total_sems"] = DMA((2, 13))
    outs["vecs_out"] = jax.ShapeDtypeStruct((8, lanes_all), F32)
    outs["cols_out"] = jax.ShapeDtypeStruct((8, cols_wide), F32)
    for b in range(2):
        for i in range(2):
            sh = SHAPES[b][i]
            slab = (sh.part, sh.width)
            for name, shape, kind in (
                    ("offset", (1, 3 * sh.inner), F32), ("xf", (4,) + slab, BF16), ("nf", (4,) + slab, BF16),
                    ("qkv", (3 * sh.length, 3 * sh.inner), BF16), ("mixed", (4, sh.part, sh.inner), BF16),
                    ("slope", (4, sh.part, sh.hidden), BF16), ("active", (4, sh.part, sh.hidden), BF16),
                    ("first", slab, F32), ("second", slab, F32)):
                scratch[f"{name}{b}{i}"] = VMEM(shape, kind)
    return call(whole_kernel, inputs, outs, scratch, 0)


def finish_kernel(g):
    for i, count in enumerate((32, 36)):
        for name in ("out", "grad"):
            src, dst = getattr(g, f"{name}{i}"), getattr(g, f"{name}{i}_end")
            if i == 0:
                dst[...] = src[...].reshape(dst.shape)
            else:
                value = src[...].astype(F32)
                for b in range(3):
                    dst[b] = value[b * count:(b + 1) * count].astype(dst.dtype)
    lane = 0
    for k, n in enumerate(f"{b}{i}" for b in range(2) for i in range(2)):
        sum_p, sum_u = getattr(g, "sum_p" + n), getattr(g, "sum_u" + n)
        proj, out, up, down = [getattr(g, p + n) for p in ("proj", "out", "up", "down")]
        a, f = proj.shape[2], up.shape[1]
        for c in range(3):
            proj[c] = sum_p[:, c * a:(c + 1) * a]
        out[...] = sum_p[:, 3 * a:4 * a]
        up[...] = sum_u[:, :f]
        down[...] = sum_u[:, f:2 * f]
        head_bias, up_bias, bias, gain = [getattr(g, p + n) for p in ("head_bias", "up_bias", "bias", "gain")]
        head_bias[0:1] = g.cols[2 * k:2 * k + 1, :a]
        head_bias[1:2] = g.cols[2 * k:2 * k + 1, 2 * a:3 * a]
        up_bias[...] = g.cols[2 * k + 1:2 * k + 2, :f]
        width = bias.shape[1]
        bias[...] = g.vecs[0:4, lane:lane + width]
        gain[...] = g.vecs[4:6, lane:lane + width]
        lane += width


def on_device(*args):
    text_in, image_in, text_lengths, image_lengths, text_cot, image_cot = args[:6]
    matrix_names = ("proj", "out", "up", "down")
    small_names = ("head_bias", "up_bias", "bias", "gain")

    inputs = {"raw_x0": text_in, "raw_x1": image_in, "raw_cot0": text_cot, "raw_cot1": image_cot,
              "lengths0": text_lengths, "lengths1": image_lengths}
    shapes = {}
    names = [f"{b}{i}" for b in range(2) for i in range(2)]
    for k, n in enumerate(names):
        for name, value in zip(matrix_names + small_names, args[6 + 8 * k:14 + 8 * k]):
            inputs[name + n] = value.transpose(1, 0, 2) if name == "proj" else value
            shapes[name + n] = jax.ShapeDtypeStruct(inputs[name + n].shape, F32)
    done = whole(inputs)
    ends, outs = {"vecs": done["vecs_out"], "cols": done["cols_out"]}, {}
    for name, like in (("out0", text_in), ("out1", image_in), ("grad0", text_in), ("grad1", image_in)):
        ends[name] = done[name + "_end"]
        outs[name + "_end"] = jax.ShapeDtypeStruct(like.shape, like.dtype)
    for n in names:
        ends["sum_p" + n] = done["sum_p" + n]
        ends["sum_u" + n] = done["sum_u" + n]
        for p in matrix_names + small_names:
            outs[p + n] = shapes[p + n]
    return tuple(value.transpose(1, 0, 2) if name.startswith("proj") else value
                 for name, value in call(finish_kernel, ends, outs, {}).items())


def solution(mesh):
    kinds = [P("rows", None, "seq"), P("rows", "seq"), P("rows", "seq"), P("rows", "seq"), P(None, "seq"),
             P(None, "seq"), P(), P()] * 4
    position = P("rows", "seq", None)
    return jax.shard_map(
        on_device, mesh=mesh,
        in_specs=tuple([position, position, P("rows", None), P("rows", None), position, position] + kinds),
        out_specs=tuple([position] * 4 + kinds), check_vma=False)
```
